32 devices in a mesh: section: 2 (over x), dp: 4 (over y, core), mp: 4 (over z).
Axes of the slice: x: 2, y: 2, z: 4, core: 2. Of those that a mesh axis runs over, the one named last changes fastest.
Arguments:
- boundary: float32 [2, 3, 4, 1370, 1024], P('section', None, 'dp', None, 'mp'), may hold values from -6 to 6
- ln1_gain: float32 [2, 1024], P('section', 'mp'), may hold values from 0.5 to 1.5
- ln1_bias: float32 [2, 1024], P('section', 'mp'), may hold values from -4 to 4
- w_query: bfloat16 [2, 1024, 1024], P('section', 'dp', 'mp'), may hold values from -0.1875 to 0.1875
- w_key: bfloat16 [2, 1024, 1024], P('section', 'dp', 'mp'), may hold values from -0.1875 to 0.1875
- w_value: bfloat16 [2, 1024, 1024], P('section', 'dp', 'mp'), may hold values from -0.1875 to 0.1875
- b_query: float32 [2, 1024], P('section', 'mp'), may hold values from -6 to 6
- b_value: float32 [2, 1024], P('section', 'mp'), may hold values from -6 to 6
- w_out: bfloat16 [2, 1024, 1024], P('section', 'mp', 'dp'), may hold values from -2 to 2
- b_out: float32 [2, 1024], P('section', 'mp'), may hold values from -4 to 4
- scale_attn: float32 [2, 1024], P('section', 'mp'), may hold values from 0.5 to 1.5
- ln2_gain: float32 [2, 1024], P('section', 'mp'), may hold values from 0.5 to 1.5
- ln2_bias: float32 [2, 1024], P('section', 'mp'), may hold values from -4 to 4
- w_fc1: bfloat16 [2, 1024, 4096], P('section', 'dp', 'mp'), may hold values from -0.1875 to 0.1875
- b_fc1: float32 [2, 4096], P('section', 'mp'), may hold values from -6 to 6
- w_fc2: bfloat16 [2, 4096, 1024], P('section', 'mp', 'dp'), may hold values from -0.09375 to 0.09375
- b_fc2: float32 [2, 1024], P('section', 'mp'), may hold values from -4 to 4
- scale_mlp: float32 [2, 1024], P('section', 'mp'), may hold values from 0.5 to 1.5
Outputs:
- ends_out: float32 [2, 3, 4, 1370, 1024], P('section', None, 'dp', None, 'mp')
- grad_ln1_gain: float32 [2, 1024], P('section', ('mp', 'dp'))
- grad_ln1_bias: float32 [2, 1024], P('section', ('mp', 'dp'))
- grad_w_query: float32 [2, 1024, 1024], P('section', 'dp', 'mp')
- grad_w_key: float32 [2, 1024, 1024], P('section', 'dp', 'mp')
- grad_w_value: float32 [2, 1024, 1024], P('section', 'dp', 'mp')
- grad_b_query: float32 [2, 1024], P('section', ('mp', 'dp'))
- grad_b_value: float32 [2, 1024], P('section', ('mp', 'dp'))
- grad_w_out: float32 [2, 1024, 1024], P('section', 'mp', 'dp')
- grad_b_out: float32 [2, 1024], P('section', ('mp', 'dp'))
- grad_scale_attn: float32 [2, 1024], P('section', ('mp', 'dp'))
- grad_ln2_gain: float32 [2, 1024], P('section', ('mp', 'dp'))
- grad_ln2_bias: float32 [2, 1024], P('section', ('mp', 'dp'))
- grad_w_fc1: float32 [2, 1024, 4096], P('section', 'dp', 'mp')
- grad_b_fc1: float32 [2, 4096], P('section', ('mp', 'dp'))
- grad_w_fc2: float32 [2, 4096, 1024], P('section', 'mp', 'dp')
- grad_b_fc2: float32 [2, 1024], P('section', ('mp', 'dp'))
- grad_scale_mlp: float32 [2, 1024], P('section', ('mp', 'dp'))
The draws below stay inside these ranges and needn't reach their ends.
All inputs are finite; a program needn't handle non-finite values.
Results may differ from the reference program's by a relative error of at most 0.02.
Values may be sent and summed in bfloat16 or wider, within the bound.
A program may use at most 384 MiB of HBM per device.

```python
import jax
import jax.numpy as jnp
from jax import lax

D = 1024
HEADS = 16
HD = 64
FF = 4096
SEQ = 1370
QBLOCKS = 2
MICRO = 3
IMAGES = 4
LAYERS = 2


def steps_of(own_key, extent, shards, smallest, top_value):
    loudness = 1.0
    for axis_at, parts in shards:
        steps = jax.random.uniform(jax.random.fold_in(jax.random.fold_in(own_key, 6), axis_at), (parts,), jnp.float32, smallest / len(shards), top_value / len(shards))
        loudness = loudness * jnp.repeat(jnp.exp(steps), extent[axis_at] // parts).reshape((-1,) + (1,) * (len(extent) - 1 - axis_at))
    return loudness


def centred(key, extent, scale, reach, pieces=(), kind=jnp.bfloat16):
    level = steps_of(key, extent, pieces, -0.22, 0.18) if pieces else 1.0
    entries = jax.random.normal(key, extent, jnp.float32) * scale * level
    return jnp.minimum(jnp.maximum(entries, -reach), reach).astype(kind)


def setup_inputs(seed: int = 0) -> dict:
    splits = jax.random.split(jax.random.key(seed), 19)
    boundary = centred(splits[0], (2, MICRO, IMAGES, SEQ, D), 1.0, 6.0, ((0, 2), (2, 4), (4, 4)), jnp.float32)
    ln1_gain = jnp.clip(0.5 + 1.0 * jax.random.uniform(splits[1], (LAYERS, D), jnp.float32) ** steps_of(splits[1], (LAYERS, D), ((0, 2), (1, 4)), -0.2, 0.2), 0.5, 1.5)
    ln1_bias = centred(splits[2], (LAYERS, D), 0.3, 4.0, ((0, 2), (1, 4)), jnp.float32)
    w_query = centred(splits[3], (LAYERS, D, D), D ** -0.5, 0.1875, ((0, 2), (1, 4), (2, 4)))
    w_key = centred(splits[4], (LAYERS, D, D), D ** -0.5, 0.1875, ((0, 2), (1, 4), (2, 4)))
    w_value = centred(splits[5], (LAYERS, D, D), D ** -0.5, 0.1875, ((0, 2), (1, 4), (2, 4)))
    b_query = centred(splits[6], (LAYERS, D), 0.5, 6.0, ((0, 2), (1, 4)), jnp.float32)
    b_value = centred(splits[7], (LAYERS, D), 0.5, 6.0, ((0, 2), (1, 4)), jnp.float32)
    w_out = centred(splits[8], (LAYERS, D, D), (max(D // 128, 1)) ** -0.5, 2.0, ((0, 2), (1, 4), (2, 4)))
    b_out = centred(splits[9], (LAYERS, D), 0.3, 4.0, ((0, 2), (1, 4)), jnp.float32)
    scale_attn = jnp.clip(0.5 + 1.0 * jax.random.uniform(splits[10], (LAYERS, D), jnp.float32) ** steps_of(splits[10], (LAYERS, D), ((0, 2), (1, 4)), -0.2, 0.2), 0.5, 1.5)
    ln2_gain = jnp.clip(0.5 + 1.0 * jax.random.uniform(splits[11], (LAYERS, D), jnp.float32) ** steps_of(splits[11], (LAYERS, D), ((0, 2), (1, 4)), -0.2, 0.2), 0.5, 1.5)
    ln2_bias = centred(splits[12], (LAYERS, D), 0.3, 4.0, ((0, 2), (1, 4)), jnp.float32)
    w_fc1 = centred(splits[13], (LAYERS, D, FF), D ** -0.5, 0.1875, ((0, 2), (1, 4), (2, 4)))
    b_fc1 = centred(splits[14], (LAYERS, FF), 0.5, 6.0, ((0, 2), (1, 4)), jnp.float32)
    w_fc2 = centred(splits[15], (LAYERS, FF, D), FF ** -0.5, 0.09375, ((0, 2), (1, 4), (2, 4)))
    b_fc2 = centred(splits[16], (LAYERS, D), 0.3, 4.0, ((0, 2), (1, 4)), jnp.float32)
    scale_mlp = jnp.clip(0.5 + 1.0 * jax.random.uniform(splits[17], (LAYERS, D), jnp.float32) ** steps_of(splits[17], (LAYERS, D), ((0, 2), (1, 4)), -0.2, 0.2), 0.5, 1.5)
    return {"boundary": boundary, "ln1_gain": ln1_gain, "ln1_bias": ln1_bias, "w_query": w_query, "w_key": w_key, "w_value": w_value, "b_query": b_query, "b_value": b_value, "w_out": w_out, "b_out": b_out, "scale_attn": scale_attn, "ln2_gain": ln2_gain, "ln2_bias": ln2_bias, "w_fc1": w_fc1, "b_fc1": b_fc1, "w_fc2": w_fc2, "b_fc2": b_fc2, "scale_mlp": scale_mlp}


@jax.custom_vjp
def low(v):
    return lax.optimization_barrier(v.astype(jnp.bfloat16)).astype(jnp.float32)

@jax.custom_vjp
def low_back(v):
    return v

def low_keep(v):
    return (low(v), None)

def low_pass(kept, grad):
    return (grad,)

def back_keep(v):
    return (v, None)

def back_low(kept, grad):
    return (low(grad),)
low.defvjp(low_keep, low_pass)
low_back.defvjp(back_keep, back_low)
highest = lax.Precision.HIGHEST
epsilon = 1e-06

def product(left, right):
    return jnp.dot(left, right, precision=highest)

def norm_rows(rows_in, gain, shift_vec):
    row_mean = lax.optimization_barrier(jnp.mean(rows_in, -1, keepdims=True))
    row_var = lax.optimization_barrier(jnp.mean(rows_in * rows_in, -1, keepdims=True)) - row_mean * row_mean
    return (rows_in - row_mean) * lax.rsqrt(row_var + epsilon) * gain + shift_vec

def attention(queries, keys, values):
    span = SEQ // QBLOCKS
    scale = HD ** (-0.5)
    blocks = queries.reshape(QBLOCKS, span, HEADS, HD)
    keys_four = keys.reshape(SEQ, HEADS, HD)
    values_four = values.reshape(SEQ, HEADS, HD)

    def one_block(part):
        scores = low_back(jnp.einsum('bhd,khd->hbk', part, keys_four, precision=highest) * scale)
        probs = low(jax.nn.softmax(scores, axis=-1))
        return jnp.einsum('hbk,khd->bhd', probs, values_four, precision=highest)
    return lax.map(jax.checkpoint(one_block), blocks).reshape(SEQ, HEADS * HD)

def block_layer(layer_params, rows_in):
    ln1_gain, ln1_bias, w_query, w_key, w_value, b_query, b_value, w_out, b_out, scale_attn, ln2_gain, ln2_bias, w_fc1, b_fc1, w_fc2, b_fc2, scale_mlp = layer_params
    normed = low(norm_rows(rows_in, ln1_gain, ln1_bias))
    queries = low_back(low(product(normed, w_query) + b_query))
    keys = low_back(low(product(normed, w_key)))
    values = low_back(low(product(normed, w_value) + b_value))
    attended = low_back(low(attention(queries, keys, values)))
    branch = low_back(product(attended, w_out) + b_out)
    middle = rows_in + scale_attn * branch
    normed_two = low(norm_rows(middle, ln2_gain, ln2_bias))
    hidden = low_back(product(normed_two, w_fc1) + b_fc1)
    active = low(jax.nn.gelu(hidden, approximate=False))
    branch_two = low_back(product(active, w_fc2) + b_fc2)
    return middle + scale_mlp * branch_two

def two_layers(weights_f32, rows_in):
    for layer_index in range(LAYERS):
        rows_in = block_layer(tuple((w[layer_index] for w in weights_f32)), rows_in)
        if layer_index + 1 < LAYERS:
            rows_in = low_back(low(rows_in))
    return rows_in

def reference(boundary, ln1_gain, ln1_bias, w_query, w_key, w_value, b_query, b_value, w_out, b_out, scale_attn, ln2_gain, ln2_bias, w_fc1, b_fc1, w_fc2, b_fc2, scale_mlp):
    weights_f32 = tuple((w.astype(jnp.float32) for w in (ln1_gain, ln1_bias, w_query, w_key, w_value, b_query, b_value, w_out, b_out, scale_attn, ln2_gain, ln2_bias, w_fc1, b_fc1, w_fc2, b_fc2, scale_mlp)))
    inputs = boundary[0].astype(jnp.float32).reshape(MICRO * IMAGES, SEQ, D)
    cotangents = boundary[1].astype(jnp.float32).reshape(MICRO * IMAGES, SEQ, D)

    def image_step(totals, pair):
        image_rows, image_cot = pair
        result, pull = jax.vjp(two_layers, weights_f32, image_rows)
        grad_weights, grad_rows = pull(image_cot)
        totals = tuple((t + g for t, g in zip(totals, grad_weights)))
        return (totals, (result, grad_rows))
    start = tuple((jnp.zeros(w.shape, jnp.float32) for w in weights_f32))
    totals, (results, grad_inputs) = lax.scan(image_step, start, (inputs, cotangents))
    ends_out = jnp.stack([grad_inputs.reshape(MICRO, IMAGES, SEQ, D), results.reshape(MICRO, IMAGES, SEQ, D)])
    return (ends_out, totals[0], totals[1], totals[2], totals[3], totals[4], totals[5], totals[6], totals[7], totals[8], totals[9], totals[10], totals[11], totals[12], totals[13], totals[14], totals[15], totals[16])
```

```python
import functools

import jax
import jax.numpy as jnp
from jax import lax
from jax.experimental import pallas as pl
from jax.experimental.pallas import tpu as pltpu
from jax.sharding import PartitionSpec as P


HD = 64
LOW = jnp.bfloat16
WIDE = jnp.float32
HBM = pl.BlockSpec(memory_space=pl.ANY)

epsilon = 1e-06
inv_root_two = 0.7071067811865476
inv_root_tau = 0.3989422804014327


class Place:
    def __init__(self):
        self.S = lax.axis_size("section")
        self.DP = lax.axis_size("dp")
        self.MP = lax.axis_size("mp")
        self.Y = self.DP // 2
        self.H = self.MP // 2
        self.s = lax.axis_index("section")
        self.d = lax.axis_index("dp")
        self.z = lax.axis_index("mp")
        self.y = lax.div(self.d, 2)
        self.c = lax.rem(self.d, 2)

    def other_y(self, r):
        return lax.rem(self.y + r, self.Y)

    def other_z(self, r):
        return lax.rem(self.z + r, self.MP)


class Moves:
    def __init__(self, send_sems, recv_sems, counts):
        self.send_sems, self.recv_sems = send_sems, recv_sems
        self.base, total = {}, 0
        for name, count in counts.items():
            self.base[name] = total
            total += count
        self.total = total
        self.sent = []

    def arrival(self, name, index):
        return self.recv_sems.at[self.base[name] + index]

    def send(self, src, dst, name, index, when=None, **to):
        at = len(self.sent)
        assert at < self.send_sems.shape[0]
        copy = pltpu.make_async_remote_copy(
            src_ref=src,
            dst_ref=dst,
            send_sem=self.send_sems.at[at],
            recv_sem=self.arrival(name, index),
            device_id=to,
        )
        self.sent.append((copy, when))
        if when is None:
            copy.start()
        else:
            pl.when(when)(copy.start)

    def wait(self, ref, name, index):
        pltpu.make_async_copy(ref, ref, self.arrival(name, index)).wait()

    def finish(self):
        for copy, when in self.sent:
            if when is None:
                copy.wait_send()
            else:
                pl.when(when)(copy.wait_send)


def tile(start, size):
    return pl.ds(pl.multiple_of(start * size, size), size)


def holder(place, c, piece):
    image = 2 * (piece // 2) + c
    return lax.div(image, place.MP), piece % 2, lax.rem(image, place.MP)


def gather_counts(S, Y, MP, groups=3):
    return dict(rows=S * MP, vectors=S * MP, piece=groups * S * Y * MP, pair=groups * S * Y * MP)


def gather_kernel(pieces, sent_ref, vec_ref, a_ref, b_ref, c_ref, rows_ref, vecs_ref, A, B, C, send_sems, recv_sems, own_sems):
    place = Place()
    s, y, c, z, d = place.s, place.y, place.c, place.z, place.d
    S, Y, MP, H = place.S, place.Y, place.MP, place.H
    moves = Moves(send_sems, recv_sems, gather_counts(S, Y, MP))
    columns = sent_ref.shape[2]
    shards, wholes = (a_ref, b_ref, c_ref), (A, B, C)

    def spot(g, l, yy, cc, zz):
        dd = yy * 2 + cc
        shard, whole = shards[g], wholes[g]
        at = (tile(dd, shard.shape[-2]), tile(zz, shard.shape[-1]))
        return whole.at[(l, slice(None)) + at] if len(shard.shape) == 3 else whole.at[(l,) + at]

    def mark(g, l, yy, zz):
        return ((g * S + l) * Y + yy) * MP + zz

    def to_pair(g, l, yy, zz, src=None, when=None):
        there = spot(g, l, yy, c, zz)
        moves.send(
            there if src is None else src, there, "pair", mark(g, l, yy, zz), when, section=s, dp=y * 2 + 1 - c, mp=z
        )

    def to_rows(g, l, yy, zz, when=None, src=None):
        there = spot(g, l, yy, c, zz)
        for r in range(1, Y):
            moves.send(
                there if src is None else src, there, "piece", mark(g, l, yy, zz), when,
                section=s, dp=place.other_y(r) * 2 + c, mp=z,
            )

    def to_section(g, l, yy, zz, when=None, src=None):
        there = spot(g, l, yy, c, zz)
        moves.send(there if src is None else src, there, "piece", mark(g, l, yy, zz), when, section=1 - s, dp=d, mp=z)

    def landed(g, l, yy, zz):
        moves.wait(spot(g, l, yy, c, zz), "piece", mark(g, l, yy, zz))

    own_copies = []

    def near(zz):
        return lax.div(zz, H) == lax.div(z, H)

    def along(g, zz, step, when, src=None):
        there = spot(g, s, y, c, zz)
        moves.send(
            there if src is None else src, there, "piece", mark(g, s, y, zz), when,
            section=s, dp=d, mp=jnp.clip(z + step, 0, MP - 1),
        )

    def columns_out(g):
        there = spot(g, s, y, c, z)
        along(g, z, 1, z + 1 < MP, shards[g])
        along(g, z, -1, z >= 1, shards[g])
        to_section(g, s, y, z, src=shards[g])
        to_rows(g, s, y, z, src=shards[g])
        to_pair(g, s, y, z, shards[g])
        copy = pltpu.make_async_copy(shards[g], there, own_sems.at[g])
        copy.start()
        own_copies.append(copy)

    def columns_in(g, far):
        for step, there in ((1, z >= far), (-1, z + far < MP)):
            zz = jnp.clip(z - step * far, 0, MP - 1)

            @pl.when(there)
            def _():
                landed(g, s, y, zz)

            along(g, zz, step, there & ((z + 1 < MP) if step == 1 else (z >= 1)))
            to_section(g, s, y, zz, there)
            to_rows(g, s, y, zz, there & ((s == 0) | near(zz)))
            to_pair(g, s, y, zz, when=there)

    def far_column(k):
        return lax.rem(lax.div(z, H) + 1, 2) * H + k

    def near_column(k):
        return lax.div(z, H) * H + k

    def nearest_first():
        return [z] + [lax.div(z, H) * H + lax.rem(z + r, H) for r in range(1, H)] + [far_column(k) for k in range(H)]

    def section_in(g, which):
        zz = nearest_first()[which]
        landed(g, 1 - s, y, zz)
        to_rows(g, 1 - s, y, zz, None if which >= H else s == 1)
        to_pair(g, 1 - s, y, zz)

    def rows_in(g):
        for r in range(1, Y):
            yy = place.other_y(r)
            for k in range(H):
                zz = jnp.where(s == 1, near_column(k), far_column(k))
                landed(g, 1, yy, zz)
                to_section(g, 1, yy, zz)
                to_pair(g, 1, yy, zz)
            for zz in range(MP):
                landed(g, 0, yy, zz)
                to_pair(g, 0, yy, zz)

    def corner_in(g):
        for r in range(1, Y):
            for k in range(H):
                zz = jnp.where(s == 1, far_column(k), near_column(k))
                landed(g, 1, place.other_y(r), zz)
                to_pair(g, 1, place.other_y(r), zz)

    for piece in range(pieces):
        to_s, to_c, to_z = holder(place, c, piece)
        here = (to_s == s) & (to_c == c) & (to_z == z)
        there = rows_ref.at[s, :, tile(z, columns)]
        moves.send(
            sent_ref.at[piece], there, "rows", s * MP + z, jnp.logical_not(here),
            section=to_s, dp=y * 2 + to_c, mp=to_z,
        )

        @pl.when(here)
        def _():
            pltpu.make_async_copy(sent_ref.at[piece], there, moves.arrival("rows", s * MP + z)).start()

    for q in range(1, S * MP):
        at = lax.rem(s * MP + z + q, S * MP)
        moves.send(vec_ref, vecs_ref.at[s * MP + z], "vectors", s * MP + z, section=lax.div(at, MP), dp=d, mp=lax.rem(at, MP))
    own_vec = pltpu.make_async_copy(vec_ref, vecs_ref.at[s * MP + z], own_sems.at[3])
    own_vec.start()

    for g in range(3):
        columns_out(g)
        own_copies[g].wait()
        for far in range(1, MP):
            columns_in(g, far)
            section_in(g, far - 1)
        section_in(g, MP - 1)
        if g:
            rows_in(g - 1)
            corner_in(g - 1)
    rows_in(2)
    corner_in(2)

    @pl.when(s * MP + z < pieces)
    def _():
        for section in range(S):
            for zz in range(MP):
                moves.wait(rows_ref.at[section, :, tile(zz, columns)], "rows", section * MP + zz)

    for q in range(1, S * MP):
        at = lax.rem(s * MP + z + q, S * MP)
        moves.wait(vecs_ref.at[at], "vectors", at)
    for g in range(3):
        for l in range(S):
            for yy in range(Y):
                for zz in range(MP):
                    moves.wait(spot(g, l, yy, 1 - c, zz), "pair", mark(g, l, yy, zz))
    own_vec.wait()
    moves.finish()


def gather(sent, vec, a, b, c):
    S, DP, MP = (lax.axis_size(name) for name in ("section", "dp", "mp"))
    Y = DP // 2
    pieces, rows, columns = sent.shape
    counts = gather_counts(S, Y, MP)
    sends = pieces + S * MP - 1 + 3 * (2 * MP + (1 + 2 * (MP - 1)) * (1 + Y) + MP * Y + (Y - 1) * (MP + 3 * (MP // 2)))
    return pl.pallas_call(
        functools.partial(gather_kernel, pieces),
        in_specs=[HBM] * 5,
        out_specs=[HBM] * 5,
        out_shape=[
            jax.ShapeDtypeStruct((S, rows, columns * MP), LOW),
            jax.ShapeDtypeStruct((S * MP,) + vec.shape, WIDE),
            jax.ShapeDtypeStruct((S, a.shape[0], a.shape[1] * DP, a.shape[2] * MP), LOW),
            jax.ShapeDtypeStruct((S, b.shape[0] * DP, b.shape[1] * MP), LOW),
            jax.ShapeDtypeStruct((S, c.shape[0] * DP, c.shape[1] * MP), LOW),
        ],
        scratch_shapes=[
            pltpu.SemaphoreType.DMA((sends,)),
            pltpu.SemaphoreType.DMA((sum(counts.values()),)),
            pltpu.SemaphoreType.DMA((4,)),
        ],
        compiler_params=pltpu.CompilerParams(has_side_effects=True),
    )(sent, vec, a, b, c)


def scatter_counts(S, Y, MP, pieces, groups=4):
    H = MP // 2
    return dict(
        back=max(pieces, MP),
        corner_x=groups * (Y - 1) * H,
        corner_y=groups * (Y - 1) * H,
        from_x=groups * MP,
        from_y=groups * (Y - 1) * MP,
        from_z=groups * MP,
        vec_pair=1,
        vec_x=1,
        vec_y=Y - 1,
        vec_z=MP,
    )


ORDER = (3, 2, 1, 0)


def scatter_kernel(
    pieces, table_ref, first_ref, last_ref, *refs
):
    place = Place()
    s, y, c, z, d = place.s, place.y, place.c, place.z, place.d
    S, Y, MP, H = place.S, place.Y, place.MP, place.H
    grads = (refs[0:2], refs[2:4], refs[4:6], refs[6:8])
    ends_ref, sums_ref, outs = refs[8], refs[9], refs[10:14]
    mine, over, across, corner_x, corner_y, from_x, from_y, from_z = (refs[14 + 4 * i : 18 + 4 * i] for i in range(8))
    send_sems, recv_sems, load_sems, vec_here, vec_pair, vec_x, vec_y, vec_z = refs[46:]
    moves = Moves(send_sems, recv_sems, scatter_counts(S, Y, MP, pieces))
    block = first_ref.shape[2]

    def part(g, l, yy, zz):
        ref = grads[g][l]
        piece = outs[g].shape
        at = (yy, slice(None), tile(zz, piece[-1]))
        return ref.at[(slice(None),) + at] if len(piece) == 3 else ref.at[at]

    moves.send(table_ref.at[1 - c], vec_pair, "vec_pair", 0, section=s, dp=y * 2 + 1 - c, mp=z)
    moves.wait(vec_pair, "vec_pair", 0)
    vec_here[...] = table_ref[c] + vec_pair[...]
    moves.send(vec_here.at[1 - s], vec_x, "vec_x", 0, section=1 - s, dp=d, mp=z)
    moves.wait(vec_x, "vec_x", 0)
    vec_here[s] = vec_here[s] + vec_x[...]
    for r in range(1, Y):
        at = Y - r - 1
        moves.send(
            vec_here.at[s, place.other_y(r)], vec_y.at[at], "vec_y", at, section=s, dp=place.other_y(r) * 2 + c, mp=z
        )
    for r in range(1, Y):
        moves.wait(vec_y.at[r - 1], "vec_y", r - 1)
    vec_here[s, y] = vec_here[s, y] + jnp.sum(vec_y[...], 0)
    for r in range(1, MP):
        moves.send(vec_here.at[s, y, place.other_z(r)], vec_z.at[z], "vec_z", z, section=s, dp=d, mp=place.other_z(r))
    vec_total = vec_here[s, y, z]
    for r in range(1, MP):
        moves.wait(vec_z.at[place.other_z(r)], "vec_z", place.other_z(r))
        vec_total = vec_total + vec_z[place.other_z(r)]
    sums_ref[...] = vec_total

    number = s * MP + z
    active = number < pieces
    piece = 2 * lax.div(number, 2) + c
    for section, ref in ((0, first_ref), (1, last_ref)):
        for zz in range(MP):
            to_c = lax.rem(number, 2)
            here = (s == section) & (to_c == c) & (z == zz)
            there = ends_ref.at[piece]
            moves.send(
                ref.at[zz], there, "back", piece, active & jnp.logical_not(here), section=section, dp=y * 2 + to_c, mp=zz
            )

            @pl.when(active & here)
            def _():
                pltpu.make_async_copy(ref.at[zz], there, moves.arrival("back", piece)).start()

    loads = []

    def by_section(g, mine_too, yy, zz, use):
        for layer in range(S):
            pl.when((s == layer) if mine_too else (s != layer))(lambda: use(part(g, layer, yy, zz)))

    def send_part(g, mine_too, yy, zz, dst, name, index, **to):
        at = len(moves.sent)
        sample = part(g, 0, yy, zz)

        def go(ref):
            pltpu.make_async_remote_copy(
                src_ref=ref, dst_ref=dst, send_sem=send_sems.at[at], recv_sem=moves.arrival(name, index), device_id=to
            ).start()

        by_section(g, mine_too, yy, zz, go)
        moves.sent.append(
            (
                pltpu.make_async_remote_copy(
                    src_ref=sample, dst_ref=dst, send_sem=send_sems.at[at], recv_sem=moves.arrival(name, index), device_id=to
                ),
                None,
            )
        )

    def load(g, mine_too, yy, zz, dst):
        at = len(loads)
        by_section(g, mine_too, yy, zz, lambda ref: pltpu.make_async_copy(ref, dst, load_sems.at[at]).start())
        loads.append(pltpu.make_async_copy(dst, dst, load_sems.at[at]))
        return at

    over_at, across_at, mine_at = {}, {}, {}
    for g in ORDER:
        for r in range(1, Y):
            for k in range(H):
                slot = ((r - 1) * H) + k
                send_part(
                    g, False, place.other_y(r), k, corner_x[g].at[slot], "corner_x", g * (Y - 1) * H + slot,
                    section=1 - s, dp=d, mp=z,
                )
                back = (Y - r) % Y
                send_part(
                    g, False, place.other_y(r), H + k, corner_y[g].at[(back - 1) * H + k], "corner_y",
                    g * (Y - 1) * H + (back - 1) * H + k,
                    section=s, dp=place.other_y(r) * 2 + c, mp=z,
                )
        for k in range(H):
            over_at[g, k] = load(g, False, y, H + k, over[g].at[k])
            for r in range(1, Y):
                across_at[g, r, k] = load(g, True, place.other_y(r), k, across[g].at[(r - 1) * H + k])
        for k in range(H):
            send_part(g, False, y, k, from_x[g].at[k], "from_x", g * MP + k, section=1 - s, dp=d, mp=z)
            for r in range(1, Y):
                back = (Y - r) % Y
                slot = (back - 1) * MP + H + k
                send_part(
                    g, True, place.other_y(r), H + k, from_y[g].at[slot], "from_y", g * (Y - 1) * MP + slot,
                    section=s, dp=place.other_y(r) * 2 + c, mp=z,
                )
    for g in ORDER:
        for zz in range(MP):
            mine_at[g, zz] = load(g, True, y, zz, mine[g].at[zz])

    def add_into(dst, *terms):
        total = dst[...].astype(WIDE)
        for term in terms:
            total = total + term[...].astype(WIDE)
        dst[...] = total.astype(LOW)

    for g in ORDER:
        for k in range(H):
            for r in range(1, Y):
                slot = (r - 1) * H + k
                moves.wait(corner_x[g].at[slot], "corner_x", g * (Y - 1) * H + slot)
                loads[across_at[g, r, k]].wait()
                add_into(across[g].at[slot], corner_x[g].at[slot])
                back = (Y - r) % Y
                out = (back - 1) * MP + k
                moves.send(
                    across[g].at[slot], from_y[g].at[out], "from_y", g * (Y - 1) * MP + out,
                    section=s, dp=place.other_y(r) * 2 + c, mp=z,
                )
            for r in range(1, Y):
                slot = (r - 1) * H + k
                moves.wait(corner_y[g].at[slot], "corner_y", g * (Y - 1) * H + slot)
            loads[over_at[g, k]].wait()
            add_into(over[g].at[k], *(corner_y[g].at[(r - 1) * H + k] for r in range(1, Y)))
            moves.send(over[g].at[k], from_x[g].at[H + k], "from_x", g * MP + H + k, section=1 - s, dp=d, mp=z)

    for g in ORDER:
        for zz in list(range(H)) + list(range(H, MP)):
            moves.wait(from_x[g].at[zz], "from_x", g * MP + zz)
            for r in range(1, Y):
                slot = (r - 1) * MP + zz
                moves.wait(from_y[g].at[slot], "from_y", g * (Y - 1) * MP + slot)
            loads[mine_at[g, zz]].wait()
            add_into(mine[g].at[zz], from_x[g].at[zz], *(from_y[g].at[(r - 1) * MP + zz] for r in range(1, Y)))
            moves.send(
                mine[g].at[zz], from_z[g].at[z], "from_z", g * MP + z, z != zz, section=s, dp=d, mp=zz
            )

    for g in ORDER:
        total = mine[g][z].astype(WIDE)
        for r in range(1, MP):
            zz = place.other_z(r)
            moves.wait(from_z[g].at[zz], "from_z", g * MP + zz)
            total = total + from_z[g][zz].astype(WIDE)
        outs[g][...] = total

    for p in range(pieces):
        moves.wait(ends_ref.at[p], "back", p)
    moves.finish()


def scatter(table, first, last, grads, shapes):
    S, DP, MP = (lax.axis_size(name) for name in ("section", "dp", "mp"))
    Y, H = DP // 2, MP // 2
    _, rows, block = first.shape
    pieces = grads["pieces"]
    flat = [grads[name][layer] for name in ("qkv", "out", "fc1", "fc2") for layer in range(S)]
    counts = scatter_counts(S, Y, MP, pieces)
    vmem = pl.BlockSpec(memory_space=pltpu.VMEM)

    def room(count):
        return [pltpu.VMEM((count,) + shape, LOW) for shape in shapes]

    sends = 2 + Y - 1 + MP - 1 + S * MP + 4 * ((Y - 1) * H * 2 + H * Y + H * Y + MP)
    return pl.pallas_call(
        functools.partial(scatter_kernel, pieces),
        in_specs=[vmem] + [HBM] * (2 + len(flat)),
        out_specs=[HBM] + [vmem] * 5,
        out_shape=[jax.ShapeDtypeStruct((pieces, rows, block), LOW), jax.ShapeDtypeStruct(table.shape[4:], WIDE)]
        + [jax.ShapeDtypeStruct(shape, WIDE) for shape in shapes],
        scratch_shapes=room(MP)
        + room(H)
        + room((Y - 1) * H)
        + room((Y - 1) * H)
        + room((Y - 1) * H)
        + room(MP)
        + room((Y - 1) * MP)
        + room(MP)
        + [
            pltpu.SemaphoreType.DMA((sends,)),
            pltpu.SemaphoreType.DMA((sum(counts.values()),)),
            pltpu.SemaphoreType.DMA((4 * (H * Y + MP),)),
            pltpu.VMEM(table.shape[1:], WIDE),
            pltpu.VMEM(table.shape[1:], WIDE),
            pltpu.VMEM(table.shape[2:], WIDE),
            pltpu.VMEM((Y - 1,) + table.shape[3:], WIDE),
            pltpu.VMEM(table.shape[3:], WIDE),
        ],
        compiler_params=pltpu.CompilerParams(has_side_effects=True, vmem_limit_bytes=60 << 20),
    )(table, first, last, *flat)


def nn(left, right):
    return lax.dot_general(left, right, (((1,), (0,)), ((), ())), preferred_element_type=WIDE)


def nt(left, right):
    return lax.dot_general(left, right, (((1,), (1,)), ((), ())), preferred_element_type=WIDE)


def tn(left, right):
    return lax.dot_general(left, right, (((0,), (0,)), ((), ())), preferred_element_type=WIDE)


def row_mean(value):
    return jnp.mean(value, 1, keepdims=True)


def column_sum(value):
    return jnp.sum(value.astype(WIDE), 0, keepdims=True)


def centre(rows_in):
    mean = row_mean(rows_in)
    inv_std = lax.rsqrt(row_mean(rows_in * rows_in) - mean * mean + epsilon)
    return (rows_in - mean) * inv_std, inv_std


def norm_back(grad, rows_in, gain):
    xhat, inv_std = centre(rows_in)
    weighted = grad * gain
    d_rows = inv_std * (weighted - row_mean(weighted) - xhat * row_mean(weighted * xhat))
    return d_rows, column_sum(grad * xhat), column_sum(grad)


def full(shape):
    return pl.BlockSpec(shape, lambda i: (0,) * len(shape))


def compute_call(kernel, steps, ins, outs, scratch, flops, args):
    return pl.pallas_call(
        kernel,
        grid=(steps,),
        in_specs=ins,
        out_specs=[spec for spec, _ in outs],
        out_shape=[shape for _, shape in outs],
        scratch_shapes=scratch,
        compiler_params=pltpu.CompilerParams(vmem_limit_bytes=58 << 20),
        cost_estimate=pl.CostEstimate(flops=flops, bytes_accessed=40 << 20, transcendentals=0),
    )(*args)


LN1_GAIN, LN1_BIAS, B_QUERY, B_VALUE, B_OUT, SCALE_ATTN, LN2_GAIN, LN2_BIAS, B_FC2, SCALE_MLP = range(10)


def project_kernel(x_ref, vec_ref, w_ref, n_ref, kv_ref, q_ref, held):
    step = pl.program_id(0)

    @pl.when(step == 0)
    def _():
        xhat, _ = centre(x_ref[...])
        low = (xhat * vec_ref[LN1_GAIN][None] + vec_ref[LN1_BIAS][None]).astype(LOW)
        held[...] = low
        n_ref[...] = low

    value = nn(held[...], w_ref[...])

    @pl.when(step == 0)
    def _():
        kv_ref[0] = value.astype(LOW)

    @pl.when(step == 1)
    def _():
        kv_ref[1] = (value + vec_ref[B_VALUE][None]).astype(LOW)

    @pl.when(step == 2)
    def _():
        q_ref[...] = (value + vec_ref[B_QUERY][None]).astype(LOW)


def project(rows_in, vec, attn, layer):
    rows, width = rows_in.shape
    low = jax.ShapeDtypeStruct((rows, width), LOW)
    return compute_call(
        project_kernel,
        3,
        [
            full(rows_in.shape),
            full(vec.shape),
            pl.BlockSpec((None, None, width, width), lambda i: (layer, lax.rem(i + 1, 3), 0, 0)),
        ],
        [
            (full(rows_in.shape), low),
            (full((2, rows, width)), jax.ShapeDtypeStruct((2, rows, width), LOW)),
            (full(rows_in.shape), low),
        ],
        [pltpu.VMEM((rows, width), LOW)],
        6 * rows * width * width,
        (rows_in, vec, attn),
    )


def attend_kernel(q_ref, k0, k1, v0, v1, mask_ref, o_ref, wide_ref, p_ref):
    bias0, bias1 = mask_ref[:, 0:1], mask_ref[:, 1:2]
    outs = []
    for head in range(q_ref.shape[1] // HD):
        at = slice(head * HD, head * HD + HD)
        q = (q_ref[:, at].astype(WIDE) * (HD**-0.5)).astype(LOW)
        s0 = nt(k0[:, at], q) + bias0
        s1 = nt(k1[:, at], q) + bias1
        top = jnp.maximum(jnp.max(s0, 0, keepdims=True), jnp.max(s1, 0, keepdims=True))
        e0 = jnp.exp(s0 - top)
        e1 = jnp.exp(s1 - top)
        scale = 1.0 / (jnp.sum(e0, 0, keepdims=True) + jnp.sum(e1, 0, keepdims=True))
        p0 = (e0 * scale).astype(LOW)
        p1 = (e1 * scale).astype(LOW)
        p_ref[head, 0] = p0
        p_ref[head, 1] = p1
        outs.append(tn(v0[:, at], p0) + tn(v1[:, at], p1))
    out = jnp.concatenate(outs, 0).T
    wide_ref[...] = out
    o_ref[...] = out.astype(LOW)


def attend(q, kv0, kv1, mask):
    rows, width = q.shape
    steps, heads = width // 128, width // HD
    one = pl.BlockSpec((rows, 128), lambda i: (0, i))
    key = pl.BlockSpec((None, rows, 128), lambda i: (0, 0, i))
    value = pl.BlockSpec((None, rows, 128), lambda i: (1, 0, i))
    return compute_call(
        attend_kernel,
        steps,
        [one, key, key, value, value, full(mask.shape)],
        [
            (one, jax.ShapeDtypeStruct((rows, width), LOW)),
            (one, jax.ShapeDtypeStruct((rows, width), WIDE)),
            (
                pl.BlockSpec((2, 2, rows, rows), lambda i: (i, 0, 0, 0)),
                jax.ShapeDtypeStruct((heads, 2, rows, rows), LOW),
            ),
        ],
        [],
        32 * heads * rows * rows * HD,
        (q, kv0, kv1, kv0, kv1, mask),
    )


def mlp_kernel(x_ref, o_ref, vec_ref, bias_ref, wo_ref, w1_ref, w2_ref, y_ref, branch_ref, middle_ref, n_ref, act_ref, slope_ref, two_ref, total):
    step = pl.program_id(0)

    @pl.when(step == 0)
    def _():
        branch = nt(o_ref[...], wo_ref[...]) + vec_ref[B_OUT][None]
        branch_ref[...] = branch.astype(LOW)
        middle = x_ref[...] + vec_ref[SCALE_ATTN][None] * branch
        middle_ref[...] = middle
        xhat, _ = centre(middle)
        n_ref[...] = (xhat * vec_ref[LN2_GAIN][None] + vec_ref[LN2_BIAS][None]).astype(LOW)
        total[...] = jnp.zeros_like(total)

    hidden = nn(n_ref[...], w1_ref[...]) + bias_ref[0:1]
    cdf = 0.5 + 0.5 * lax.erf(hidden * inv_root_two)
    active = (hidden * cdf).astype(LOW)
    act_ref[...] = active
    slope_ref[...] = (cdf + hidden * jnp.exp(-0.5 * hidden * hidden) * inv_root_tau).astype(LOW)
    total[...] += nt(active, w2_ref[...])

    @pl.when(step == pl.num_programs(0) - 1)
    def _():
        two = total[...] + vec_ref[B_FC2][None]
        two_ref[...] = two.astype(LOW)
        y_ref[...] = middle_ref[...] + vec_ref[SCALE_MLP][None] * two


CHUNK = 512


def mlp(rows_in, out, vec, bias, weights, layer):
    attn, fc1, fc2 = weights
    rows, width = rows_in.shape
    hidden = fc1.shape[2]
    low = (full(rows_in.shape), jax.ShapeDtypeStruct((rows, width), LOW))
    wide = (full(rows_in.shape), jax.ShapeDtypeStruct((rows, width), WIDE))
    units = (pl.BlockSpec((rows, CHUNK), lambda i: (0, i)), jax.ShapeDtypeStruct((rows, hidden), LOW))
    weight = pl.BlockSpec((None, width, CHUNK), lambda i: (layer, 0, i))
    return compute_call(
        mlp_kernel,
        hidden // CHUNK,
        [
            full(rows_in.shape),
            full(rows_in.shape),
            full(vec.shape),
            pl.BlockSpec((8, CHUNK), lambda i: (0, i)),
            pl.BlockSpec((None, None, width, width), lambda i: (layer, 3, 0, 0)),
            weight,
            weight,
        ],
        [wide, low, wide, low, units, units, low],
        [pltpu.VMEM((rows, width), WIDE)],
        4 * rows * width * hidden,
        (rows_in, out, vec, bias, attn, fc1, fc2),
    )


def store_halves(value, even_first, own_ref, there_ref, lead=()):
    count = own_ref.shape[len(lead)]
    size = own_ref.shape[len(lead) + 1]
    for d in range(2 * count):
        part = value[d * size : (d + 1) * size].astype(LOW)

        def put(ref, part=part, d=d):
            ref[lead + (d // 2,)] = part

        if d % 2 == 0:
            pl.when(even_first)(lambda: put(own_ref))
            pl.when(jnp.logical_not(even_first))(lambda: put(there_ref))
        else:
            pl.when(even_first)(lambda: put(there_ref))
            pl.when(jnp.logical_not(even_first))(lambda: put(own_ref))


def mlp_back_kernel(
    c_ref, dy_ref, vec_ref, two_ref, act_ref, slope_ref, n_ref, middle_ref, branch_ref, o_ref, wo_ref, w1_ref, w2_ref,
    grad_ref, do_ref, own1, there1, own2, there2, own_o, there_o, sums_ref, units_ref, dm, total,
):
    step = pl.program_id(0)
    even = c_ref[0] == 0

    @pl.when(step == 0)
    def _():
        low = (dy_ref[...] * vec_ref[SCALE_MLP][None]).astype(LOW)
        dm[...] = low
        sums_ref[0:1] = column_sum(dy_ref[...] * two_ref[...].astype(WIDE))
        sums_ref[1:2] = column_sum(low)
        total[...] = jnp.zeros_like(total)

    df = (nn(dm[...], w2_ref[...]) * slope_ref[...].astype(WIDE)).astype(LOW)
    units_ref[...] = jnp.broadcast_to(column_sum(df), units_ref.shape)
    store_halves(tn(dm[...], act_ref[...]), even, own2, there2)
    store_halves(tn(n_ref[...], df), even, own1, there1)
    total[...] += nt(df, w1_ref[...])

    @pl.when(step == pl.num_programs(0) - 1)
    def _():
        d_rows, d_gain, d_bias = norm_back(total[...], middle_ref[...], vec_ref[LN2_GAIN][None])
        sums_ref[2:3] = d_gain
        sums_ref[3:4] = d_bias
        grad = dy_ref[...] + d_rows
        grad_ref[...] = grad
        sums_ref[4:5] = column_sum(grad * branch_ref[...].astype(WIDE))
        da = (grad * vec_ref[SCALE_ATTN][None]).astype(LOW)
        sums_ref[5:6] = column_sum(da)
        sums_ref[6:8] = jnp.zeros((2, sums_ref.shape[1]), WIDE)
        do_ref[...] = nn(da, wo_ref[...]).astype(LOW)
        store_halves(tn(da, o_ref[...]), even, own_o, there_o)


def mlp_back(half, dy, vec, saved, weights, layer, count):
    attn, fc1, fc2 = weights
    rows, width = dy.shape
    hidden = fc1.shape[2]
    block = width // (2 * count)
    whole = full(dy.shape)
    low = (whole, jax.ShapeDtypeStruct((rows, width), LOW))
    wide = (whole, jax.ShapeDtypeStruct((rows, width), WIDE))
    units = pl.BlockSpec((rows, CHUNK), lambda i: (0, i))
    weight = pl.BlockSpec((None, width, CHUNK), lambda i: (layer, 0, i))
    grad = (
        pl.BlockSpec((count, block, CHUNK), lambda i: (0, 0, i)),
        jax.ShapeDtypeStruct((count, block, hidden), LOW),
    )
    grad_o = (full((count, block, width)), jax.ShapeDtypeStruct((count, block, width), LOW))
    return compute_call(
        mlp_back_kernel,
        hidden // CHUNK,
        [
            pl.BlockSpec(memory_space=pltpu.SMEM),
            whole,
            full(vec.shape),
            whole,
            units,
            units,
            whole,
            whole,
            whole,
            whole,
            pl.BlockSpec((None, None, width, width), lambda i: (layer, 3, 0, 0)),
            weight,
            weight,
        ],
        [
            wide,
            low,
            grad,
            grad,
            grad,
            grad,
            grad_o,
            grad_o,
            (full((8, width)), jax.ShapeDtypeStruct((8, width), WIDE)),
            (pl.BlockSpec((8, CHUNK), lambda i: (0, i)), jax.ShapeDtypeStruct((8, hidden), WIDE)),
        ],
        [pltpu.VMEM((rows, width), LOW), pltpu.VMEM((rows, width), WIDE)],
        8 * rows * width * hidden,
        (
            half,
            dy,
            vec,
            saved["two"],
            saved["active"],
            saved["slope"],
            saved["n_two"],
            saved["middle"],
            saved["branch"],
            saved["out"],
            attn,
            fc1,
            fc2,
        ),
    )


def attend_back_kernel(q_ref, k0, k1, v0, v1, p_ref, g_ref, o_ref, d0_ref, d1_ref):
    outs = []
    for head in range(q_ref.shape[1] // HD):
        at = slice(head * HD, head * HD + HD)
        q = q_ref[:, at]
        g = g_ref[:, at]
        prod = g.astype(WIDE) * o_ref[:, at]
        dot = jnp.sum(prod.T, 0, keepdims=True)
        dq = None
        for half, (k, v, out, first) in enumerate(((k0, v0, d0_ref, 1), (k1, v1, d1_ref, 0))):
            p = p_ref[head, half]
            out[first + 1, :, at] = nn(p, g).astype(LOW)
            ds = (p.astype(WIDE) * (nt(v[:, at], g) - dot)).astype(LOW)
            part = tn(k[:, at], ds)
            dq = part if dq is None else dq + part
            out[first, :, at] = (nn(ds, q) * (HD**-0.5)).astype(LOW)
        outs.append(dq * (HD**-0.5))
    d0_ref[0] = jnp.concatenate(outs, 0).T.astype(LOW)


def attend_back(q, kv0, kv1, probs, grad, out):
    rows, width = q.shape
    steps, heads = width // 128, width // HD
    one = pl.BlockSpec((rows, 128), lambda i: (0, i))
    key = pl.BlockSpec((None, rows, 128), lambda i: (0, 0, i))
    value = pl.BlockSpec((None, rows, 128), lambda i: (1, 0, i))

    def several(count):
        return (
            pl.BlockSpec((count, rows, 128), lambda i: (0, 0, i)),
            jax.ShapeDtypeStruct((count, rows, width), LOW),
        )

    return compute_call(
        attend_back_kernel,
        steps,
        [one, key, key, value, value, pl.BlockSpec((2, 2, rows, rows), lambda i: (i, 0, 0, 0)), one, one],
        [several(3), several(2)],
        [],
        40 * heads * rows * rows * HD,
        (q, kv0, kv1, kv0, kv1, probs, grad, out),
    )


def project_back_kernel(
    c_ref, d0_ref, d1_ref, n_ref, x_ref, grad_ref, vec_ref, w_ref, dx_ref, own, there, sums_ref, total
):
    step = pl.program_id(0)
    even = c_ref[0] == 0

    @pl.when(step == 0)
    def _():
        total[...] = jnp.zeros_like(total)

    theirs = jnp.where(step == 0, 0.0, d1_ref[...].astype(WIDE))
    grad = (d0_ref[...].astype(WIDE) + theirs).astype(LOW)
    store_halves(tn(n_ref[...], grad), even, own, there)
    total[...] += nt(grad, w_ref[...])
    sums = column_sum(grad)

    @pl.when(step == 0)
    def _():
        sums_ref[0:1] = sums

    @pl.when(step == 2)
    def _():
        sums_ref[1:2] = sums
        d_rows, d_gain, d_bias = norm_back(total[...], x_ref[...], vec_ref[LN1_GAIN][None])
        sums_ref[2:3] = d_gain
        sums_ref[3:4] = d_bias
        sums_ref[4:8] = jnp.zeros((4, sums_ref.shape[1]), WIDE)
        dx_ref[...] = grad_ref[...] + d_rows


def project_back(half, d0, d1, saved, grad, vec, attn, layer, count):
    rows, width = grad.shape
    block = width // (2 * count)
    whole = full(grad.shape)
    out = (
        pl.BlockSpec((None, count, block, width), lambda i: (i, 0, 0, 0)),
        jax.ShapeDtypeStruct((3, count, block, width), LOW),
    )
    return compute_call(
        project_back_kernel,
        3,
        [
            pl.BlockSpec(memory_space=pltpu.SMEM),
            pl.BlockSpec((None, rows, width), lambda i: (i, 0, 0)),
            pl.BlockSpec((None, rows, width), lambda i: (jnp.maximum(i - 1, 0), 0, 0)),
            whole,
            whole,
            whole,
            full(vec.shape),
            pl.BlockSpec((None, None, width, width), lambda i: (layer, i, 0, 0)),
        ],
        [
            (whole, jax.ShapeDtypeStruct((rows, width), WIDE)),
            out,
            out,
            (full((8, width)), jax.ShapeDtypeStruct((8, width), WIDE)),
        ],
        [pltpu.VMEM((rows, width), WIDE)],
        12 * rows * width * width,
        (half, d0, d1, saved["n_one"], saved["rows_in"], grad, vec, attn),
    )


def pick(stack, index, axis=0):
    return lax.dynamic_index_in_dim(stack, index, axis, keepdims=False)


def layer_forward(rows_in, vec, bias, weights, layer, mask, from_pair):
    n_one, kv0, q = project(rows_in, vec, weights[0], layer)
    kv1 = from_pair(kv0)
    out, out_wide, probs = attend(q, kv0, kv1, mask)
    leaving, branch, middle, n_two, active, slope, two = mlp(rows_in, out, vec, bias, weights, layer)
    saved = dict(
        rows_in=rows_in,
        n_one=n_one,
        q=q,
        kv0=kv0,
        kv1=kv1,
        out=out,
        out_wide=out_wide,
        probs=probs,
        branch=branch,
        middle=middle,
        n_two=n_two,
        active=active,
        slope=slope,
        two=two,
    )
    return (leaving, saved)


def layer_backward(grad_rows, saved, vec, weights, layer, half, from_pair):
    count = lax.axis_size("dp") // 2
    grad_middle, d_out, own1, there1, own2, there2, own_o, there_o, sums, units = mlp_back(
        half, grad_rows, vec, saved, weights, layer, count
    )

    def joined(own, there):
        return (own.astype(WIDE) + from_pair(there).astype(WIDE)).astype(LOW)

    g_fc2, g_fc1, g_out = joined(own2, there2), joined(own1, there1), joined(own_o, there_o)
    d0, d1 = attend_back(saved["q"], saved["kv0"], saved["kv1"], saved["probs"], d_out, saved["out_wide"])
    grad_in, own, there, sums_one = project_back(
        half, d0, from_pair(d1), saved, grad_middle, vec, weights[0], layer, count
    )
    g_qkv = joined(own, there)
    vectors = dict(
        ln1_gain=sums_one[2],
        ln1_bias=sums_one[3],
        b_query=sums_one[0],
        b_value=sums_one[1],
        b_out=sums[5],
        scale_attn=sums[4],
        ln2_gain=sums[2],
        ln2_bias=sums[3],
        b_fc1=units[0],
        b_fc2=sums[1],
        scale_mlp=sums[0],
    )
    return (grad_in, dict(qkv=g_qkv, out=g_out, fc1=g_fc1, fc2=g_fc2), vectors)


NARROW = ("ln1_gain", "ln1_bias", "b_query", "b_value", "b_out", "scale_attn", "ln2_gain", "ln2_bias", "b_fc2", "scale_mlp")


def local(
    boundary,
    ln1_gain,
    ln1_bias,
    w_query,
    w_key,
    w_value,
    b_query,
    b_value,
    w_out,
    b_out,
    scale_attn,
    ln2_gain,
    ln2_bias,
    w_fc1,
    b_fc1,
    w_fc2,
    b_fc2,
    scale_mlp,
):
    place = Place()
    _, micros, images, seq_len, columns = boundary.shape
    S, DP, MP = place.S, place.DP, place.MP
    width = columns * MP
    rows = -(-seq_len // 32) * 16
    pieces = 2 * micros
    number = place.s * MP + place.z
    active = number < pieces

    def from_pair(value):
        return lax.ppermute(value, "dp", [(i, i + 1 - 2 * (i % 2)) for i in range(DP)])

    images_low = boundary.reshape(micros, seq_len, columns).astype(LOW)
    sent = jnp.pad(images_low, ((0, 0), (0, 2 * rows - seq_len), (0, 0))).reshape(pieces, rows, columns)
    keys = jnp.arange(rows)[:, None] + rows * jnp.stack([place.c, 1 - place.c])[None]
    mask = jnp.where(keys < seq_len, 0.0, -1e30).astype(WIDE)
    mask = jnp.pad(mask, ((0, 0), (0, 126)))
    half = place.c.reshape(1)
    narrow = (ln1_gain, ln1_bias, b_query, b_value, b_out, scale_attn, ln2_gain, ln2_bias, b_fc2, scale_mlp)
    packed = jnp.concatenate([v[0] for v in narrow] + [b_fc1[0]])
    lines = -(-packed.shape[0] // 1024) * 8
    packed = jnp.pad(packed, (0, lines * 128 - packed.shape[0])).reshape(lines, 128)
    attn_shard = jnp.stack([w_query[0], w_key[0], w_value[0], w_out[0].T])
    arrived, vecs, *weights = gather(sent, packed, attn_shard, w_fc1[0], w_fc2[0].T)
    arrived = jnp.where(active, arrived.astype(WIDE), 0.0)
    vecs = vecs.reshape(S, MP, -1)
    vectors, biases = [], []
    for layer in range(S):
        start = len(NARROW) * columns
        table = vecs[layer, :, :start].reshape(MP, len(NARROW), columns)
        table = jnp.moveaxis(table, 0, 1).reshape(len(NARROW), width)
        vectors.append(jnp.pad(table, ((0, 16 - len(NARROW)), (0, 0))))
        bias = vecs[layer, :, start : start + b_fc1.shape[1]].reshape(1, -1)
        biases.append(jnp.pad(bias, ((0, 7), (0, 0))))

    saved = []
    rows_now = arrived[0]
    for layer in range(S):
        rows_now, kept = layer_forward(rows_now, vectors[layer], biases[layer], weights, layer, mask, from_pair)
        saved.append(kept)
        if layer + 1 < S:
            rows_now = rows_now.astype(LOW).astype(WIDE)
    end_rows = rows_now

    grad_now = arrived[1]
    matrix_grads, vector_grads = [None] * S, [None] * S
    for layer in reversed(range(S)):
        grad_now, matrix_grads[layer], vector_grads[layer] = layer_backward(
            grad_now, saved[layer], vectors[layer], weights, layer, half, from_pair
        )
        if layer:
            grad_now = grad_now.astype(LOW).astype(WIDE)

    def by_column(value):
        return jnp.stack([value[:, i * columns : (i + 1) * columns].astype(LOW) for i in range(MP)])

    grads = {name: [matrix_grads[layer][name] for layer in range(S)] for name in ("qkv", "out", "fc1", "fc2")}
    grads["pieces"] = pieces
    shapes = [(3,) + w_query.shape[1:], w_query.shape[1:], w_fc1.shape[1:], (w_fc2.shape[2], w_fc2.shape[1])]
    names = NARROW + ("b_fc1",)
    table = jnp.stack(
        [
            jnp.concatenate([vector_grads[layer][name].reshape(MP, DP, -1) for name in names], 2)
            for layer in range(S)
        ]
    )
    lines = -(-table.shape[3] // 1024) * 8
    table = jnp.pad(table, ((0, 0), (0, 0), (0, 0), (0, lines * 128 - table.shape[3])))
    table = table.reshape(S, MP, DP // 2, 2, lines, 128).transpose(3, 0, 2, 1, 4, 5)
    ends, summed, g_qkv, g_out, g_fc1, g_fc2 = scatter(table, by_column(grad_now), by_column(end_rows), grads, shapes)
    ends_out = ends.reshape(micros, 2 * rows, columns)[:, :seq_len].astype(WIDE).reshape(boundary.shape)
    summed = summed.reshape(-1)
    v, start = {}, 0
    for name in names:
        size = (b_fc1.shape[1] if name == "b_fc1" else columns) // DP
        v[name] = summed[start : start + size][None]
        start += size

    return (
        ends_out,
        v["ln1_gain"],
        v["ln1_bias"],
        g_qkv[0][None],
        g_qkv[1][None],
        g_qkv[2][None],
        v["b_query"],
        v["b_value"],
        g_out.T[None],
        v["b_out"],
        v["scale_attn"],
        v["ln2_gain"],
        v["ln2_bias"],
        g_fc1[None],
        v["b_fc1"],
        g_fc2.T[None],
        v["b_fc2"],
        v["scale_mlp"],
    )


def solution(mesh):
    return jax.shard_map(
        local,
        mesh=mesh,
        in_specs=(
            P("section", None, "dp", None, "mp"),
            P("section", "mp"),
            P("section", "mp"),
            P("section", "dp", "mp"),
            P("section", "dp", "mp"),
            P("section", "dp", "mp"),
            P("section", "mp"),
            P("section", "mp"),
            P("section", "mp", "dp"),
            P("section", "mp"),
            P("section", "mp"),
            P("section", "mp"),
            P("section", "mp"),
            P("section", "dp", "mp"),
            P("section", "mp"),
            P("section", "mp", "dp"),
            P("section", "mp"),
            P("section", "mp"),
        ),
        out_specs=(
            P("section", None, "dp", None, "mp"),
            P("section", ("mp", "dp")),
            P("section", ("mp", "dp")),
            P("section", "dp", "mp"),
            P("section", "dp", "mp"),
            P("section", "dp", "mp"),
            P("section", ("mp", "dp")),
            P("section", ("mp", "dp")),
            P("section", "mp", "dp"),
            P("section", ("mp", "dp")),
            P("section", ("mp", "dp")),
            P("section", ("mp", "dp")),
            P("section", ("mp", "dp")),
            P("section", "dp", "mp"),
            P("section", ("mp", "dp")),
            P("section", "mp", "dp"),
            P("section", ("mp", "dp")),
            P("section", ("mp", "dp")),
        ),
        check_vma=False,
    )
```

```python
import functools

import jax
import jax.numpy as jnp
from jax import lax
from jax.experimental import pallas as pl
from jax.experimental.pallas import tpu as pltpu
from jax.sharding import PartitionSpec as P


HD = 64
LOW = jnp.bfloat16
WIDE = jnp.float32
HBM = pl.BlockSpec(memory_space=pl.ANY)

epsilon = 1e-06
inv_root_two = 0.7071067811865476
inv_root_tau = 0.3989422804014327


class Place:
    def __init__(self):
        self.S = lax.axis_size("section")
        self.DP = lax.axis_size("dp")
        self.MP = lax.axis_size("mp")
        self.Y = self.DP // 2
        self.H = self.MP // 2
        self.s = lax.axis_index("section")
        self.d = lax.axis_index("dp")
        self.z = lax.axis_index("mp")
        self.y = lax.div(self.d, 2)
        self.c = lax.rem(self.d, 2)
        self.nearest = sorted(range(self.MP), key=lambda r: min(r, self.MP - r))

    def other_y(self, r):
        return lax.rem(self.y + r, self.Y)

    def other_z(self, r):
        return lax.rem(self.z + r, self.MP)


class Moves:
    def __init__(self, send_sems, recv_sems, counts):
        self.send_sems, self.recv_sems = send_sems, recv_sems
        self.base, total = {}, 0
        for name, count in counts.items():
            self.base[name] = total
            total += count
        self.total = total
        self.sent = []

    def arrival(self, name, index):
        return self.recv_sems.at[self.base[name] + index]

    def send(self, src, dst, name, index, when=None, **to):
        at = len(self.sent)
        assert at < self.send_sems.shape[0]
        copy = pltpu.make_async_remote_copy(
            src_ref=src,
            dst_ref=dst,
            send_sem=self.send_sems.at[at],
            recv_sem=self.arrival(name, index),
            device_id=to,
        )
        self.sent.append((copy, when))
        if when is None:
            copy.start()
        else:
            pl.when(when)(copy.start)

    def send_one_of(self, options, name, when, **to):
        at = len(self.sent)
        assert at < self.send_sems.shape[0]
        for cond, src, dst, index in options:
            copy = pltpu.make_async_remote_copy(
                src_ref=src,
                dst_ref=dst,
                send_sem=self.send_sems.at[at],
                recv_sem=self.arrival(name, index),
                device_id=to,
            )
            pl.when(cond)(copy.start)
        self.sent.append((copy, when))

    def wait(self, ref, name, index):
        pltpu.make_async_copy(ref, ref, self.arrival(name, index)).wait()

    def finish(self):
        for copy, when in self.sent:
            if when is None:
                copy.wait_send()
            else:
                pl.when(when)(copy.wait_send)


def tile(start, size):
    return pl.ds(pl.multiple_of(start * size, size), size)


def holder(place, c, piece):
    image = 2 * (piece // 2) + c
    return lax.div(image, place.MP), piece % 2, lax.rem(image, place.MP)


def gather_counts(S, Y, MP, groups=3):
    return dict(rows=MP, vectors=S * MP, piece=groups * S * Y * MP, pair=groups * S * Y * MP)


def gather_kernel(pieces, sent_ref, vec_ref, a_ref, b_ref, c_ref, rows_ref, vecs_ref, *refs):
    place = Place()
    s, y, c, z, d = place.s, place.y, place.c, place.z, place.d
    S, Y, MP, H = place.S, place.Y, place.MP, place.H
    shards = (a_ref, b_ref, c_ref)
    wholes = (refs[0:S], refs[S : 2 * S], refs[2 * S : 3 * S])
    send_sems, recv_sems, own_sems = refs[3 * S :]
    moves = Moves(send_sems, recv_sems, gather_counts(S, Y, MP))
    columns = sent_ref.shape[2]

    def spot(g, l, yy, cc, zz):
        dd = yy * 2 + cc
        shard, whole = shards[g], wholes[g][l]
        at = (tile(dd, shard.shape[-2]), tile(zz, shard.shape[-1]))
        return whole.at[(slice(None),) + at] if len(shard.shape) == 3 else whole.at[at]

    def mark(g, l, yy, zz):
        return ((g * S + l) * Y + yy) * MP + zz

    def each(mine):
        return [(layer, (s == layer) if mine else (s != layer)) for layer in range(S)]

    def hand(g, mine, yy, zz, name, when, src, **to):
        moves.send_one_of(
            [
                (
                    cond if when is None else cond & when,
                    spot(g, layer, yy, c, zz) if src is None else src,
                    spot(g, layer, yy, c, zz),
                    mark(g, layer, yy, zz),
                )
                for layer, cond in each(mine)
            ],
            name,
            when,
            **to,
        )

    def to_pair(g, mine, zz, src=None, when=None):
        hand(g, mine, y, zz, "pair", when, src, section=s, dp=y * 2 + 1 - c, mp=z)

    def to_section(g, zz, when=None, src=None):
        hand(g, True, y, zz, "piece", when, src, section=1 - s, dp=d, mp=z)

    def along(g, zz, step, when, src=None):
        hand(g, True, y, zz, "piece", when, src, section=s, dp=d, mp=jnp.clip(z + step, 0, MP - 1))

    def rows_if(g, mine, zz, first_layer, there, src=None):
        when = first_layer | (zz < H) if g == 1 else first_layer
        for r in range(1, Y):
            hand(g, mine, y, zz, "piece", when & there, src, section=s, dp=place.other_y(r) * 2 + c, mp=z)

    def landed(g, l, yy, zz):
        moves.wait(spot(g, 0, yy, c, zz), "piece", mark(g, l, yy, zz))

    own_copies = []

    def columns_out(g):
        along(g, z, 1, z + 1 < MP, shards[g])
        along(g, z, -1, z >= 1, shards[g])
        to_section(g, z, src=shards[g])
        rows_if(g, True, z, s == 0, z >= 0, shards[g])
        to_pair(g, True, z, shards[g])
        for layer, cond in each(True):
            copy = pltpu.make_async_copy(shards[g], spot(g, layer, y, c, z), own_sems.at[g])
            pl.when(cond)(copy.start)
        own_copies.append(copy)

    def columns_in(g, far):
        for step, there in ((1, z >= far), (-1, z + far < MP)):
            zz = jnp.clip(z - step * far, 0, MP - 1)

            @pl.when(there)
            def _():
                landed(g, s, y, zz)

            along(g, zz, step, there & ((z + 1 < MP) if step == 1 else (z >= 1)))
            to_section(g, zz, there)
            rows_if(g, True, zz, s == 0, there)
            to_pair(g, True, zz, when=there)

    def section_in(g, far):
        for step, there in ((1, z >= far), (-1, z + far < MP))[: 2 if far else 1]:
            zz = jnp.clip(z - step * far, 0, MP - 1)

            @pl.when(there)
            def _():
                landed(g, 1 - s, y, zz)

            rows_if(g, False, zz, s == 1, there)
            to_pair(g, False, zz, when=there)

    def rows_in(g):
        for r in range(1, Y):
            yy = place.other_y(r)
            for layer, zz in [(0, zz) for zz in range(MP)] + ([(1, zz) for zz in range(H)] if g == 1 else []):
                landed(g, layer, yy, zz)
                there = spot(g, layer, yy, c, zz)
                moves.send(there, there, "pair", mark(g, layer, yy, zz), section=s, dp=y * 2 + 1 - c, mp=z)

    for q in range(1, S * MP):
        at = lax.rem(s * MP + z + q, S * MP)
        moves.send(vec_ref, vecs_ref.at[s * MP + z], "vectors", s * MP + z, section=lax.div(at, MP), dp=d, mp=lax.rem(at, MP))
    own_vec = pltpu.make_async_copy(vec_ref, vecs_ref.at[s * MP + z], own_sems.at[3])
    own_vec.start()

    for g in range(3):
        columns_out(g)
    for piece in range(pieces):
        to_s, to_c, to_z = holder(place, c, piece)
        here = (to_s == s) & (to_c == c) & (to_z == z)
        there = rows_ref.at[:, tile(z, columns)]
        moves.send(
            sent_ref.at[piece], there, "rows", z, (s == 0) & jnp.logical_not(here),
            section=to_s, dp=y * 2 + to_c, mp=to_z,
        )

        @pl.when((s == 0) & here)
        def _():
            pltpu.make_async_copy(sent_ref.at[piece], there, moves.arrival("rows", z)).start()

    for far in range(1, MP):
        for g in range(3):
            columns_in(g, far)
            section_in(g, far - 1)
    for g in range(3):
        section_in(g, MP - 1)
    for g in range(3):
        rows_in(g)

    @pl.when(s * MP + z < pieces)
    def _():
        for zz in range(MP):
            moves.wait(rows_ref.at[:, tile(zz, columns)], "rows", zz)

    for q in range(1, S * MP):
        at = lax.rem(s * MP + z + q, S * MP)
        moves.wait(vecs_ref.at[at], "vectors", at)
    for g in range(3):
        for zz in range(MP):
            for r in range(Y):
                yy = place.other_y(r)
                moves.wait(spot(g, 0, yy, 1 - c, zz), "pair", mark(g, 0, yy, zz))
                if g == 1 and zz < H and r:
                    moves.wait(spot(g, 1, yy, 1 - c, zz), "pair", mark(g, 1, yy, zz))
            for layer in range(1, S):
                moves.wait(spot(g, 0, y, 1 - c, zz), "pair", mark(g, layer, y, zz))
    own_vec.wait()
    for copy in own_copies:
        copy.wait()
    moves.finish()


def gather(sent, vec, a, b, c):
    S, DP, MP = (lax.axis_size(name) for name in ("section", "dp", "mp"))
    Y = DP // 2
    pieces, rows, columns = sent.shape
    counts = gather_counts(S, Y, MP)
    sends = pieces + S * MP - 1 + 3 * (2 * MP + (2 * MP - 1) * (1 + 2 * Y) + (Y - 1) * MP) + (Y - 1) * (MP // 2)
    whole = [
        jax.ShapeDtypeStruct(shard.shape[:-2] + (shard.shape[-2] * DP, shard.shape[-1] * MP), LOW) for shard in (a, b, c)
    ]
    got = pl.pallas_call(
        functools.partial(gather_kernel, pieces),
        in_specs=[HBM] * 5,
        out_specs=[HBM] * (2 + 3 * S),
        out_shape=[
            jax.ShapeDtypeStruct((rows, columns * MP), LOW),
            jax.ShapeDtypeStruct((S * MP,) + vec.shape, WIDE),
        ]
        + [shape for shape in whole for _ in range(S)],
        scratch_shapes=[
            pltpu.SemaphoreType.DMA((sends,)),
            pltpu.SemaphoreType.DMA((sum(counts.values()),)),
            pltpu.SemaphoreType.DMA((4,)),
        ],
        compiler_params=pltpu.CompilerParams(has_side_effects=True),
    )(sent, vec, a, b, c)
    return got[0], got[1], [[got[2 + g * S + layer] for g in range(3)] for layer in range(S)]


def scatter_counts(S, Y, MP, pieces, groups=4):
    return dict(
        back=max(pieces, MP),
        pair=groups * Y * MP,
        from_x=groups * MP,
        from_y=groups * (Y - 1) * MP,
        from_z=groups * MP,
        vec_pair=1,
        vec_x=1,
        vec_y=Y - 1,
        vec_z=MP,
    )


ORDER = (3, 2, 0, 1)


def scatter_kernel(pieces, table_ref, first_ref, last_ref, *refs):
    place = Place()
    s, y, c, z, d = place.s, place.y, place.c, place.z, place.d
    S, Y, MP = place.S, place.Y, place.MP
    own, there, above = refs[0:4], refs[4:8], refs[8:12]
    ends_ref, sums_ref, outs = refs[12], refs[13], refs[14:18]
    held, paired, mine, from_x, from_y, from_z = (refs[18 + 4 * i : 22 + 4 * i] for i in range(6))
    send_sems, recv_sems, load_sems, vec_here, vec_pair, vec_x, vec_y, vec_z, landing = refs[42:]
    moves = Moves(send_sems, recv_sems, scatter_counts(S, Y, MP, pieces))

    def part(ref, g, zz, yy=None):
        at = (slice(None), tile(zz, outs[g].shape[-1]))
        if yy is not None:
            at = (yy,) + at
        if len(outs[g].shape) == 3:
            at = (slice(None),) + at
        return ref.at[at]

    moves.send(table_ref.at[1 - c], vec_pair, "vec_pair", 0, section=s, dp=y * 2 + 1 - c, mp=z)
    moves.wait(vec_pair, "vec_pair", 0)
    vec_here[...] = table_ref[c] + vec_pair[...]
    moves.send(vec_here.at[1 - s], vec_x, "vec_x", 0, section=1 - s, dp=d, mp=z)

    loads = {}

    def load(src, dst, when, key):
        at = len(loads)
        copy = pltpu.make_async_copy(src, dst, load_sems.at[at])
        if when is None:
            copy.start()
        else:
            pl.when(when)(copy.start)
        loads[key] = (copy, when)

    steps = [(g, k) for g in ORDER for k in place.nearest[::-1]]
    for g, k in steps:
        zz = place.other_z(k)
        for r in list(range(1, Y)) + [0]:
            slot = place.other_y(r) * MP + zz
            moves.send(
                part(there[g], g, zz, place.other_y(r)), paired[g].at[slot], "pair", g * Y * MP + slot,
                section=s, dp=y * 2 + 1 - c, mp=z,
            )
            load(part(own[g], g, zz, place.other_y(r)), held[g].at[slot], None, ("own", g, k, r))
        load(part(above[g], g, zz), mine[g].at[zz], s == 1, ("above", g, k))

    moves.wait(vec_x, "vec_x", 0)
    vec_here[s] = vec_here[s] + vec_x[...]
    for r in range(1, Y):
        at = Y - r - 1
        moves.send(
            vec_here.at[s, place.other_y(r)], vec_y.at[at], "vec_y", at, section=s, dp=place.other_y(r) * 2 + c, mp=z
        )
    for r in range(1, Y):
        moves.wait(vec_y.at[r - 1], "vec_y", r - 1)
    vec_here[s, y] = vec_here[s, y] + jnp.sum(vec_y[...], 0)
    for r in range(1, MP):
        moves.send(vec_here.at[s, y, place.other_z(r)], vec_z.at[z], "vec_z", z, section=s, dp=d, mp=place.other_z(r))

    number = s * MP + z
    active = number < pieces
    piece = 2 * lax.div(number, 2) + c
    for section, ref in ((0, first_ref), (1, last_ref)):
        for zz in range(MP):
            to_c = lax.rem(number, 2)
            here = (s == section) & (to_c == c) & (z == zz)
            dst = landing.at[piece]
            moves.send(
                ref.at[zz], dst, "back", piece, active & jnp.logical_not(here), section=section, dp=y * 2 + to_c, mp=zz
            )

            @pl.when(active & here)
            def _():
                pltpu.make_async_copy(ref.at[zz], dst, moves.arrival("back", piece)).start()

    for g, k in steps:
        zz = place.other_z(k)
        moves.send(part(above[g], g, zz), from_x[g].at[zz], "from_x", g * MP + zz, s == 0, section=1 - s, dp=d, mp=z)

    def loaded(key):
        copy, when = loads[key]
        if when is None:
            copy.wait()
        else:
            pl.when(when)(copy.wait)

    def add_into(dst, *terms):
        total = dst[...].astype(WIDE)
        for term in terms:
            total = total + term[...].astype(WIDE)
        dst[...] = total.astype(LOW)

    def pair_step(g, k):
        zz = place.other_z(k)
        for r in list(range(1, Y)) + [0]:
            slot = place.other_y(r) * MP + zz
            moves.wait(paired[g].at[slot], "pair", g * Y * MP + slot)
            loaded(("own", g, k, r))
            if r:
                add_into(held[g].at[slot], paired[g].at[slot])
                out = (Y - r - 1) * MP + zz
                moves.send(
                    held[g].at[slot], from_y[g].at[out], "from_y", g * (Y - 1) * MP + out,
                    section=s, dp=place.other_y(r) * 2 + c, mp=z,
                )

    def rows_step(g, k):
        zz = place.other_z(k)
        slot = y * MP + zz
        slots = [(r - 1) * MP + zz for r in range(1, Y)]
        for at in slots:
            moves.wait(from_y[g].at[at], "from_y", g * (Y - 1) * MP + at)
        add_into(held[g].at[slot], paired[g].at[slot], *(from_y[g].at[at] for at in slots))
        moves.send(held[g].at[slot], from_x[g].at[zz], "from_x", g * MP + zz, s == 1, section=1 - s, dp=d, mp=z)

    def section_step(g, k):
        zz = place.other_z(k)
        moves.wait(from_x[g].at[zz], "from_x", g * MP + zz)
        loaded(("above", g, k))

        @pl.when(s == 0)
        def _():
            total = held[g][y * MP + zz].astype(WIDE) + from_x[g][zz].astype(WIDE)
            mine[g][zz] = total.astype(LOW)

        @pl.when(s == 1)
        def _():
            add_into(mine[g].at[zz], from_x[g].at[zz])

        if k:
            moves.send(mine[g].at[zz], from_z[g].at[z], "from_z", g * MP + z, section=s, dp=d, mp=zz)

    def columns_step(g):
        total = mine[g][z].astype(WIDE)
        for k in range(1, MP):
            zz = place.other_z(k)
            moves.wait(from_z[g].at[zz], "from_z", g * MP + zz)
            total = total + from_z[g][zz].astype(WIDE)
        outs[g][...] = total

    early, lag = 4, 2
    for at in range(-early, len(steps) + lag):
        if at + early < len(steps):
            pair_step(*steps[at + early])
        if 0 <= at < len(steps):
            rows_step(*steps[at])
        if at >= lag:
            section_step(*steps[at - lag])
        if at == 1:
            total = vec_here[s, y, z]
            for r in range(1, MP):
                moves.wait(vec_z.at[place.other_z(r)], "vec_z", place.other_z(r))
                total = total + vec_z[place.other_z(r)]
            sums_ref[...] = total

    rows = landing.shape[1]
    rest = ends_ref.shape[1] - rows
    for p in range(pieces):
        moves.wait(landing.at[p], "back", p)
        if p % 2 == 0:
            ends_ref[p // 2, 0:rows] = landing[p]
        else:
            ends_ref[p // 2, rows:] = landing[p][:rest]

    for g in ORDER:
        columns_step(g)
    moves.finish()


def scatter(table, first, last, grads, shapes, ends_shape):
    S, DP, MP = (lax.axis_size(name) for name in ("section", "dp", "mp"))
    Y = DP // 2
    _, rows, block = first.shape
    pieces = grads["pieces"]
    names = ("qkv", "out", "fc1", "fc2")
    flat = [grads["own"][n] for n in names] + [grads["there"][n] for n in names] + [grads["above"][n] for n in names]
    counts = scatter_counts(S, Y, MP, pieces)
    vmem = pl.BlockSpec(memory_space=pltpu.VMEM)

    def room(count):
        return [pltpu.VMEM((count,) + shape, LOW) for shape in shapes]

    sends = 2 + Y - 1 + MP - 1 + S * MP + 4 * (Y * MP + (Y - 1) * MP + 2 * MP + MP - 1)
    return pl.pallas_call(
        functools.partial(scatter_kernel, pieces),
        in_specs=[vmem] + [HBM] * (2 + len(flat)),
        out_specs=[vmem] * 6,
        out_shape=[jax.ShapeDtypeStruct(ends_shape, LOW), jax.ShapeDtypeStruct(table.shape[4:], WIDE)]
        + [jax.ShapeDtypeStruct(shape, WIDE) for shape in shapes],
        scratch_shapes=room(Y * MP)
        + room(Y * MP)
        + room(MP)
        + room(MP)
        + room((Y - 1) * MP)
        + room(MP)
        + [
            pltpu.SemaphoreType.DMA((sends,)),
            pltpu.SemaphoreType.DMA((sum(counts.values()),)),
            pltpu.SemaphoreType.DMA((4 * (Y + 1) * MP,)),
            pltpu.VMEM(table.shape[1:], WIDE),
            pltpu.VMEM(table.shape[1:], WIDE),
            pltpu.VMEM(table.shape[2:], WIDE),
            pltpu.VMEM((Y - 1,) + table.shape[3:], WIDE),
            pltpu.VMEM(table.shape[3:], WIDE),
            pltpu.VMEM((pieces, rows, block), LOW),
        ],
        compiler_params=pltpu.CompilerParams(has_side_effects=True, vmem_limit_bytes=63 << 20),
    )(table, first, last, *flat)


def nn(left, right):
    return lax.dot_general(left, right, (((1,), (0,)), ((), ())), preferred_element_type=WIDE)


def nt(left, right):
    return lax.dot_general(left, right, (((1,), (1,)), ((), ())), preferred_element_type=WIDE)


def tn(left, right):
    return lax.dot_general(left, right, (((0,), (0,)), ((), ())), preferred_element_type=WIDE)


def row_mean(value):
    return jnp.mean(value, 1, keepdims=True)


def column_sum(value):
    return jnp.sum(value.astype(WIDE), 0, keepdims=True)


def centre(rows_in):
    mean = row_mean(rows_in)
    inv_std = lax.rsqrt(row_mean(rows_in * rows_in) - mean * mean + epsilon)
    return (rows_in - mean) * inv_std, inv_std


def norm_back(grad, rows_in, gain):
    xhat, inv_std = centre(rows_in)
    weighted = grad * gain
    d_rows = inv_std * (weighted - row_mean(weighted) - xhat * row_mean(weighted * xhat))
    return d_rows, column_sum(grad * xhat), column_sum(grad)


def full(shape):
    return pl.BlockSpec(shape, lambda i: (0,) * len(shape))


def compute_call(kernel, steps, ins, outs, scratch, flops, args):
    return pl.pallas_call(
        kernel,
        grid=(steps,),
        in_specs=ins,
        out_specs=[spec for spec, _ in outs],
        out_shape=[shape for _, shape in outs],
        scratch_shapes=scratch,
        compiler_params=pltpu.CompilerParams(vmem_limit_bytes=58 << 20),
        cost_estimate=pl.CostEstimate(flops=1000, bytes_accessed=1000, transcendentals=0),
    )(*args)


LN1_GAIN, LN1_BIAS, B_QUERY, B_VALUE, B_OUT, SCALE_ATTN, LN2_GAIN, LN2_BIAS, B_FC2, SCALE_MLP = range(10)


def project_kernel(x_ref, vec_ref, w_ref, n_ref, kv_ref, q_ref, held):
    step = pl.program_id(0)

    @pl.when(step == 0)
    def _():
        xhat, _ = centre(x_ref[...])
        low = (xhat * vec_ref[LN1_GAIN][None] + vec_ref[LN1_BIAS][None]).astype(LOW)
        held[...] = low
        n_ref[...] = low

    value = nn(held[...], w_ref[...])

    @pl.when(step == 0)
    def _():
        kv_ref[0] = value.astype(LOW)

    @pl.when(step == 1)
    def _():
        kv_ref[1] = (value + vec_ref[B_VALUE][None]).astype(LOW)

    @pl.when(step == 2)
    def _():
        q_ref[...] = (value + vec_ref[B_QUERY][None]).astype(LOW)


def project(rows_in, vec, attn):
    rows, width = rows_in.shape
    low = jax.ShapeDtypeStruct((rows, width), LOW)
    return compute_call(
        project_kernel,
        3,
        [
            full(rows_in.shape),
            full(vec.shape),
            pl.BlockSpec((None, width, width), lambda i: (lax.rem(i + 1, 3), 0, 0)),
        ],
        [
            (full(rows_in.shape), low),
            (full((2, rows, width)), jax.ShapeDtypeStruct((2, rows, width), LOW)),
            (full(rows_in.shape), low),
        ],
        [pltpu.VMEM((rows, width), LOW)],
        6 * rows * width * width,
        (rows_in, vec, attn),
    )


def attend_kernel(q_ref, k0, k1, v0, v1, mask_ref, o_ref, wide_ref, p_ref):
    bias0, bias1 = mask_ref[:, 0:1], mask_ref[:, 1:2]
    outs = []
    for head in range(q_ref.shape[1] // HD):
        at = slice(head * HD, head * HD + HD)
        q = (q_ref[:, at].astype(WIDE) * (HD**-0.5)).astype(LOW)
        s0 = nt(k0[:, at], q) + bias0
        s1 = nt(k1[:, at], q) + bias1
        top = jnp.maximum(jnp.max(s0, 0, keepdims=True), jnp.max(s1, 0, keepdims=True))
        e0 = jnp.exp(s0 - top)
        e1 = jnp.exp(s1 - top)
        scale = 1.0 / (jnp.sum(e0, 0, keepdims=True) + jnp.sum(e1, 0, keepdims=True))
        p0 = (e0 * scale).astype(LOW)
        p1 = (e1 * scale).astype(LOW)
        p_ref[head, 0] = p0
        p_ref[head, 1] = p1
        outs.append(tn(v0[:, at], p0) + tn(v1[:, at], p1))
    out = jnp.concatenate(outs, 0).T
    wide_ref[...] = out
    o_ref[...] = out.astype(LOW)


def attend(q, kv0, kv1, mask):
    rows, width = q.shape
    steps, heads = width // 128, width // HD
    one = pl.BlockSpec((rows, 128), lambda i: (0, i))
    key = pl.BlockSpec((None, rows, 128), lambda i: (0, 0, i))
    value = pl.BlockSpec((None, rows, 128), lambda i: (1, 0, i))
    return compute_call(
        attend_kernel,
        steps,
        [one, key, key, value, value, full(mask.shape)],
        [
            (one, jax.ShapeDtypeStruct((rows, width), LOW)),
            (one, jax.ShapeDtypeStruct((rows, width), WIDE)),
            (
                pl.BlockSpec((2, 2, rows, rows), lambda i: (i, 0, 0, 0)),
                jax.ShapeDtypeStruct((heads, 2, rows, rows), LOW),
            ),
        ],
        [],
        32 * heads * rows * rows * HD,
        (q, kv0, kv1, kv0, kv1, mask),
    )


def mlp_kernel(x_ref, o_ref, vec_ref, bias_ref, wo_ref, w1_ref, w2_ref, y_ref, branch_ref, middle_ref, n_ref, act_ref, slope_ref, two_ref, total):
    step = pl.program_id(0)

    @pl.when(step == 0)
    def _():
        branch = nt(o_ref[...], wo_ref[...]) + vec_ref[B_OUT][None]
        branch_ref[...] = branch.astype(LOW)
        middle = x_ref[...] + vec_ref[SCALE_ATTN][None] * branch
        middle_ref[...] = middle
        xhat, _ = centre(middle)
        n_ref[...] = (xhat * vec_ref[LN2_GAIN][None] + vec_ref[LN2_BIAS][None]).astype(LOW)
        total[...] = jnp.zeros_like(total)

    hidden = nn(n_ref[...], w1_ref[...]) + bias_ref[0:1]
    cdf = 0.5 + 0.5 * lax.erf(hidden * inv_root_two)
    active = (hidden * cdf).astype(LOW)
    act_ref[...] = active
    slope_ref[...] = (cdf + hidden * jnp.exp(-0.5 * hidden * hidden) * inv_root_tau).astype(LOW)
    total[...] += nt(active, w2_ref[...])

    @pl.when(step == pl.num_programs(0) - 1)
    def _():
        two = total[...] + vec_ref[B_FC2][None]
        two_ref[...] = two.astype(LOW)
        y_ref[...] = middle_ref[...] + vec_ref[SCALE_MLP][None] * two


CHUNK = 512


def mlp(rows_in, out, vec, bias, weights):
    attn, fc1, fc2 = weights
    rows, width = rows_in.shape
    hidden = fc1.shape[1]
    low = (full(rows_in.shape), jax.ShapeDtypeStruct((rows, width), LOW))
    wide = (full(rows_in.shape), jax.ShapeDtypeStruct((rows, width), WIDE))
    units = (pl.BlockSpec((rows, CHUNK), lambda i: (0, i)), jax.ShapeDtypeStruct((rows, hidden), LOW))
    weight = pl.BlockSpec((width, CHUNK), lambda i: (0, i))
    return compute_call(
        mlp_kernel,
        hidden // CHUNK,
        [
            full(rows_in.shape),
            full(rows_in.shape),
            full(vec.shape),
            pl.BlockSpec((8, CHUNK), lambda i: (0, i)),
            pl.BlockSpec((None, width, width), lambda i: (3, 0, 0)),
            weight,
            weight,
        ],
        [wide, low, wide, low, units, units, low],
        [pltpu.VMEM((rows, width), WIDE)],
        4 * rows * width * hidden,
        (rows_in, out, vec, bias, attn, fc1, fc2),
    )


def store_halves(value, even_first, own_ref, there_ref, lead=()):
    count = own_ref.shape[len(lead)]
    size = own_ref.shape[len(lead) + 1]
    for d in range(2 * count):
        part = value[d * size : (d + 1) * size].astype(LOW)

        def put(ref, part=part, d=d):
            ref[lead + (d // 2,)] = part

        if d % 2 == 0:
            pl.when(even_first)(lambda: put(own_ref))
            pl.when(jnp.logical_not(even_first))(lambda: put(there_ref))
        else:
            pl.when(even_first)(lambda: put(there_ref))
            pl.when(jnp.logical_not(even_first))(lambda: put(own_ref))


def mlp_back_kernel(
    c_ref, dy_ref, vec_ref, two_ref, act_ref, slope_ref, n_ref, middle_ref, branch_ref, o_ref, wo_ref, w1_ref, w2_ref,
    grad_ref, do_ref, own1, there1, own2, there2, own_o, there_o, sums_ref, units_ref, dm, dm_t, n_t, total,
):
    step = pl.program_id(0)
    even = c_ref[0] == 0

    @pl.when(step == 0)
    def _():
        low = (dy_ref[...] * vec_ref[SCALE_MLP][None]).astype(LOW)
        dm[...] = low
        dm_t[...] = low.T
        n_t[...] = n_ref[...].T
        sums_ref[0:1] = column_sum(dy_ref[...] * two_ref[...].astype(WIDE))
        sums_ref[1:2] = column_sum(low)
        total[...] = jnp.zeros_like(total)

    df = (nn(dm[...], w2_ref[...]) * slope_ref[...].astype(WIDE)).astype(LOW)
    units_ref[...] = jnp.broadcast_to(column_sum(df), units_ref.shape)
    store_halves(nn(dm_t[...], act_ref[...]), even, own2, there2)
    store_halves(nn(n_t[...], df), even, own1, there1)
    total[...] += nt(df, w1_ref[...])

    @pl.when(step == pl.num_programs(0) - 1)
    def _():
        d_rows, d_gain, d_bias = norm_back(total[...], middle_ref[...], vec_ref[LN2_GAIN][None])
        sums_ref[2:3] = d_gain
        sums_ref[3:4] = d_bias
        grad = dy_ref[...] + d_rows
        grad_ref[...] = grad
        sums_ref[4:5] = column_sum(grad * branch_ref[...].astype(WIDE))
        da = (grad * vec_ref[SCALE_ATTN][None]).astype(LOW)
        sums_ref[5:6] = column_sum(da)
        sums_ref[6:8] = jnp.zeros((2, sums_ref.shape[1]), WIDE)
        do_ref[...] = nn(da, wo_ref[...]).astype(LOW)
        store_halves(tn(da, o_ref[...]), even, own_o, there_o)


def mlp_back(half, dy, vec, saved, weights, count):
    attn, fc1, fc2 = weights
    rows, width = dy.shape
    hidden = fc1.shape[1]
    block = width // (2 * count)
    whole = full(dy.shape)
    low = (whole, jax.ShapeDtypeStruct((rows, width), LOW))
    wide = (whole, jax.ShapeDtypeStruct((rows, width), WIDE))
    units = pl.BlockSpec((rows, CHUNK), lambda i: (0, i))
    weight = pl.BlockSpec((width, CHUNK), lambda i: (0, i))
    grad = (
        pl.BlockSpec((count, block, CHUNK), lambda i: (0, 0, i)),
        jax.ShapeDtypeStruct((count, block, hidden), LOW),
    )
    grad_o = (full((count, block, width)), jax.ShapeDtypeStruct((count, block, width), LOW))
    return compute_call(
        mlp_back_kernel,
        hidden // CHUNK,
        [
            pl.BlockSpec(memory_space=pltpu.SMEM),
            whole,
            full(vec.shape),
            whole,
            units,
            units,
            whole,
            whole,
            whole,
            whole,
            pl.BlockSpec((None, width, width), lambda i: (3, 0, 0)),
            weight,
            weight,
        ],
        [
            wide,
            low,
            grad,
            grad,
            grad,
            grad,
            grad_o,
            grad_o,
            (full((8, width)), jax.ShapeDtypeStruct((8, width), WIDE)),
            (pl.BlockSpec((8, CHUNK), lambda i: (0, i)), jax.ShapeDtypeStruct((8, hidden), WIDE)),
        ],
        [
            pltpu.VMEM((rows, width), LOW),
            pltpu.VMEM((width, rows), LOW),
            pltpu.VMEM((width, rows), LOW),
            pltpu.VMEM((rows, width), WIDE),
        ],
        8 * rows * width * hidden,
        (
            half,
            dy,
            vec,
            saved["two"],
            saved["active"],
            saved["slope"],
            saved["n_two"],
            saved["middle"],
            saved["branch"],
            saved["out"],
            attn,
            fc1,
            fc2,
        ),
    )


def attend_back_kernel(q_ref, k0, k1, v0, v1, p_ref, g_ref, o_ref, d0_ref, d1_ref):
    outs = []
    for head in range(q_ref.shape[1] // HD):
        at = slice(head * HD, head * HD + HD)
        q = q_ref[:, at]
        g = g_ref[:, at]
        prod = g.astype(WIDE) * o_ref[:, at]
        dot = jnp.sum(prod.T, 0, keepdims=True)
        dq = None
        for half, (k, v, out, first) in enumerate(((k0, v0, d0_ref, 1), (k1, v1, d1_ref, 0))):
            p = p_ref[head, half]
            out[first + 1, :, at] = nn(p, g).astype(LOW)
            ds = (p.astype(WIDE) * (nt(v[:, at], g) - dot)).astype(LOW)
            part = tn(k[:, at], ds)
            dq = part if dq is None else dq + part
            out[first, :, at] = (nn(ds, q) * (HD**-0.5)).astype(LOW)
        outs.append(dq * (HD**-0.5))
    d0_ref[0] = jnp.concatenate(outs, 0).T.astype(LOW)


def attend_back(q, kv0, kv1, probs, grad, out):
    rows, width = q.shape
    steps, heads = width // 128, width // HD
    one = pl.BlockSpec((rows, 128), lambda i: (0, i))
    key = pl.BlockSpec((None, rows, 128), lambda i: (0, 0, i))
    value = pl.BlockSpec((None, rows, 128), lambda i: (1, 0, i))

    def several(count):
        return (
            pl.BlockSpec((count, rows, 128), lambda i: (0, 0, i)),
            jax.ShapeDtypeStruct((count, rows, width), LOW),
        )

    return compute_call(
        attend_back_kernel,
        steps,
        [one, key, key, value, value, pl.BlockSpec((2, 2, rows, rows), lambda i: (i, 0, 0, 0)), one, one],
        [several(3), several(2)],
        [],
        40 * heads * rows * rows * HD,
        (q, kv0, kv1, kv0, kv1, probs, grad, out),
    )


def project_back_kernel(
    c_ref, d0_ref, d1_ref, n_ref, x_ref, grad_ref, vec_ref, w_ref, dx_ref, own, there, sums_ref, n_t, total
):
    step = pl.program_id(0)
    even = c_ref[0] == 0

    @pl.when(step == 0)
    def _():
        total[...] = jnp.zeros_like(total)
        n_t[...] = n_ref[...].T

    theirs = jnp.where(step == 0, 0.0, d1_ref[...].astype(WIDE))
    grad = (d0_ref[...].astype(WIDE) + theirs).astype(LOW)
    store_halves(nn(n_t[...], grad), even, own, there)
    total[...] += nt(grad, w_ref[...])
    sums = column_sum(grad)

    @pl.when(step == 0)
    def _():
        sums_ref[0:1] = sums

    @pl.when(step == 2)
    def _():
        sums_ref[1:2] = sums
        d_rows, d_gain, d_bias = norm_back(total[...], x_ref[...], vec_ref[LN1_GAIN][None])
        sums_ref[2:3] = d_gain
        sums_ref[3:4] = d_bias
        sums_ref[4:8] = jnp.zeros((4, sums_ref.shape[1]), WIDE)
        dx_ref[...] = grad_ref[...] + d_rows


def project_back(half, d0, d1, saved, grad, vec, attn, count):
    rows, width = grad.shape
    block = width // (2 * count)
    whole = full(grad.shape)
    out = (
        pl.BlockSpec((None, count, block, width), lambda i: (i, 0, 0, 0)),
        jax.ShapeDtypeStruct((3, count, block, width), LOW),
    )
    return compute_call(
        project_back_kernel,
        3,
        [
            pl.BlockSpec(memory_space=pltpu.SMEM),
            pl.BlockSpec((None, rows, width), lambda i: (i, 0, 0)),
            pl.BlockSpec((None, rows, width), lambda i: (jnp.maximum(i - 1, 0), 0, 0)),
            whole,
            whole,
            whole,
            full(vec.shape),
            pl.BlockSpec((None, width, width), lambda i: (i, 0, 0)),
        ],
        [
            (whole, jax.ShapeDtypeStruct((rows, width), WIDE)),
            out,
            out,
            (full((8, width)), jax.ShapeDtypeStruct((8, width), WIDE)),
        ],
        [pltpu.VMEM((width, rows), LOW), pltpu.VMEM((rows, width), WIDE)],
        12 * rows * width * width,
        (half, d0, d1, saved["n_one"], saved["rows_in"], grad, vec, attn),
    )


def pick(stack, index, axis=0):
    return lax.dynamic_index_in_dim(stack, index, axis, keepdims=False)


def after(value, *others):
    return lax.optimization_barrier((value,) + others)[0]


def layer_forward(rows_in, vec, bias, weights, mask, from_pair, meanwhile):
    n_one, kv0, q = project(rows_in, vec, weights[0])
    kv1 = from_pair(kv0)
    out, out_wide, probs = attend(q, kv0, kv1, mask)
    out = meanwhile(0, q, out)
    leaving, branch, middle, n_two, active, slope, two = mlp(rows_in, out, vec, bias, weights)
    leaving = meanwhile(1, out, leaving)
    saved = dict(
        rows_in=rows_in,
        n_one=n_one,
        q=q,
        kv0=kv0,
        kv1=kv1,
        out=out,
        out_wide=out_wide,
        probs=probs,
        branch=branch,
        middle=middle,
        n_two=n_two,
        active=active,
        slope=slope,
        two=two,
    )
    return (leaving, saved)


def layer_backward(grad_rows, saved, vec, weights, half, from_pair, sums_over, meanwhile):
    count = lax.axis_size("dp") // 2
    grad_middle, d_out, own1, there1, own2, there2, own_o, there_o, sums, units = mlp_back(
        half, grad_rows, vec, saved, weights, count
    )
    d_out = meanwhile("fc2", grad_rows, d_out)
    d0, d1 = attend_back(saved["q"], saved["kv0"], saved["kv1"], saved["probs"], d_out, saved["out_wide"])
    own, there = dict(out=own_o, fc1=own1, fc2=own2), dict(out=there_o, fc1=there1, fc2=there2)
    d0 = meanwhile("fc1", d_out, d0)
    d1 = from_pair(d1)
    d0 = sums_over(own, there, d0)
    grad_in, own["qkv"], there["qkv"], sums_one = project_back(
        half, d0, d1, saved, grad_middle, vec, weights[0], count
    )
    grad_in = sums_over(dict(qkv=own["qkv"]), dict(qkv=there["qkv"]), grad_in)
    grad_in = meanwhile("out", d0, grad_in)
    grad_in = meanwhile("qkv", d0, grad_in)
    vectors = dict(
        ln1_gain=sums_one[2],
        ln1_bias=sums_one[3],
        b_query=sums_one[0],
        b_value=sums_one[1],
        b_out=sums[5],
        scale_attn=sums[4],
        ln2_gain=sums[2],
        ln2_bias=sums[3],
        b_fc1=units[0],
        b_fc2=sums[1],
        scale_mlp=sums[0],
    )
    return (grad_in, own, there, vectors)


NARROW = ("ln1_gain", "ln1_bias", "b_query", "b_value", "b_out", "scale_attn", "ln2_gain", "ln2_bias", "b_fc2", "scale_mlp")


def local(
    boundary,
    ln1_gain,
    ln1_bias,
    w_query,
    w_key,
    w_value,
    b_query,
    b_value,
    w_out,
    b_out,
    scale_attn,
    ln2_gain,
    ln2_bias,
    w_fc1,
    b_fc1,
    w_fc2,
    b_fc2,
    scale_mlp,
):
    place = Place()
    _, micros, images, seq_len, columns = boundary.shape
    S, DP, MP = place.S, place.DP, place.MP
    width = columns * MP
    rows = -(-seq_len // 32) * 16
    pieces = 2 * micros
    number = place.s * MP + place.z
    active = number < pieces

    def from_pair(value):
        return lax.ppermute(value, "dp", [(i, i + 1 - 2 * (i % 2)) for i in range(DP)])

    def from_row(value, r):
        return lax.ppermute(value, "dp", [(i, (i - 2 * r) % DP) for i in range(DP)])

    turns = max(pieces, MP)
    spots = [(i, j, k) for i in range(S) for j in range(DP) for k in range(MP)]

    def move(value, target):
        number_of = {spot: i for i, spot in enumerate(spots)}
        pairs = [(number_of[spot], number_of[target(*spot)]) for spot in spots if target(*spot) is not None]
        return lax.ppermute(value, ("section", "dp", "mp"), pairs)

    def bring(blocks, which, began):
        got = []
        for turn in which:

            def target(i, j, k, turn=turn):
                piece = (turn + k) % turns
                image = 2 * (piece // 2) + j % 2
                if i != 1 or piece >= pieces:
                    return None
                return (image // MP, j // 2 * 2 + piece % 2, image % MP)

            piece = jnp.minimum(lax.rem(place.z + turn, turns), pieces - 1)
            got.append(move(after(pick(blocks, piece), began), target))
        return got

    def brought(got):
        here = 2 * lax.div(number, 2) + place.c
        stack = jnp.stack(got)
        return jnp.concatenate([pick(stack, lax.rem(here + turns - zz % turns, turns)) for zz in range(MP)], 1)

    def by_column(value):
        return jnp.stack([value[:, i * columns : (i + 1) * columns].astype(LOW) for i in range(MP)])

    waiting, above = {}, {}

    def sums_over(own, there, before):
        parts = []
        for name in own:
            axis = own[name].ndim - 3
            got = from_pair(there[name])

            def row(r, value=own[name], got=got, axis=axis):
                at = lax.rem(place.y + r, DP // 2)
                return pick(value, at, axis).astype(WIDE) + pick(got, at, axis).astype(WIDE)

            others = [row(r).astype(LOW) for r in range(1, DP // 2)]
            parts += others
            waiting[name] = (row, others)
        return after(before, *parts)

    def rows_meanwhile(name, before, done):
        row, others = waiting[name]
        got = [from_row(after(part, before), DP // 2 - r) for r, part in enumerate(others, 1)]
        got, done = lax.optimization_barrier((got, done))
        above[name] = (row, got)
        return done

    def sums_done(name):
        row, got = above[name]
        total = row(0)
        for other in got:
            total = total + other.astype(WIDE)
        return total.astype(LOW)

    def first_unit(at, weight):
        return weight.shape[-1] // 2 if at == 1 else 0

    def own_block(at, weight):
        axis, block = weight.ndim - 2, weight.shape[-2] // DP
        weight = weight[..., first_unit(at, weight) :]
        return lax.dynamic_slice_in_dim(weight, place.d * block, block, axis)

    def fill_rows(layer, at, weight, began, done):
        axis, block = weight.ndim - 2, weight.shape[-2] // DP
        value = after(sliced[layer][at], began)
        for r in range(1, DP // 2):
            got, done = lax.optimization_barrier((from_row(value, r), done))
            row = lax.rem(place.y + r, DP // 2) * 2
            for rows_of, part in ((row + place.c, got), (row + 1 - place.c, from_pair(got))):
                start = [jnp.int32(0)] * weight.ndim
                start[axis], start[-1] = rows_of * block, jnp.int32(first_unit(at, weight))
                weight = lax.dynamic_update_slice(weight, part, start)
        return weight, done

    images_low = boundary.reshape(micros, seq_len, columns).astype(LOW)
    sent = jnp.pad(images_low, ((0, 0), (0, 2 * rows - seq_len), (0, 0))).reshape(pieces, rows, columns)
    keys = jnp.arange(rows)[:, None] + rows * jnp.stack([place.c, 1 - place.c])[None]
    mask = jnp.where(keys < seq_len, 0.0, -1e30).astype(WIDE)
    mask = jnp.pad(mask, ((0, 0), (0, 126)))
    half = place.c.reshape(1)
    narrow = (ln1_gain, ln1_bias, b_query, b_value, b_out, scale_attn, ln2_gain, ln2_bias, b_fc2, scale_mlp)
    packed = jnp.concatenate([v[0] for v in narrow] + [b_fc1[0]])
    lines = -(-packed.shape[0] // 1024) * 8
    packed = jnp.pad(packed, (0, lines * 128 - packed.shape[0])).reshape(lines, 128)
    attn_shard = jnp.stack([w_query[0], w_key[0], w_value[0], w_out[0].T])
    arrived, vecs, weights = gather(sent, packed, attn_shard, w_fc1[0], w_fc2[0].T)
    sliced = {layer: [own_block(at, w) for at, w in enumerate(weights[layer])] for layer in range(1, S)}
    arrived = after(arrived, *(w for layer in sliced for w in sliced[layer]))
    arrived = jnp.where(active, arrived.astype(WIDE), 0.0)
    vecs = vecs.reshape(S, MP, -1)
    vectors, biases = [], []
    for layer in range(S):
        start = len(NARROW) * columns
        table = vecs[layer, :, :start].reshape(MP, len(NARROW), columns)
        table = jnp.moveaxis(table, 0, 1).reshape(len(NARROW), width)
        vectors.append(jnp.pad(table, ((0, 16 - len(NARROW)), (0, 0))))
        bias = vecs[layer, :, start : start + b_fc1.shape[1]].reshape(1, -1)
        biases.append(jnp.pad(bias, ((0, 7), (0, 0))))

    saved, cotangent = [], []
    split = [range(turns)[i * turns // 3 : (i + 1) * turns // 3] for i in range(3)]
    rows_now = arrived
    for layer in range(S):
        def meanwhile(stage, before, done, layer=layer):
            at = 2 * layer + stage
            if at > 2:
                return done
            few, done = lax.optimization_barrier((bring(sent, split[at], before), done))
            cotangent.extend(few)
            weights[1][at], done = fill_rows(1, at, weights[1][at], before, done)
            return done

        rows_now, kept = layer_forward(
            rows_now, vectors[layer], biases[layer], weights[layer], mask, from_pair, meanwhile
        )
        saved.append(kept)
        if layer + 1 < S:
            rows_now = rows_now.astype(LOW).astype(WIDE)
    end_rows = rows_now

    grad_now = jnp.where(active, brought(cotangent).astype(WIDE), 0.0)
    vector_grads = [None] * S

    for layer in reversed(range(S)):
        grad_now, own, there, vector_grads[layer] = layer_backward(
            grad_now, saved[layer], vectors[layer], weights[layer], half, from_pair,
            sums_over if layer else (lambda own, there, before: before),
            (lambda name, before, done: done) if layer else rows_meanwhile,
        )
        if layer:
            grad_now = grad_now.astype(LOW).astype(WIDE)

    above = {name: sums_done(name) for name in ("fc2", "fc1", "out", "qkv")}
    grads = dict(own=own, there=there, above=above, pieces=pieces)
    shapes = [(3,) + w_query.shape[1:], w_query.shape[1:], w_fc1.shape[1:], (w_fc2.shape[2], w_fc2.shape[1])]
    names = NARROW + ("b_fc1",)
    table = jnp.stack(
        [
            jnp.concatenate([vector_grads[layer][name].reshape(MP, DP, -1) for name in names], 2)
            for layer in range(S)
        ]
    )
    lines = -(-table.shape[3] // 1024) * 8
    table = jnp.pad(table, ((0, 0), (0, 0), (0, 0), (0, lines * 128 - table.shape[3])))
    table = table.reshape(S, MP, DP // 2, 2, lines, 128).transpose(3, 0, 2, 1, 4, 5)
    ends, summed, g_qkv, g_out, g_fc1, g_fc2 = scatter(
        table, by_column(grad_now), by_column(end_rows), grads, shapes, (micros, seq_len, columns)
    )
    ends_out = ends.astype(WIDE).reshape(boundary.shape)
    summed = summed.reshape(-1)
    v, start = {}, 0
    for name in names:
        size = (b_fc1.shape[1] if name == "b_fc1" else columns) // DP
        v[name] = summed[start : start + size][None]
        start += size

    return (
        ends_out,
        v["ln1_gain"],
        v["ln1_bias"],
        g_qkv[0][None],
        g_qkv[1][None],
        g_qkv[2][None],
        v["b_query"],
        v["b_value"],
        g_out.T[None],
        v["b_out"],
        v["scale_attn"],
        v["ln2_gain"],
        v["ln2_bias"],
        g_fc1[None],
        v["b_fc1"],
        g_fc2.T[None],
        v["b_fc2"],
        v["scale_mlp"],
    )


def solution(mesh):
    return jax.shard_map(
        local,
        mesh=mesh,
        in_specs=(
            P("section", None, "dp", None, "mp"),
            P("section", "mp"),
            P("section", "mp"),
            P("section", "dp", "mp"),
            P("section", "dp", "mp"),
            P("section", "dp", "mp"),
            P("section", "mp"),
            P("section", "mp"),
            P("section", "mp", "dp"),
            P("section", "mp"),
            P("section", "mp"),
            P("section", "mp"),
            P("section", "mp"),
            P("section", "dp", "mp"),
            P("section", "mp"),
            P("section", "mp", "dp"),
            P("section", "mp"),
            P("section", "mp"),
        ),
        out_specs=(
            P("section", None, "dp", None, "mp"),
            P("section", ("mp", "dp")),
            P("section", ("mp", "dp")),
            P("section", "dp", "mp"),
            P("section", "dp", "mp"),
            P("section", "dp", "mp"),
            P("section", ("mp", "dp")),
            P("section", ("mp", "dp")),
            P("section", "mp", "dp"),
            P("section", ("mp", "dp")),
            P("section", ("mp", "dp")),
            P("section", ("mp", "dp")),
            P("section", ("mp", "dp")),
            P("section", "dp", "mp"),
            P("section", ("mp", "dp")),
            P("section", "mp", "dp"),
            P("section", ("mp", "dp")),
            P("section", ("mp", "dp")),
        ),
        check_vma=False,
    )
```

```python
import functools

import jax
import jax.numpy as jnp
from jax import lax
from jax.experimental import pallas as pl
from jax.experimental.pallas import tpu as pltpu
from jax.sharding import PartitionSpec as P


HD = 64
LOW = jnp.bfloat16
WIDE = jnp.float32
HBM = pl.BlockSpec(memory_space=pltpu.HBM)

epsilon = 1e-06
inv_root_two = 0.7071067811865476
inv_root_tau = 0.3989422804014327


class Place:
    def __init__(self):
        self.S = lax.axis_size("section")
        self.DP = lax.axis_size("dp")
        self.MP = lax.axis_size("mp")
        self.Y = self.DP // 2
        self.H = self.MP // 2
        self.s = lax.axis_index("section")
        self.d = lax.axis_index("dp")
        self.z = lax.axis_index("mp")
        self.y = lax.div(self.d, 2)
        self.c = lax.rem(self.d, 2)
        self.nearest = sorted(range(self.MP), key=lambda r: min(r, self.MP - r))

    def other_y(self, r):
        return lax.rem(self.y + r, self.Y)

    def other_z(self, r):
        return lax.rem(self.z + r, self.MP)


class Moves:
    def __init__(self, send_sems, recv_sems, counts):
        self.send_sems, self.recv_sems = send_sems, recv_sems
        self.base, total = {}, 0
        for name, count in counts.items():
            self.base[name] = total
            total += count
        self.total = total
        self.sent = []

    def arrival(self, name, index):
        return self.recv_sems.at[self.base[name] + index]

    def send(self, src, dst, name, index, when=None, **to):
        at = len(self.sent)
        assert at < self.send_sems.shape[0]
        copy = pltpu.make_async_remote_copy(
            src_ref=src,
            dst_ref=dst,
            send_sem=self.send_sems.at[at],
            recv_sem=self.arrival(name, index),
            device_id=to,
        )
        self.sent.append((copy, when))
        if when is None:
            copy.start()
        else:
            pl.when(when)(copy.start)

    def send_one_of(self, options, name, when, **to):
        at = len(self.sent)
        assert at < self.send_sems.shape[0]
        for cond, src, dst, index in options:
            copy = pltpu.make_async_remote_copy(
                src_ref=src,
                dst_ref=dst,
                send_sem=self.send_sems.at[at],
                recv_sem=self.arrival(name, index),
                device_id=to,
            )
            pl.when(cond)(copy.start)
        self.sent.append((copy, when))

    def wait(self, ref, name, index):
        pltpu.make_async_copy(ref, ref, self.arrival(name, index)).wait()

    def finish(self):
        for copy, when in self.sent:
            if when is None:
                copy.wait_send()
            else:
                pl.when(when)(copy.wait_send)


def tile(start, size):
    return pl.ds(pl.multiple_of(start * size, size), size)


def holder(place, c, piece):
    image = 2 * (piece // 2) + c
    return lax.div(image, place.MP), piece % 2, lax.rem(image, place.MP)


def gather_counts(S, Y, MP, groups=4):
    return dict(rows=MP, vectors=S * MP, biases=S * MP, piece=groups * S * Y * MP, pair=groups * S * Y * MP)


def gather_kernel(pieces, tokens_ref, vec_ref, bias_ref, *refs):
    place = Place()
    s, y, c, z, d = place.s, place.y, place.c, place.z, place.d
    S, Y, MP, H = place.S, place.Y, place.MP, place.H
    shards, refs = refs[:4], refs[4:]
    rows_ref, sent_ref, vecs_ref, biases_ref = refs[:4]
    wholes = [refs[4 + g * S : 4 + (g + 1) * S] for g in range(4)]
    later, refs = refs[4 + 4 * S : 8 + 4 * S], refs[8 + 4 * S :]
    send_sems, recv_sems, own_sems, wide, load_sems = refs
    moves = Moves(send_sems, recv_sems, gather_counts(S, Y, MP))
    columns = sent_ref.shape[2]
    groups = range(4)

    def spot(g, l, yy, cc, zz):
        dd = yy * 2 + cc
        shard, whole = shards[g], wholes[g][l]
        at = (tile(dd, shard.shape[-2]), tile(zz, shard.shape[-1]))
        return whole.at[(slice(None),) + at] if len(shard.shape) == 3 else whole.at[at]

    def mark(g, l, yy, zz):
        return ((g * S + l) * Y + yy) * MP + zz

    def each(mine):
        return [(layer, (s == layer) if mine else (s != layer)) for layer in range(S)]

    def hand(g, mine, yy, zz, name, when, src, **to):
        moves.send_one_of(
            [
                (
                    cond if when is None else cond & when,
                    spot(g, layer, yy, c, zz) if src is None else src,
                    spot(g, layer, yy, c, zz),
                    mark(g, layer, yy, zz),
                )
                for layer, cond in each(mine)
            ],
            name,
            when,
            **to,
        )

    def to_pair(g, mine, zz, src=None, when=None):
        hand(g, mine, y, zz, "pair", when, src, section=s, dp=y * 2 + 1 - c, mp=z)

    def to_section(g, zz, when=None, src=None):
        hand(g, True, y, zz, "piece", when, src, section=1 - s, dp=d, mp=z)

    def along(g, zz, step, when, src=None):
        hand(g, True, y, zz, "piece", when, src, section=s, dp=d, mp=jnp.clip(z + step, 0, MP - 1))

    def rows_if(g, mine, zz, first_layer, there, src=None):
        when = first_layer | (zz < H) if g == 2 else first_layer
        for r in range(1, Y):
            hand(g, mine, y, zz, "piece", when & there, src, section=s, dp=place.other_y(r) * 2 + c, mp=z)

    def landed(g, l, yy, zz):
        moves.wait(spot(g, 0, yy, c, zz), "piece", mark(g, l, yy, zz))

    own_copies = []

    def columns_out(g):
        along(g, z, 1, z + 1 < MP, shards[g])
        along(g, z, -1, z >= 1, shards[g])
        to_section(g, z, src=shards[g])
        rows_if(g, True, z, s == 0, z >= 0, shards[g])
        to_pair(g, True, z, shards[g])
        for layer, cond in each(True):
            copy = pltpu.make_async_copy(shards[g], spot(g, layer, y, c, z), own_sems.at[g])
            pl.when(cond)(copy.start)
        own_copies.append(copy)

    def columns_in(g, far):
        for step, there in ((1, z >= far), (-1, z + far < MP)):
            zz = jnp.clip(z - step * far, 0, MP - 1)

            @pl.when(there)
            def _():
                landed(g, s, y, zz)

            along(g, zz, step, there & ((z + 1 < MP) if step == 1 else (z >= 1)))
            to_section(g, zz, there)
            rows_if(g, True, zz, s == 0, there)
            to_pair(g, True, zz, when=there)

    def section_in(g, far):
        for step, there in ((1, z >= far), (-1, z + far < MP))[: 2 if far else 1]:
            zz = jnp.clip(z - step * far, 0, MP - 1)

            @pl.when(there)
            def _():
                landed(g, 1 - s, y, zz)

            rows_if(g, False, zz, s == 1, there)
            to_pair(g, False, zz, when=there)

    def rows_in(g):
        for r in range(1, Y):
            yy = place.other_y(r)
            for layer, zz in [(0, zz) for zz in range(MP)] + ([(1, zz) for zz in range(H)] if g == 2 else []):
                landed(g, layer, yy, zz)
                there = spot(g, layer, yy, c, zz)
                moves.send(there, there, "pair", mark(g, layer, yy, zz), section=s, dp=y * 2 + 1 - c, mp=z)

    rows = rows_ref.shape[0]
    spare = 2 * rows - tokens_ref.shape[1]
    loads = []
    for piece in range(pieces):
        start = (rows - spare) * (piece % 2)
        copy = pltpu.make_async_copy(
            tokens_ref.at[piece // 2, pl.ds(start, rows), 0], wide.at[piece], load_sems.at[piece]
        )
        copy.start()
        loads.append(copy)

    own_vectors = []
    for i, (ref, whole, name) in enumerate(((vec_ref, vecs_ref, "vectors"), (bias_ref, biases_ref, "biases"))):
        there = whole.at[s, :, tile(z, ref.shape[1])]
        for q in range(1, S * MP):
            at = lax.rem(s * MP + z + q, S * MP)
            moves.send(ref, there, name, s * MP + z, section=lax.div(at, MP), dp=d, mp=lax.rem(at, MP))
        own_vectors.append(pltpu.make_async_copy(ref, there, own_sems.at[4 + i]))
        own_vectors[-1].start()

    for g in groups:
        columns_out(g)
    for piece in range(pieces):
        loads[piece].wait()
        low = wide[piece]
        if piece % 2 and spare:
            low = jnp.where(lax.broadcasted_iota(jnp.int32, (rows, 1), 0) < spare, 0.0, low)
        sent_ref[piece] = low.astype(LOW)
    for piece in range(pieces):
        to_s, to_c, to_z = holder(place, c, piece)
        here = (to_s == s) & (to_c == c) & (to_z == z)
        there = rows_ref.at[:, tile(z, columns)]
        moves.send(
            sent_ref.at[piece], there, "rows", z, (s == 0) & jnp.logical_not(here),
            section=to_s, dp=y * 2 + to_c, mp=to_z,
        )

        @pl.when((s == 0) & here)
        def _():
            pltpu.make_async_copy(sent_ref.at[piece], there, moves.arrival("rows", z)).start()

    for far in range(1, MP):
        for g in groups:
            columns_in(g, far)
            section_in(g, far - 1)
    for g in groups:
        section_in(g, MP - 1)
    for copy in own_copies:
        copy.wait()
    later_copies = []
    for g in groups:
        shard, there = shards[g], later[g]
        at = (tile(d, shard.shape[-2]),)
        if g < 2:
            at = at + (slice(None),)
        else:
            at = at + (tile(1 if g == 2 else s, there.shape[-1]),)
        src = wholes[g][1].at[(slice(None),) + at] if len(shard.shape) == 3 else wholes[g][1].at[at]
        copy = pltpu.make_async_copy(src, there, own_sems.at[6 + g])
        copy.start()
        later_copies.append(copy)
    for g in groups:
        rows_in(g)

    @pl.when(s * MP + z < pieces)
    def _():
        for zz in range(MP):
            moves.wait(rows_ref.at[:, tile(zz, columns)], "rows", zz)

    for q in range(1, S * MP):
        at = lax.rem(s * MP + z + q, S * MP)
        for ref, whole, name in ((vec_ref, vecs_ref, "vectors"), (bias_ref, biases_ref, "biases")):
            moves.wait(whole.at[lax.div(at, MP), :, tile(lax.rem(at, MP), ref.shape[1])], name, at)
    for g in groups:
        for zz in range(MP):
            for r in range(Y):
                yy = place.other_y(r)
                moves.wait(spot(g, 0, yy, 1 - c, zz), "pair", mark(g, 0, yy, zz))
                if g == 2 and zz < H and r:
                    moves.wait(spot(g, 1, yy, 1 - c, zz), "pair", mark(g, 1, yy, zz))
            for layer in range(1, S):
                moves.wait(spot(g, 0, y, 1 - c, zz), "pair", mark(g, layer, y, zz))
    for copy in own_vectors + later_copies:
        copy.wait()
    moves.finish()


def gather(tokens, vec, bias, *shards):
    S, DP, MP = (lax.axis_size(name) for name in ("section", "dp", "mp"))
    Y = DP // 2
    micros, seq_len, _, columns = tokens.shape
    pieces, rows = 2 * micros, half_rows(seq_len)
    counts = gather_counts(S, Y, MP)
    sends = pieces + 2 * (S * MP - 1) + 4 * (2 * MP + (2 * MP - 1) * (1 + 2 * Y) + (Y - 1) * MP) + (Y - 1) * (MP // 2)
    whole = [
        jax.ShapeDtypeStruct(shard.shape[:-2] + (shard.shape[-2] * DP, shard.shape[-1] * MP), LOW) for shard in shards
    ]
    later = [
        jax.ShapeDtypeStruct(shard.shape[:-1] + (shard.shape[-1] * MP // (1 if g < 2 else 2),), LOW)
        for g, shard in enumerate(shards)
    ]
    vmem = pl.BlockSpec(memory_space=pltpu.VMEM)
    got = pl.pallas_call(
        functools.partial(gather_kernel, pieces),
        in_specs=[vmem] * 7,
        out_specs=[HBM, vmem] + [HBM] * (2 + 4 * S) + [vmem] * 4,
        out_shape=[
            jax.ShapeDtypeStruct((rows, columns * MP), LOW),
            jax.ShapeDtypeStruct((pieces, rows, columns), LOW),
            jax.ShapeDtypeStruct((S, vec.shape[0], vec.shape[1] * MP), WIDE),
            jax.ShapeDtypeStruct((S, bias.shape[0], bias.shape[1] * MP), WIDE),
        ]
        + [shape for shape in whole for _ in range(S)]
        + later,
        scratch_shapes=[
            pltpu.SemaphoreType.DMA((sends,)),
            pltpu.SemaphoreType.DMA((sum(counts.values()),)),
            pltpu.SemaphoreType.DMA((10,)),
            pltpu.VMEM((pieces, rows, columns), WIDE),
            pltpu.SemaphoreType.DMA((pieces,)),
        ],
        compiler_params=pltpu.CompilerParams(has_side_effects=True, vmem_limit_bytes=63 << 20),
    )(tokens, vec, bias, *shards)
    return got[:4], [[got[4 + g * S + layer] for g in range(4)] for layer in range(S)], got[4 + 4 * S :]


def half_rows(seq_len):
    return -(-seq_len // 32) * 16


def scatter_counts(S, Y, MP, pieces, groups=4):
    return dict(
        back=max(pieces, MP),
        pair=groups * Y * MP,
        from_x=groups * MP,
        from_y=groups * (Y - 1) * MP,
        from_z=groups * MP,
        vec_pair=1,
        vec_x=1,
        vec_y=Y - 1,
        vec_z=MP,
    )


ORDER = (3, 2, 0, 1)


def scatter_kernel(pieces, table_ref, first_ref, last_ref, *refs):
    place = Place()
    s, y, c, z, d = place.s, place.y, place.c, place.z, place.d
    S, Y, MP = place.S, place.Y, place.MP
    own, there, above = refs[0:4], refs[4:8], refs[8:12]
    ends_ref, sums_ref, outs = refs[12], refs[13], refs[14:18]
    held, paired, mine, from_x, from_y, from_z = (refs[18 + 4 * i : 22 + 4 * i] for i in range(6))
    send_sems, recv_sems, load_sems, vec_here, vec_pair, vec_x, vec_y, vec_z = refs[42:]
    moves = Moves(send_sems, recv_sems, scatter_counts(S, Y, MP, pieces))

    def part(ref, g, zz, yy=None):
        at = (slice(None), tile(zz, outs[g].shape[-1]))
        if yy is not None:
            at = (yy,) + at
        if len(outs[g].shape) == 3:
            at = (slice(None),) + at
        return ref.at[at]

    moves.send(table_ref.at[1 - c], vec_pair, "vec_pair", 0, section=s, dp=y * 2 + 1 - c, mp=z)
    moves.wait(vec_pair, "vec_pair", 0)
    vec_here[...] = table_ref[c] + vec_pair[...]
    moves.send(vec_here.at[1 - s], vec_x, "vec_x", 0, section=1 - s, dp=d, mp=z)

    loads = {}

    def load(src, dst, when, key):
        at = len(loads)
        copy = pltpu.make_async_copy(src, dst, load_sems.at[at])
        if when is None:
            copy.start()
        else:
            pl.when(when)(copy.start)
        loads[key] = (copy, when)

    steps = [(g, k) for g in ORDER for k in place.nearest[::-1]]
    for g, k in steps:
        zz = place.other_z(k)
        for r in list(range(1, Y)) + [0]:
            slot = place.other_y(r) * MP + zz
            moves.send(
                part(there[g], g, zz, place.other_y(r)), paired[g].at[slot], "pair", g * Y * MP + slot,
                section=s, dp=y * 2 + 1 - c, mp=z,
            )
            load(part(own[g], g, zz, place.other_y(r)), held[g].at[slot], None, ("own", g, k, r))
        load(part(above[g], g, zz), mine[g].at[zz], s == 1, ("above", g, k))

    moves.wait(vec_x, "vec_x", 0)
    vec_here[s] = vec_here[s] + vec_x[...]
    for r in range(1, Y):
        at = Y - r - 1
        moves.send(
            vec_here.at[s, place.other_y(r)], vec_y.at[at], "vec_y", at, section=s, dp=place.other_y(r) * 2 + c, mp=z
        )
    for r in range(1, Y):
        moves.wait(vec_y.at[r - 1], "vec_y", r - 1)
    vec_here[s, y] = vec_here[s, y] + jnp.sum(vec_y[...], 0)
    for r in range(1, MP):
        moves.send(vec_here.at[s, y, place.other_z(r)], vec_z.at[z], "vec_z", z, section=s, dp=d, mp=place.other_z(r))

    number = s * MP + z
    active = number < pieces
    piece = 2 * lax.div(number, 2) + c
    for section, ref in ((0, first_ref), (1, last_ref)):
        for zz in range(MP):
            to_c = lax.rem(number, 2)
            here = (s == section) & (to_c == c) & (z == zz)
            dst = ends_ref.at[piece]
            moves.send(
                ref.at[zz], dst, "back", piece, active & jnp.logical_not(here), section=section, dp=y * 2 + to_c, mp=zz
            )

            @pl.when(active & here)
            def _():
                pltpu.make_async_copy(ref.at[zz], dst, moves.arrival("back", piece)).start()

    for g, k in steps:
        zz = place.other_z(k)
        moves.send(part(above[g], g, zz), from_x[g].at[zz], "from_x", g * MP + zz, s == 0, section=1 - s, dp=d, mp=z)

    def loaded(key):
        copy, when = loads[key]
        if when is None:
            copy.wait()
        else:
            pl.when(when)(copy.wait)

    def add_into(dst, *terms):
        total = dst[...].astype(WIDE)
        for term in terms:
            total = total + term[...].astype(WIDE)
        dst[...] = total.astype(LOW)

    def pair_step(g, k):
        zz = place.other_z(k)
        for r in list(range(1, Y)) + [0]:
            slot = place.other_y(r) * MP + zz
            moves.wait(paired[g].at[slot], "pair", g * Y * MP + slot)
            loaded(("own", g, k, r))
            if r:
                add_into(held[g].at[slot], paired[g].at[slot])
                out = (Y - r - 1) * MP + zz
                moves.send(
                    held[g].at[slot], from_y[g].at[out], "from_y", g * (Y - 1) * MP + out,
                    section=s, dp=place.other_y(r) * 2 + c, mp=z,
                )

    def rows_step(g, k):
        zz = place.other_z(k)
        slot = y * MP + zz
        slots = [(r - 1) * MP + zz for r in range(1, Y)]
        for at in slots:
            moves.wait(from_y[g].at[at], "from_y", g * (Y - 1) * MP + at)
        add_into(held[g].at[slot], paired[g].at[slot], *(from_y[g].at[at] for at in slots))
        moves.send(held[g].at[slot], from_x[g].at[zz], "from_x", g * MP + zz, s == 1, section=1 - s, dp=d, mp=z)

    def section_step(g, k):
        zz = place.other_z(k)
        moves.wait(from_x[g].at[zz], "from_x", g * MP + zz)
        loaded(("above", g, k))

        @pl.when(s == 0)
        def _():
            total = held[g][y * MP + zz].astype(WIDE) + from_x[g][zz].astype(WIDE)
            mine[g][zz] = total.astype(LOW)

        @pl.when(s == 1)
        def _():
            add_into(mine[g].at[zz], from_x[g].at[zz])

        if k:
            moves.send(mine[g].at[zz], from_z[g].at[z], "from_z", g * MP + z, section=s, dp=d, mp=zz)

    def columns_step(g):
        total = mine[g][z].astype(WIDE)
        for k in range(1, MP):
            zz = place.other_z(k)
            moves.wait(from_z[g].at[zz], "from_z", g * MP + zz)
            total = total + from_z[g][zz].astype(WIDE)
        outs[g][...] = total

    early, lag = 4, 2
    for at in range(-early, len(steps) + lag):
        if at + early < len(steps):
            pair_step(*steps[at + early])
        if 0 <= at < len(steps):
            rows_step(*steps[at])
        if at >= lag:
            section_step(*steps[at - lag])
        if at == 1:
            total = vec_here[s, y, z]
            for r in range(1, MP):
                moves.wait(vec_z.at[place.other_z(r)], "vec_z", place.other_z(r))
                total = total + vec_z[place.other_z(r)]
            sums_ref[...] = total

    for g in ORDER:
        columns_step(g)
    for p in range(pieces):
        moves.wait(ends_ref.at[p], "back", p)
    moves.finish()


def scatter(table, first, last, grads, shapes):
    S, DP, MP = (lax.axis_size(name) for name in ("section", "dp", "mp"))
    Y = DP // 2
    _, rows, block = first.shape
    pieces = grads["pieces"]
    names = ("qkv", "out", "fc1", "fc2")
    flat = [grads["own"][n] for n in names] + [grads["there"][n] for n in names] + [grads["above"][n] for n in names]
    counts = scatter_counts(S, Y, MP, pieces)
    vmem = pl.BlockSpec(memory_space=pltpu.VMEM)

    def room(count):
        return [pltpu.VMEM((count,) + shape, LOW) for shape in shapes]

    sends = 2 + Y - 1 + MP - 1 + S * MP + 4 * (Y * MP + (Y - 1) * MP + 2 * MP + MP - 1)
    return pl.pallas_call(
        functools.partial(scatter_kernel, pieces),
        in_specs=[vmem] + [HBM] * (2 + len(flat)),
        out_specs=[HBM] + [vmem] * 5,
        out_shape=[jax.ShapeDtypeStruct((pieces, rows, block), LOW), jax.ShapeDtypeStruct(table.shape[4:], WIDE)]
        + [jax.ShapeDtypeStruct(shape, WIDE) for shape in shapes],
        scratch_shapes=room(Y * MP)
        + room(Y * MP)
        + room(MP)
        + room(MP)
        + room((Y - 1) * MP)
        + room(MP)
        + [
            pltpu.SemaphoreType.DMA((sends,)),
            pltpu.SemaphoreType.DMA((sum(counts.values()),)),
            pltpu.SemaphoreType.DMA((4 * (Y + 1) * MP,)),
            pltpu.VMEM(table.shape[1:], WIDE),
            pltpu.VMEM(table.shape[1:], WIDE),
            pltpu.VMEM(table.shape[2:], WIDE),
            pltpu.VMEM((Y - 1,) + table.shape[3:], WIDE),
            pltpu.VMEM(table.shape[3:], WIDE),
        ],
        compiler_params=pltpu.CompilerParams(has_side_effects=True, vmem_limit_bytes=63 << 20),
    )(table, first, last, *flat)


def finish_kernel(small, landing_ref, sums_ref, qkv_ref, out_ref, fc1_ref, fc2_ref, ends_ref, *refs):
    projections, (g_out, g_fc1, g_fc2), vectors = refs[0:3], refs[3:6], refs[6:-2]
    wide, sems = refs[-2:]
    pieces, rows, _ = landing_ref.shape
    seq_len = ends_ref.shape[1]

    def end_copy(p):
        start = (seq_len - rows) * (p % 2)
        return pltpu.make_async_copy(wide.at[p], ends_ref.at[p // 2, pl.ds(start, rows), 0], sems.at[p])

    for p in list(range(1, pieces, 2)) + list(range(0, pieces, 2)):
        wide[p] = landing_ref[p].astype(WIDE)
        if p % 2:
            end_copy(p).start()
    for p in range(1, pieces, 2):
        end_copy(p).wait()
        end_copy(p - 1).start()
    for kind, ref in enumerate(projections):
        ref[...] = qkv_ref[kind]
    g_out[...] = out_ref[...].T
    g_fc1[...] = fc1_ref[...]
    g_fc2[...] = fc2_ref[...].T
    start = 0
    for ref in vectors:
        size = ref.shape[1]
        done = 0
        while done < size:
            row, lane = divmod(start + done, 128)
            count = min(128 - lane, size - done)
            ref[0:1, done : done + count] = sums_ref[row : row + 1, lane : lane + count]
            done += count
        start += size
    for p in range(0, pieces, 2):
        end_copy(p).wait()


def finish(ends, sums, grads, seq_len, sizes):
    pieces, rows, columns = ends.shape
    vmem = pl.BlockSpec(memory_space=pltpu.VMEM)
    qkv, out, fc1, fc2 = grads
    shapes = [qkv.shape[1:]] * 3 + [out.shape[::-1], fc1.shape, fc2.shape[::-1]] + [(1, size) for size in sizes]
    return pl.pallas_call(
        functools.partial(finish_kernel, sizes[0]),
        in_specs=[vmem] * 6,
        out_specs=[HBM] + [vmem] * len(shapes),
        out_shape=[jax.ShapeDtypeStruct((pieces // 2, seq_len, 1, columns), WIDE)]
        + [jax.ShapeDtypeStruct(shape, WIDE) for shape in shapes],
        scratch_shapes=[pltpu.VMEM((pieces, rows, columns), WIDE), pltpu.SemaphoreType.DMA((pieces,))],
        compiler_params=pltpu.CompilerParams(vmem_limit_bytes=32 << 20),
    )(ends, sums, qkv, out, fc1, fc2)


def nn(left, right):
    return lax.dot_general(left, right, (((1,), (0,)), ((), ())), preferred_element_type=WIDE)


def nt(left, right):
    return lax.dot_general(left, right, (((1,), (1,)), ((), ())), preferred_element_type=WIDE)


def tn(left, right):
    return lax.dot_general(left, right, (((0,), (0,)), ((), ())), preferred_element_type=WIDE)


def row_mean(value):
    return jnp.mean(value, 1, keepdims=True)


def column_sum(value):
    return jnp.sum(value.astype(WIDE), 0, keepdims=True)


def centre(rows_in):
    mean = row_mean(rows_in)
    inv_std = lax.rsqrt(row_mean(rows_in * rows_in) - mean * mean + epsilon)
    return (rows_in - mean) * inv_std, inv_std


def norm_back(grad, rows_in, gain):
    xhat, inv_std = centre(rows_in)
    weighted = grad * gain
    d_rows = inv_std * (weighted - row_mean(weighted) - xhat * row_mean(weighted * xhat))
    return d_rows, column_sum(grad * xhat), column_sum(grad)


def full(shape):
    return pl.BlockSpec(shape, lambda i: (0,) * len(shape))


def compute_call(kernel, steps, ins, outs, scratch, flops, args):
    return pl.pallas_call(
        kernel,
        grid=(steps,),
        in_specs=ins,
        out_specs=[spec for spec, _ in outs],
        out_shape=[shape for _, shape in outs],
        scratch_shapes=scratch,
        compiler_params=pltpu.CompilerParams(vmem_limit_bytes=58 << 20),
        cost_estimate=pl.CostEstimate(flops=1000, bytes_accessed=1000, transcendentals=0),
    )(*args)


LN1_GAIN, LN1_BIAS, B_QUERY, B_VALUE, B_OUT, SCALE_ATTN, LN2_GAIN, LN2_BIAS, B_FC2, SCALE_MLP = range(10)


def project_kernel(x_ref, vec_ref, w_ref, n_ref, kv_ref, q_ref):
    step = pl.program_id(0)

    @pl.when(step == 0)
    def _():
        xhat, _ = centre(x_ref[...])
        n_ref[...] = (xhat * vec_ref[LN1_GAIN][None] + vec_ref[LN1_BIAS][None]).astype(LOW)
        kv_ref[0] = nn(n_ref[...], w_ref[...]).astype(LOW)

    @pl.when(step == 1)
    def _():
        kv_ref[1] = (nn(n_ref[...], w_ref[...]) + vec_ref[B_VALUE][None]).astype(LOW)

    @pl.when(step == 2)
    def _():
        q_ref[...] = (nn(n_ref[...], w_ref[...]) + vec_ref[B_QUERY][None]).astype(LOW)


def project(rows_in, vec, attn):
    rows, width = rows_in.shape
    low = jax.ShapeDtypeStruct((rows, width), LOW)
    return compute_call(
        project_kernel,
        3,
        [
            full(rows_in.shape),
            full(vec.shape),
            pl.BlockSpec((None, width, width), lambda i: (lax.rem(i + 1, 3), 0, 0)),
        ],
        [
            (full(rows_in.shape), low),
            (full((2, rows, width)), jax.ShapeDtypeStruct((2, rows, width), LOW)),
            (full(rows_in.shape), low),
        ],
        [],
        6 * rows * width * width,
        (rows_in, vec, attn),
    )


PAD = 32
GROUP = 4


def of_head(value, head):
    lane = lax.broadcasted_iota(jnp.int32, (1, value.shape[1]), 1)
    return jnp.where((lane >= head * HD) & (lane < (head + 1) * HD), value, jnp.zeros_like(value))


def attend_kernel(q_ref, k0, k1, v0, v1, mask_ref, o_ref, wide_ref, scale_ref, p_ref, score_ref):
    rows = q_ref.shape[0]
    heads = q_ref.shape[1] // HD
    q = (q_ref[...].astype(WIDE) * (HD**-0.5)).astype(LOW)
    tops, totals, sums, outs, scales = {}, {}, {}, [], []

    def put(store, head, value, join):
        store[head] = join(store[head], value) if head in store else value

    for turn in range(heads + 2):
        for half, (k, v) in enumerate(((k0, v0), (k1, v1))):
            head = turn
            if head < heads:
                lanes = slice(head // 2 * 128, head // 2 * 128 + 128)
                score = nt(k[:, lanes], of_head(q[:, lanes], head % 2))
                first = score[:PAD] + mask_ref[:PAD, half : half + 1]
                score_ref[head % 2, half, :PAD] = first
                score_ref[head % 2, half, PAD:] = score[PAD:]
                put(tops, head, jnp.max(first, 0, keepdims=True), jnp.maximum)
                put(tops, head, jnp.max(score[PAD:], 0, keepdims=True), jnp.maximum)
            head = turn - 1
            if 0 <= head < heads:
                power = jnp.exp(score_ref[head % 2, half] - tops[head])
                put(totals, head, jnp.sum(power, 0, keepdims=True), jnp.add)
                p_ref[head, half] = power.astype(LOW)
            head = turn - 2
            if 0 <= head < heads:
                lanes = slice(head // 2 * 128, head // 2 * 128 + 128)
                put(sums, head, tn(v[:, lanes], p_ref[head, half]), jnp.add)
        head = turn - 2
        if 0 <= head < heads:
            scale = 1.0 / totals[head]
            outs.append(sums[head][head % 2 * HD : (head % 2 + 1) * HD] * scale)
            scales.append(jnp.broadcast_to(scale, (HD, rows)))
    out = jnp.concatenate(outs, 0).T
    wide_ref[...] = out
    o_ref[...] = out.astype(LOW)
    scale_ref[...] = jnp.concatenate(scales, 0).T


def attend(q, kv0, kv1, mask):
    rows, width = q.shape
    heads = width // HD
    lanes = GROUP * HD
    one = pl.BlockSpec((rows, lanes), lambda i: (0, i))
    key = pl.BlockSpec((None, rows, lanes), lambda i: (0, 0, i))
    value = pl.BlockSpec((None, rows, lanes), lambda i: (1, 0, i))
    return compute_call(
        attend_kernel,
        heads // GROUP,
        [one, key, key, value, value, full(mask.shape)],
        [
            (one, jax.ShapeDtypeStruct((rows, width), LOW)),
            (one, jax.ShapeDtypeStruct((rows, width), WIDE)),
            (one, jax.ShapeDtypeStruct((rows, width), WIDE)),
            (
                pl.BlockSpec((GROUP, 2, rows, rows), lambda i: (i, 0, 0, 0)),
                jax.ShapeDtypeStruct((heads, 2, rows, rows), LOW),
            ),
        ],
        [pltpu.VMEM((2, 2, rows, rows), WIDE)],
        32 * heads * rows * rows * HD,
        (q, kv0, kv1, kv0, kv1, mask),
    )


def mlp_kernel(x_ref, o_ref, vec_ref, bias_ref, wo_ref, w1_ref, w2_ref, y_ref, branch_ref, middle_ref, n_ref, act_ref, slope_ref, two_ref, total):
    step = pl.program_id(0)

    @pl.when(step == 0)
    def _():
        branch = nt(o_ref[...], wo_ref[...]) + vec_ref[B_OUT][None]
        branch_ref[...] = branch.astype(LOW)
        middle = x_ref[...] + vec_ref[SCALE_ATTN][None] * branch
        middle_ref[...] = middle
        xhat, _ = centre(middle)
        n_ref[...] = (xhat * vec_ref[LN2_GAIN][None] + vec_ref[LN2_BIAS][None]).astype(LOW)
        total[...] = jnp.zeros_like(total)

    hidden = nn(n_ref[...], w1_ref[...]) + bias_ref[0:1]
    cdf = 0.5 + 0.5 * lax.erf(hidden * inv_root_two)
    active = (hidden * cdf).astype(LOW)
    act_ref[...] = active
    slope_ref[...] = (cdf + hidden * jnp.exp(-0.5 * hidden * hidden) * inv_root_tau).astype(LOW)
    total[...] += nt(active, w2_ref[...])

    @pl.when(step == pl.num_programs(0) - 1)
    def _():
        two = total[...] + vec_ref[B_FC2][None]
        two_ref[...] = two.astype(LOW)
        y_ref[...] = middle_ref[...] + vec_ref[SCALE_MLP][None] * two


CHUNK = 512


def mlp(rows_in, out, vec, bias, weights):
    _, w_out, fc1, fc2 = weights
    rows, width = rows_in.shape
    hidden = fc1.shape[1]
    low = (full(rows_in.shape), jax.ShapeDtypeStruct((rows, width), LOW))
    wide = (full(rows_in.shape), jax.ShapeDtypeStruct((rows, width), WIDE))
    units = (pl.BlockSpec((rows, CHUNK), lambda i: (0, i)), jax.ShapeDtypeStruct((rows, hidden), LOW))
    weight = pl.BlockSpec((width, CHUNK), lambda i: (0, i))
    return compute_call(
        mlp_kernel,
        hidden // CHUNK,
        [
            full(rows_in.shape),
            full(rows_in.shape),
            full(vec.shape),
            pl.BlockSpec((8, CHUNK), lambda i: (0, i)),
            full((width, width)),
            weight,
            weight,
        ],
        [wide, low, wide, low, units, units, low],
        [pltpu.VMEM((rows, width), WIDE)],
        4 * rows * width * hidden,
        (rows_in, out, vec, bias, w_out, fc1, fc2),
    )


def own_rows_first(dst, value, c, count):
    size = value.shape[0] // (2 * count)
    for d in range(2 * count):
        at = lax.rem(c + d, 2) * count + d // 2
        dst[pl.ds(pl.multiple_of(at * size, size), size)] = value[d * size : (d + 1) * size]


def store_halves(value, own_ref, there_ref):
    count, size, _ = own_ref.shape
    for i in range(count):
        own_ref[i] = value[i * size : (i + 1) * size].astype(LOW)
        there_ref[i] = value[(count + i) * size : (count + i + 1) * size].astype(LOW)


def mlp_back_kernel(
    c_ref, dy_ref, vec_ref, two_ref, act_ref, slope_ref, n_ref, middle_ref, branch_ref, o_ref, wo_ref, w1_ref, w2_ref,
    grad_ref, do_ref, own1, there1, own2, there2, own_o, there_o, sums_ref, units_ref, dm, dm_t, n_t, total,
):
    step = pl.program_id(0)
    c, count = c_ref[0], own1.shape[0]

    @pl.when(step == 0)
    def _():
        low = (dy_ref[...] * vec_ref[SCALE_MLP][None]).astype(LOW)
        dm[...] = low
        own_rows_first(dm_t, low.T, c, count)
        own_rows_first(n_t, n_ref[...].T, c, count)
        sums_ref[0:1] = column_sum(dy_ref[...] * two_ref[...].astype(WIDE))
        sums_ref[1:2] = column_sum(low)
        total[...] = jnp.zeros_like(total)

    df = (nn(dm[...], w2_ref[...]) * slope_ref[...].astype(WIDE)).astype(LOW)
    units_ref[...] = jnp.broadcast_to(column_sum(df), units_ref.shape)
    store_halves(nn(dm_t[...], act_ref[...]), own2, there2)
    store_halves(nn(n_t[...], df), own1, there1)
    total[...] += nt(df, w1_ref[...])

    @pl.when(step == pl.num_programs(0) - 1)
    def _():
        d_rows, d_gain, d_bias = norm_back(total[...], middle_ref[...], vec_ref[LN2_GAIN][None])
        sums_ref[2:3] = d_gain
        sums_ref[3:4] = d_bias
        grad = dy_ref[...] + d_rows
        grad_ref[...] = grad
        sums_ref[4:5] = column_sum(grad * branch_ref[...].astype(WIDE))
        da = (grad * vec_ref[SCALE_ATTN][None]).astype(LOW)
        sums_ref[5:6] = column_sum(da)
        sums_ref[6:8] = jnp.zeros((2, sums_ref.shape[1]), WIDE)
        do_ref[...] = nn(da, wo_ref[...]).astype(LOW)
        own_rows_first(dm_t, da.T, c, count)
        store_halves(nn(dm_t[...], o_ref[...]), own_o, there_o)


def mlp_back(half, dy, vec, saved, weights, count):
    _, w_out, fc1, fc2 = weights
    rows, width = dy.shape
    hidden = fc1.shape[1]
    block = width // (2 * count)
    whole = full(dy.shape)
    low = (whole, jax.ShapeDtypeStruct((rows, width), LOW))
    wide = (whole, jax.ShapeDtypeStruct((rows, width), WIDE))
    units = pl.BlockSpec((rows, CHUNK), lambda i: (0, i))
    weight = pl.BlockSpec((width, CHUNK), lambda i: (0, i))
    grad = (
        pl.BlockSpec((count, block, CHUNK), lambda i: (0, 0, i)),
        jax.ShapeDtypeStruct((count, block, hidden), LOW),
    )
    grad_o = (full((count, block, width)), jax.ShapeDtypeStruct((count, block, width), LOW))
    return compute_call(
        mlp_back_kernel,
        hidden // CHUNK,
        [
            pl.BlockSpec(memory_space=pltpu.SMEM),
            whole,
            full(vec.shape),
            whole,
            units,
            units,
            whole,
            whole,
            whole,
            whole,
            full((width, width)),
            weight,
            weight,
        ],
        [
            wide,
            low,
            grad,
            grad,
            grad,
            grad,
            grad_o,
            grad_o,
            (full((8, width)), jax.ShapeDtypeStruct((8, width), WIDE)),
            (pl.BlockSpec((8, CHUNK), lambda i: (0, i)), jax.ShapeDtypeStruct((8, hidden), WIDE)),
        ],
        [
            pltpu.VMEM((rows, width), LOW),
            pltpu.VMEM((width, rows), LOW),
            pltpu.VMEM((width, rows), LOW),
            pltpu.VMEM((rows, width), WIDE),
        ],
        8 * rows * width * hidden,
        (
            half,
            dy,
            vec,
            saved["two"],
            saved["active"],
            saved["slope"],
            saved["n_two"],
            saved["middle"],
            saved["branch"],
            saved["out"],
            w_out,
            fc1,
            fc2,
        ),
    )


def attend_back_kernel(q_ref, k0, k1, v0, v1, p_ref, g_ref, o_ref, scale_ref, d0_ref, d1_ref):
    q = q_ref[...]
    scaled = (g_ref[...].astype(WIDE) * scale_ref[...]).astype(LOW)
    dots = (scaled.astype(WIDE) * o_ref[...]).T
    sums = {}
    dqs = []
    for head in range(q_ref.shape[1] // HD):
        g, here = of_head(scaled, head), of_head(q, head)
        dot = jnp.sum(dots[head * HD : (head + 1) * HD], 0, keepdims=True)
        dq = None
        for half, (k, v) in enumerate(((k0, v0), (k1, v1))):
            p = p_ref[head, half]
            ds = (p.astype(WIDE) * (nt(v[...], g) - dot)).astype(LOW)
            part = tn(k[...], ds)
            dq = part if dq is None else dq + part
            for name, value in (("v", nn(p, g)), ("k", nn(ds, here))):
                sums[name, half] = value if head == 0 else sums[name, half] + value
        dqs.append(dq[head * HD : (head + 1) * HD])
    d0_ref[0] = (jnp.concatenate(dqs, 0).T * (HD**-0.5)).astype(LOW)
    for half, (out, first) in enumerate(((d0_ref, 1), (d1_ref, 0))):
        out[first] = (sums["k", half] * (HD**-0.5)).astype(LOW)
        out[first + 1] = sums["v", half].astype(LOW)


def attend_back(q, kv0, kv1, probs, grad, out, scales):
    rows, width = q.shape
    steps, heads = width // 128, width // HD
    one = pl.BlockSpec((rows, 128), lambda i: (0, i))
    key = pl.BlockSpec((None, rows, 128), lambda i: (0, 0, i))
    value = pl.BlockSpec((None, rows, 128), lambda i: (1, 0, i))

    def several(count):
        return (
            pl.BlockSpec((count, rows, 128), lambda i: (0, 0, i)),
            jax.ShapeDtypeStruct((count, rows, width), LOW),
        )

    return compute_call(
        attend_back_kernel,
        steps,
        [one, key, key, value, value, pl.BlockSpec((2, 2, rows, rows), lambda i: (i, 0, 0, 0)), one, one, one],
        [several(3), several(2)],
        [],
        40 * heads * rows * rows * HD,
        (q, kv0, kv1, kv0, kv1, probs, grad, out, scales),
    )


def project_back_kernel(
    c_ref, d0_ref, d1_ref, n_ref, x_ref, grad_ref, vec_ref, w_ref, dx_ref, own, there, sums_ref, n_t, total
):
    step = pl.program_id(0)
    c, count = c_ref[0], own.shape[0]

    @pl.when(step == 0)
    def _():
        total[...] = jnp.zeros_like(total)
        own_rows_first(n_t, n_ref[...].T, c, count)

    theirs = jnp.where(step == 0, 0.0, d1_ref[...].astype(WIDE))
    grad = (d0_ref[...].astype(WIDE) + theirs).astype(LOW)
    store_halves(nn(n_t[...], grad), own, there)
    total[...] += nt(grad, w_ref[...])
    sums = column_sum(grad)

    @pl.when(step == 0)
    def _():
        sums_ref[0:1] = sums

    @pl.when(step == 2)
    def _():
        sums_ref[1:2] = sums
        d_rows, d_gain, d_bias = norm_back(total[...], x_ref[...], vec_ref[LN1_GAIN][None])
        sums_ref[2:3] = d_gain
        sums_ref[3:4] = d_bias
        sums_ref[4:8] = jnp.zeros((4, sums_ref.shape[1]), WIDE)
        dx_ref[...] = grad_ref[...] + d_rows


def project_back(half, d0, d1, saved, grad, vec, attn, count):
    rows, width = grad.shape
    block = width // (2 * count)
    whole = full(grad.shape)
    out = (
        pl.BlockSpec((None, count, block, width), lambda i: (i, 0, 0, 0)),
        jax.ShapeDtypeStruct((3, count, block, width), LOW),
    )
    return compute_call(
        project_back_kernel,
        3,
        [
            pl.BlockSpec(memory_space=pltpu.SMEM),
            pl.BlockSpec((None, rows, width), lambda i: (i, 0, 0)),
            pl.BlockSpec((None, rows, width), lambda i: (jnp.maximum(i - 1, 0), 0, 0)),
            whole,
            whole,
            whole,
            full(vec.shape),
            pl.BlockSpec((None, width, width), lambda i: (i, 0, 0)),
        ],
        [
            (whole, jax.ShapeDtypeStruct((rows, width), WIDE)),
            out,
            out,
            (full((8, width)), jax.ShapeDtypeStruct((8, width), WIDE)),
        ],
        [pltpu.VMEM((width, rows), LOW), pltpu.VMEM((rows, width), WIDE)],
        12 * rows * width * width,
        (half, d0, d1, saved["n_one"], saved["rows_in"], grad, vec, attn),
    )


def pick(stack, index, axis=0):
    return lax.dynamic_index_in_dim(stack, index, axis, keepdims=False)


def after(value, *others):
    return lax.optimization_barrier((value,) + others)[0]


def layer_forward(rows_in, vec, bias, weights, mask, from_pair, meanwhile):
    n_one, kv0, q = project(rows_in, vec, weights[0])
    kv1 = from_pair(kv0)
    out, out_wide, scales, probs = attend(q, kv0, kv1, mask)
    out = meanwhile(0, q, out)
    leaving, branch, middle, n_two, active, slope, two = mlp(rows_in, out, vec, bias, weights)
    leaving = meanwhile(1, out, leaving)
    saved = dict(
        rows_in=rows_in,
        n_one=n_one,
        q=q,
        kv0=kv0,
        kv1=kv1,
        out=out,
        out_wide=out_wide,
        scales=scales,
        probs=probs,
        branch=branch,
        middle=middle,
        n_two=n_two,
        active=active,
        slope=slope,
        two=two,
    )
    return (leaving, saved)


def layer_backward(grad_rows, saved, vec, weights, half, from_pair, sums_over, meanwhile):
    count = lax.axis_size("dp") // 2
    grad_middle, d_out, own1, there1, own2, there2, own_o, there_o, sums, units = mlp_back(
        half, grad_rows, vec, saved, weights, count
    )
    d_out = meanwhile("fc2", grad_rows, d_out)
    d0, d1 = attend_back(saved["q"], saved["kv0"], saved["kv1"], saved["probs"], d_out, saved["out_wide"], saved["scales"])
    own, there = dict(out=own_o, fc1=own1, fc2=own2), dict(out=there_o, fc1=there1, fc2=there2)
    d0 = meanwhile("fc1", d_out, d0)
    d1 = from_pair(d1)
    d0 = sums_over(own, there, d0)
    grad_in, own["qkv"], there["qkv"], sums_one = project_back(
        half, d0, d1, saved, grad_middle, vec, weights[0], count
    )
    grad_in = meanwhile("out", d0, grad_in)
    grad_in = meanwhile("qkv", d0, grad_in)
    vectors = dict(
        ln1_gain=sums_one[2],
        ln1_bias=sums_one[3],
        b_query=sums_one[0],
        b_value=sums_one[1],
        b_out=sums[5],
        scale_attn=sums[4],
        ln2_gain=sums[2],
        ln2_bias=sums[3],
        b_fc1=units[0],
        b_fc2=sums[1],
        scale_mlp=sums[0],
    )
    return (grad_in, own, there, vectors)


NARROW = ("ln1_gain", "ln1_bias", "b_query", "b_value", "b_out", "scale_attn", "ln2_gain", "ln2_bias", "b_fc2", "scale_mlp")


def local(
    boundary,
    ln1_gain,
    ln1_bias,
    w_query,
    w_key,
    w_value,
    b_query,
    b_value,
    w_out,
    b_out,
    scale_attn,
    ln2_gain,
    ln2_bias,
    w_fc1,
    b_fc1,
    w_fc2,
    b_fc2,
    scale_mlp,
):
    place = Place()
    _, micros, images, seq_len, columns = boundary.shape
    S, DP, MP = place.S, place.DP, place.MP
    width = columns * MP
    rows = half_rows(seq_len)
    pieces = 2 * micros
    number = place.s * MP + place.z
    active = number < pieces

    def from_pair(value):
        return lax.ppermute(value, "dp", [(i, i + 1 - 2 * (i % 2)) for i in range(DP)])

    def from_row(value, r):
        return lax.ppermute(value, "dp", [(i, (i - 2 * r) % DP) for i in range(DP)])

    turns = max(pieces, MP)
    spots = [(i, j, k) for i in range(S) for j in range(DP) for k in range(MP)]

    def move(value, target):
        number_of = {spot: i for i, spot in enumerate(spots)}
        pairs = [(number_of[spot], number_of[target(*spot)]) for spot in spots if target(*spot) is not None]
        return lax.ppermute(value, ("section", "dp", "mp"), pairs)

    def bring(blocks, which, began):
        got = []
        for turn in which:

            def target(i, j, k, turn=turn):
                piece = (turn + k) % turns
                image = 2 * (piece // 2) + j % 2
                if i != 1 or piece >= pieces:
                    return None
                return (image // MP, j // 2 * 2 + piece % 2, image % MP)

            piece = jnp.minimum(lax.rem(place.z + turn, turns), pieces - 1)
            got.append(move(after(pick(blocks, piece), began), target))
        return got

    def brought(got):
        here = 2 * lax.div(number, 2) + place.c
        stack = jnp.stack(got)
        return jnp.concatenate([pick(stack, lax.rem(here + turns - zz % turns, turns)) for zz in range(MP)], 1)

    def by_column(value):
        return jnp.stack([value[:, i * columns : (i + 1) * columns].astype(LOW) for i in range(MP)])

    waiting, above, projections = {}, {}, []

    def join(name, own, got):
        axis = own.ndim - 3

        def row(r):
            at = lax.rem(place.y + r, DP // 2)
            return pick(own, at, axis).astype(WIDE) + pick(got, at, axis).astype(WIDE)

        others = [row(r).astype(LOW) for r in range(1, DP // 2)]
        waiting[name] = (row, others)
        return others

    def sums_over(own, there, before):
        parts = []
        for name in own:
            parts += join(name, own[name], from_pair(there[name]))
        return after(before, *parts)

    def rows_meanwhile(name, before, done):
        if name == "fc2":
            own, there = projections
            got, done = lax.optimization_barrier((from_pair(after(there, before)), done))
            projections[:] = [own, got]
        row, others = waiting[name]
        got = [from_row(after(part, before), DP // 2 - r) for r, part in enumerate(others, 1)]
        got, done = lax.optimization_barrier((got, done))
        above[name] = (row, got)
        if name == "fc1":
            done = after(done, *join("qkv", *projections))
        return done

    def sums_done(name):
        row, got = above[name]
        total = row(0)
        for other in got:
            total = total + other.astype(WIDE)
        return total.astype(LOW)

    def from_rows(value, began):
        return [from_row(after(value, began), r) for r in range(1, DP // 2)]

    def from_section(value):
        return lax.ppermute(value, "section", [(i, S - 1 - i) for i in range(S)])

    def put_rows(weight, got, first=0):
        axis, block = weight.ndim - 2, weight.shape[-2] // DP
        for r, value in enumerate(got, 1):
            row = lax.rem(place.y + r, DP // 2) * 2
            for rows_of, part in ((row + place.c, value), (row + 1 - place.c, from_pair(value))):
                start = [jnp.int32(0)] * weight.ndim
                start[axis], start[-1] = rows_of * block, jnp.int32(first)
                weight = lax.dynamic_update_slice(weight, part, start)
        return weight

    spare = jnp.arange(rows)[:, None] < 2 * rows - seq_len
    mask = jnp.where(spare & (jnp.stack([place.c, 1 - place.c]) == 1)[None], -1e30, 0.0).astype(WIDE)
    mask = jnp.pad(mask, ((0, 0), (0, 126)))
    half = place.c.reshape(1)
    narrow = (ln1_gain, ln1_bias, b_query, b_value, b_out, scale_attn, ln2_gain, ln2_bias, b_fc2, scale_mlp)
    table = jnp.concatenate(list(narrow) + [jnp.zeros((16 - len(narrow), columns), WIDE)], 0)
    bias = jnp.broadcast_to(b_fc1, (8, b_fc1.shape[1]))
    qkv_shard = jnp.stack([w_query[0], w_key[0], w_value[0]])
    tokens = boundary.reshape(micros, seq_len, 1, columns)
    (arrived, sent, tables, all_biases), weights, later = gather(
        tokens, table, bias, qkv_shard, w_out[0].T, w_fc1[0], w_fc2[0].T
    )
    arrived = jnp.where(active, arrived.astype(WIDE), 0.0)
    vectors = [tables[layer] for layer in range(S)]
    biases = [all_biases[layer] for layer in range(S)]

    saved, cotangent, halves = [], [], []
    split = [range(turns)[i * turns // 3 : (i + 1) * turns // 3] for i in range(3)]
    rows_now = arrived
    for layer in range(S):
        def meanwhile(stage, before, done, layer=layer):
            at = 2 * layer + stage
            if at > 2:
                return done
            got = bring(sent, split[at], before)
            if at == 0:
                got, new, done = lax.optimization_barrier((got, from_rows(later[0], before), done))
                weights[1][0] = put_rows(weights[1][0], new)
            elif at == 1:
                got, new, done = lax.optimization_barrier((got, from_rows(later[3], before), done))
                halves.extend(new)
            else:
                new = ([from_section(after(h, before)) for h in halves], from_rows(later[2], before), from_rows(later[1], before))
                got, new, done = lax.optimization_barrier((got, new, done))
                first = place.s == 0
                fc2 = [
                    jnp.where(first, jnp.concatenate([h, o], -1), jnp.concatenate([o, h], -1))
                    for h, o in zip(halves, new[0])
                ]
                weights[1][3] = put_rows(weights[1][3], fc2)
                weights[1][2] = put_rows(weights[1][2], new[1], weights[1][2].shape[-1] // 2)
                weights[1][1] = put_rows(weights[1][1], new[2])
            cotangent.extend(got)
            return done

        rows_now, kept = layer_forward(
            rows_now, vectors[layer], biases[layer], weights[layer], mask, from_pair, meanwhile
        )
        saved.append(kept)
        if layer + 1 < S:
            rows_now = rows_now.astype(LOW).astype(WIDE)
    end_rows = rows_now

    grad_now = jnp.where(active, brought(cotangent).astype(WIDE), 0.0)
    vector_grads = [None] * S

    for layer in reversed(range(S)):
        grad_now, own, there, vector_grads[layer] = layer_backward(
            grad_now, saved[layer], vectors[layer], weights[layer], half, from_pair,
            sums_over if layer else (lambda own, there, before: before),
            (lambda name, before, done: done) if layer else rows_meanwhile,
        )
        if layer:
            projections[:] = [own["qkv"], there["qkv"]]
            grad_now = grad_now.astype(LOW).astype(WIDE)

    above = {name: sums_done(name) for name in ("fc2", "fc1", "out", "qkv")}
    grads = dict(own=own, there=there, above=above, pieces=pieces)
    shapes = [qkv_shard.shape, w_query.shape[1:], w_fc1.shape[1:], (w_fc2.shape[2], w_fc2.shape[1])]
    names = NARROW + ("b_fc1",)
    table = jnp.stack(
        [
            jnp.concatenate([vector_grads[layer][name].reshape(MP, DP, -1) for name in names], 2)
            for layer in range(S)
        ]
    )
    lines = -(-table.shape[3] // 1024) * 8
    table = jnp.pad(table, ((0, 0), (0, 0), (0, 0), (0, lines * 128 - table.shape[3])))
    table = table.reshape(S, MP, DP // 2, 2, lines, 128).transpose(3, 0, 2, 1, 4, 5)
    ends, summed, *sums = scatter(table, by_column(grad_now), by_column(end_rows), grads, shapes)
    sizes = [columns // DP] * len(NARROW) + [b_fc1.shape[1] // DP]
    ends, g_query, g_key, g_value, g_out, g_fc1, g_fc2, *vector_sums = finish(ends, summed, sums, seq_len, sizes)
    v = dict(zip(names, vector_sums))
    return (
        ends.reshape(boundary.shape),
        v["ln1_gain"],
        v["ln1_bias"],
        g_query[None],
        g_key[None],
        g_value[None],
        v["b_query"],
        v["b_value"],
        g_out[None],
        v["b_out"],
        v["scale_attn"],
        v["ln2_gain"],
        v["ln2_bias"],
        g_fc1[None],
        v["b_fc1"],
        g_fc2[None],
        v["b_fc2"],
        v["scale_mlp"],
    )


def solution(mesh):
    return jax.shard_map(
        local,
        mesh=mesh,
        in_specs=(
            P("section", None, "dp", None, "mp"),
            P("section", "mp"),
            P("section", "mp"),
            P("section", "dp", "mp"),
            P("section", "dp", "mp"),
            P("section", "dp", "mp"),
            P("section", "mp"),
            P("section", "mp"),
            P("section", "mp", "dp"),
            P("section", "mp"),
            P("section", "mp"),
            P("section", "mp"),
            P("section", "mp"),
            P("section", "dp", "mp"),
            P("section", "mp"),
            P("section", "mp", "dp"),
            P("section", "mp"),
            P("section", "mp"),
        ),
        out_specs=(
            P("section", None, "dp", None, "mp"),
            P("section", ("mp", "dp")),
            P("section", ("mp", "dp")),
            P("section", "dp", "mp"),
            P("section", "dp", "mp"),
            P("section", "dp", "mp"),
            P("section", ("mp", "dp")),
            P("section", ("mp", "dp")),
            P("section", "mp", "dp"),
            P("section", ("mp", "dp")),
            P("section", ("mp", "dp")),
            P("section", ("mp", "dp")),
            P("section", ("mp", "dp")),
            P("section", "dp", "mp"),
            P("section", ("mp", "dp")),
            P("section", "mp", "dp"),
            P("section", ("mp", "dp")),
            P("section", ("mp", "dp")),
        ),
        check_vma=False,
    )
```

```python
import functools

import jax
import jax.numpy as jnp
from jax import lax
from jax.experimental import pallas as pl
from jax.experimental.pallas import tpu as pltpu
from jax.sharding import PartitionSpec as P


HD = 64
LOW = jnp.bfloat16
WIDE = jnp.float32
HBM = pl.BlockSpec(memory_space=pltpu.HBM)

epsilon = 1e-06
inv_root_two = 0.7071067811865476
inv_root_tau = 0.3989422804014327


class Place:
    def __init__(self):
        self.S = lax.axis_size("section")
        self.DP = lax.axis_size("dp")
        self.MP = lax.axis_size("mp")
        self.Y = self.DP // 2
        self.H = self.MP // 2
        self.s = lax.axis_index("section")
        self.d = lax.axis_index("dp")
        self.z = lax.axis_index("mp")
        self.y = lax.div(self.d, 2)
        self.c = lax.rem(self.d, 2)
        self.nearest = sorted(range(self.MP), key=lambda r: min(r, self.MP - r))

    def other_y(self, r):
        return lax.rem(self.y + r, self.Y)

    def other_z(self, r):
        return lax.rem(self.z + r, self.MP)


class Moves:
    def __init__(self, send_sems, recv_sems, counts):
        self.send_sems, self.recv_sems = send_sems, recv_sems
        self.base, total = {}, 0
        for name, count in counts.items():
            self.base[name] = total
            total += count
        self.total = total
        self.sent = []

    def arrival(self, name, index):
        return self.recv_sems.at[self.base[name] + index]

    def send(self, src, dst, name, index, when=None, **to):
        at = len(self.sent)
        assert at < self.send_sems.shape[0]
        copy = pltpu.make_async_remote_copy(
            src_ref=src,
            dst_ref=dst,
            send_sem=self.send_sems.at[at],
            recv_sem=self.arrival(name, index),
            device_id=to,
        )
        self.sent.append((copy, when))
        if when is None:
            copy.start()
        else:
            pl.when(when)(copy.start)

    def send_one_of(self, options, name, when, **to):
        at = len(self.sent)
        assert at < self.send_sems.shape[0]
        for cond, src, dst, index in options:
            copy = pltpu.make_async_remote_copy(
                src_ref=src,
                dst_ref=dst,
                send_sem=self.send_sems.at[at],
                recv_sem=self.arrival(name, index),
                device_id=to,
            )
            pl.when(cond)(copy.start)
        self.sent.append((copy, when))

    def wait(self, ref, name, index):
        pltpu.make_async_copy(ref, ref, self.arrival(name, index)).wait()

    def finish(self):
        for copy, when in self.sent:
            if when is None:
                copy.wait_send()
            else:
                pl.when(when)(copy.wait_send)


def tile(start, size):
    return pl.ds(pl.multiple_of(start * size, size), size)


def holder(place, c, piece):
    image = 2 * (piece // 2) + c
    return lax.div(image, place.MP), piece % 2, lax.rem(image, place.MP)


def gather_counts(S, Y, MP, groups=4):
    return dict(rows=MP, vectors=S * MP, biases=S * MP, piece=groups * S * Y * MP, pair=groups * S * Y * MP)


def gather_kernel(pieces, tokens_ref, vec_ref, bias_ref, *refs):
    place = Place()
    s, y, c, z, d = place.s, place.y, place.c, place.z, place.d
    S, Y, MP, H = place.S, place.Y, place.MP, place.H
    shards, refs = refs[:4], refs[4:]
    rows_ref, sent_ref, vecs_ref, biases_ref = refs[:4]
    wholes = [refs[4 + g * S : 4 + (g + 1) * S] for g in range(4)]
    later, refs = refs[4 + 4 * S : 8 + 4 * S], refs[8 + 4 * S :]
    send_sems, recv_sems, own_sems, wide, load_sems = refs
    moves = Moves(send_sems, recv_sems, gather_counts(S, Y, MP))
    columns = sent_ref.shape[2]
    groups = range(4)

    def spot(g, l, yy, cc, zz):
        dd = yy * 2 + cc
        shard, whole = shards[g], wholes[g][l]
        at = (tile(dd, shard.shape[-2]), tile(zz, shard.shape[-1]))
        return whole.at[(slice(None),) + at] if len(shard.shape) == 3 else whole.at[at]

    def mark(g, l, yy, zz):
        return ((g * S + l) * Y + yy) * MP + zz

    def each(mine):
        return [(layer, (s == layer) if mine else (s != layer)) for layer in range(S)]

    def hand(g, mine, yy, zz, name, when, src, **to):
        moves.send_one_of(
            [
                (
                    cond if when is None else cond & when,
                    spot(g, layer, yy, c, zz) if src is None else src,
                    spot(g, layer, yy, c, zz),
                    mark(g, layer, yy, zz),
                )
                for layer, cond in each(mine)
            ],
            name,
            when,
            **to,
        )

    def to_pair(g, mine, zz, src=None, when=None):
        hand(g, mine, y, zz, "pair", when, src, section=s, dp=y * 2 + 1 - c, mp=z)

    def to_section(g, zz, when=None, src=None):
        hand(g, True, y, zz, "piece", when, src, section=1 - s, dp=d, mp=z)

    def along(g, zz, step, when, src=None):
        hand(g, True, y, zz, "piece", when, src, section=s, dp=d, mp=jnp.clip(z + step, 0, MP - 1))

    def rows_if(g, mine, zz, first_layer, there, src=None):
        when = first_layer | (zz < H) if g == 2 else first_layer
        for r in range(1, Y):
            hand(g, mine, y, zz, "piece", when & there, src, section=s, dp=place.other_y(r) * 2 + c, mp=z)

    def landed(g, l, yy, zz):
        moves.wait(spot(g, 0, yy, c, zz), "piece", mark(g, l, yy, zz))

    own_copies = []

    def columns_out(g):
        along(g, z, 1, z + 1 < MP, shards[g])
        along(g, z, -1, z >= 1, shards[g])
        to_section(g, z, src=shards[g])
        rows_if(g, True, z, s == 0, z >= 0, shards[g])
        to_pair(g, True, z, shards[g])
        for layer, cond in each(True):
            copy = pltpu.make_async_copy(shards[g], spot(g, layer, y, c, z), own_sems.at[g])
            pl.when(cond)(copy.start)
        own_copies.append(copy)

    def columns_in(g, far):
        for step, there in ((1, z >= far), (-1, z + far < MP)):
            zz = jnp.clip(z - step * far, 0, MP - 1)

            @pl.when(there)
            def _():
                landed(g, s, y, zz)

            along(g, zz, step, there & ((z + 1 < MP) if step == 1 else (z >= 1)))
            to_section(g, zz, there)
            rows_if(g, True, zz, s == 0, there)
            to_pair(g, True, zz, when=there)

    def section_in(g, far):
        for step, there in ((1, z >= far), (-1, z + far < MP))[: 2 if far else 1]:
            zz = jnp.clip(z - step * far, 0, MP - 1)

            @pl.when(there)
            def _():
                landed(g, 1 - s, y, zz)

            rows_if(g, False, zz, s == 1, there)
            to_pair(g, False, zz, when=there)

    def rows_in(g):
        for r in range(1, Y):
            yy = place.other_y(r)
            for layer, zz in [(0, zz) for zz in range(MP)] + ([(1, zz) for zz in range(H)] if g == 2 else []):
                landed(g, layer, yy, zz)
                there = spot(g, layer, yy, c, zz)
                moves.send(there, there, "pair", mark(g, layer, yy, zz), section=s, dp=y * 2 + 1 - c, mp=z)

    rows = rows_ref.shape[0]
    spare = 2 * rows - tokens_ref.shape[1]
    loads = []
    for piece in range(pieces):
        start = (rows - spare) * (piece % 2)
        copy = pltpu.make_async_copy(
            tokens_ref.at[piece // 2, pl.ds(start, rows), 0], wide.at[piece], load_sems.at[piece]
        )
        copy.start()
        loads.append(copy)

    own_vectors = []
    for i, (ref, whole, name) in enumerate(((vec_ref, vecs_ref, "vectors"), (bias_ref, biases_ref, "biases"))):
        there = whole.at[s, :, tile(z, ref.shape[1])]
        for q in range(1, S * MP):
            at = lax.rem(s * MP + z + q, S * MP)
            moves.send(ref, there, name, s * MP + z, section=lax.div(at, MP), dp=d, mp=lax.rem(at, MP))
        own_vectors.append(pltpu.make_async_copy(ref, there, own_sems.at[4 + i]))
        own_vectors[-1].start()

    for g in groups:
        columns_out(g)
    for piece in range(pieces):
        loads[piece].wait()
        low = wide[piece]
        if piece % 2 and spare:
            low = jnp.where(lax.broadcasted_iota(jnp.int32, (rows, 1), 0) < spare, 0.0, low)
        sent_ref[piece] = low.astype(LOW)
    for piece in range(pieces):
        to_s, to_c, to_z = holder(place, c, piece)
        here = (to_s == s) & (to_c == c) & (to_z == z)
        there = rows_ref.at[:, tile(z, columns)]
        moves.send(
            sent_ref.at[piece], there, "rows", z, (s == 0) & jnp.logical_not(here),
            section=to_s, dp=y * 2 + to_c, mp=to_z,
        )

        @pl.when((s == 0) & here)
        def _():
            pltpu.make_async_copy(sent_ref.at[piece], there, moves.arrival("rows", z)).start()

    for far in range(1, MP):
        for g in groups:
            columns_in(g, far)
            section_in(g, far - 1)
    for g in groups:
        section_in(g, MP - 1)
    for copy in own_copies:
        copy.wait()
    later_copies = []
    for g in groups:
        shard, there = shards[g], later[g]
        at = (tile(d, shard.shape[-2]),)
        if g < 2:
            at = at + (slice(None),)
        else:
            at = at + (tile(1 if g == 2 else s, there.shape[-1]),)
        src = wholes[g][1].at[(slice(None),) + at] if len(shard.shape) == 3 else wholes[g][1].at[at]
        copy = pltpu.make_async_copy(src, there, own_sems.at[6 + g])
        copy.start()
        later_copies.append(copy)
    for g in groups:
        rows_in(g)

    @pl.when(s * MP + z < pieces)
    def _():
        for zz in range(MP):
            moves.wait(rows_ref.at[:, tile(zz, columns)], "rows", zz)

    for q in range(1, S * MP):
        at = lax.rem(s * MP + z + q, S * MP)
        for ref, whole, name in ((vec_ref, vecs_ref, "vectors"), (bias_ref, biases_ref, "biases")):
            moves.wait(whole.at[lax.div(at, MP), :, tile(lax.rem(at, MP), ref.shape[1])], name, at)
    for g in groups:
        for zz in range(MP):
            for r in range(Y):
                yy = place.other_y(r)
                moves.wait(spot(g, 0, yy, 1 - c, zz), "pair", mark(g, 0, yy, zz))
                if g == 2 and zz < H and r:
                    moves.wait(spot(g, 1, yy, 1 - c, zz), "pair", mark(g, 1, yy, zz))
            for layer in range(1, S):
                moves.wait(spot(g, 0, y, 1 - c, zz), "pair", mark(g, layer, y, zz))
    for copy in own_vectors + later_copies:
        copy.wait()
    moves.finish()


def gather(tokens, vec, bias, *shards):
    S, DP, MP = (lax.axis_size(name) for name in ("section", "dp", "mp"))
    Y = DP // 2
    micros, seq_len, _, columns = tokens.shape
    pieces, rows = 2 * micros, half_rows(seq_len)
    counts = gather_counts(S, Y, MP)
    sends = pieces + 2 * (S * MP - 1) + 4 * (2 * MP + (2 * MP - 1) * (1 + 2 * Y) + (Y - 1) * MP) + (Y - 1) * (MP // 2)
    whole = [
        jax.ShapeDtypeStruct(shard.shape[:-2] + (shard.shape[-2] * DP, shard.shape[-1] * MP), LOW) for shard in shards
    ]
    later = [
        jax.ShapeDtypeStruct(shard.shape[:-1] + (shard.shape[-1] * MP // (1 if g < 2 else 2),), LOW)
        for g, shard in enumerate(shards)
    ]
    vmem = pl.BlockSpec(memory_space=pltpu.VMEM)
    got = pl.pallas_call(
        functools.partial(gather_kernel, pieces),
        in_specs=[vmem] * 7,
        out_specs=[HBM, vmem] + [HBM] * (2 + 4 * S) + [vmem] * 4,
        out_shape=[
            jax.ShapeDtypeStruct((rows, columns * MP), LOW),
            jax.ShapeDtypeStruct((pieces, rows, columns), LOW),
            jax.ShapeDtypeStruct((S, vec.shape[0], vec.shape[1] * MP), WIDE),
            jax.ShapeDtypeStruct((S, bias.shape[0], bias.shape[1] * MP), WIDE),
        ]
        + [shape for shape in whole for _ in range(S)]
        + later,
        scratch_shapes=[
            pltpu.SemaphoreType.DMA((sends,)),
            pltpu.SemaphoreType.DMA((sum(counts.values()),)),
            pltpu.SemaphoreType.DMA((10,)),
            pltpu.VMEM((pieces, rows, columns), WIDE),
            pltpu.SemaphoreType.DMA((pieces,)),
        ],
        compiler_params=pltpu.CompilerParams(has_side_effects=True, vmem_limit_bytes=63 << 20),
    )(tokens, vec, bias, *shards)
    return got[:4], [[got[4 + g * S + layer] for g in range(4)] for layer in range(S)], got[4 + 4 * S :]


def half_rows(seq_len):
    return -(-seq_len // 32) * 16


def scatter_counts(S, Y, MP, pieces, groups=4):
    return dict(
        back=max(pieces, MP),
        pair=groups * Y * MP,
        from_x=groups * MP,
        from_y=groups * (Y - 1) * MP,
        from_z=groups * MP,
        vec_pair=1,
        vec_x=1,
        vec_y=Y - 1,
        vec_z=MP,
    )


ORDER = (3, 2, 0, 1)


def scatter_kernel(pieces, table_ref, first_ref, last_ref, *refs):
    place = Place()
    s, y, c, z, d = place.s, place.y, place.c, place.z, place.d
    S, Y, MP = place.S, place.Y, place.MP
    own, there, above = refs[0:4], refs[4:8], refs[8:12]
    ends_ref, sums_ref, outs = refs[12], refs[13], refs[14:18]
    held, paired, mine, from_x, from_y, from_z = (refs[18 + 4 * i : 22 + 4 * i] for i in range(6))
    send_sems, recv_sems, load_sems, vec_here, vec_pair, vec_x, vec_y, vec_z = refs[42:]
    moves = Moves(send_sems, recv_sems, scatter_counts(S, Y, MP, pieces))

    def part(ref, g, zz, yy=None):
        at = (slice(None), tile(zz, outs[g].shape[-1]))
        if yy is not None:
            at = (yy,) + at
        if len(outs[g].shape) == 3:
            at = (slice(None),) + at
        return ref.at[at]

    moves.send(table_ref.at[1 - c], vec_pair, "vec_pair", 0, section=s, dp=y * 2 + 1 - c, mp=z)
    moves.wait(vec_pair, "vec_pair", 0)
    vec_here[...] = table_ref[c] + vec_pair[...]
    moves.send(vec_here.at[1 - s], vec_x, "vec_x", 0, section=1 - s, dp=d, mp=z)

    loads = {}

    def load(src, dst, when, key):
        at = len(loads)
        copy = pltpu.make_async_copy(src, dst, load_sems.at[at])
        if when is None:
            copy.start()
        else:
            pl.when(when)(copy.start)
        loads[key] = (copy, when)

    steps = [(g, k) for g in ORDER for k in place.nearest[::-1]]
    for g, k in steps:
        zz = place.other_z(k)
        for r in list(range(1, Y)) + [0]:
            slot = place.other_y(r) * MP + zz
            moves.send(
                part(there[g], g, zz, place.other_y(r)), paired[g].at[slot], "pair", g * Y * MP + slot,
                section=s, dp=y * 2 + 1 - c, mp=z,
            )
            load(part(own[g], g, zz, place.other_y(r)), held[g].at[slot], None, ("own", g, k, r))
        load(part(above[g], g, zz), mine[g].at[zz], s == 1, ("above", g, k))

    moves.wait(vec_x, "vec_x", 0)
    vec_here[s] = vec_here[s] + vec_x[...]
    for r in range(1, Y):
        at = Y - r - 1
        moves.send(
            vec_here.at[s, place.other_y(r)], vec_y.at[at], "vec_y", at, section=s, dp=place.other_y(r) * 2 + c, mp=z
        )
    for r in range(1, Y):
        moves.wait(vec_y.at[r - 1], "vec_y", r - 1)
    vec_here[s, y] = vec_here[s, y] + jnp.sum(vec_y[...], 0)
    for r in range(1, MP):
        moves.send(vec_here.at[s, y, place.other_z(r)], vec_z.at[z], "vec_z", z, section=s, dp=d, mp=place.other_z(r))

    number = s * MP + z
    active = number < pieces
    piece = 2 * lax.div(number, 2) + c
    for section, ref in ((0, first_ref), (1, last_ref)):
        for zz in range(MP):
            to_c = lax.rem(number, 2)
            here = (s == section) & (to_c == c) & (z == zz)
            dst = ends_ref.at[piece]
            moves.send(
                ref.at[:, tile(zz, dst.shape[1])], dst, "back", piece, active & jnp.logical_not(here), section=section, dp=y * 2 + to_c, mp=zz
            )

            @pl.when(active & here)
            def _():
                pltpu.make_async_copy(ref.at[:, tile(zz, dst.shape[1])], dst, moves.arrival("back", piece)).start()

    for g, k in steps:
        zz = place.other_z(k)
        moves.send(part(above[g], g, zz), from_x[g].at[zz], "from_x", g * MP + zz, s == 0, section=1 - s, dp=d, mp=z)

    def loaded(key):
        copy, when = loads[key]
        if when is None:
            copy.wait()
        else:
            pl.when(when)(copy.wait)

    def add_into(dst, *terms):
        total = dst[...].astype(WIDE)
        for term in terms:
            total = total + term[...].astype(WIDE)
        dst[...] = total.astype(LOW)

    def pair_step(g, k):
        zz = place.other_z(k)
        for r in list(range(1, Y)) + [0]:
            slot = place.other_y(r) * MP + zz
            moves.wait(paired[g].at[slot], "pair", g * Y * MP + slot)
            loaded(("own", g, k, r))
            if r:
                add_into(held[g].at[slot], paired[g].at[slot])
                out = (Y - r - 1) * MP + zz
                moves.send(
                    held[g].at[slot], from_y[g].at[out], "from_y", g * (Y - 1) * MP + out,
                    section=s, dp=place.other_y(r) * 2 + c, mp=z,
                )

    def rows_step(g, k):
        zz = place.other_z(k)
        slot = y * MP + zz
        slots = [(r - 1) * MP + zz for r in range(1, Y)]
        for at in slots:
            moves.wait(from_y[g].at[at], "from_y", g * (Y - 1) * MP + at)
        add_into(held[g].at[slot], paired[g].at[slot], *(from_y[g].at[at] for at in slots))
        moves.send(held[g].at[slot], from_x[g].at[zz], "from_x", g * MP + zz, s == 1, section=1 - s, dp=d, mp=z)

    def section_step(g, k):
        zz = place.other_z(k)
        moves.wait(from_x[g].at[zz], "from_x", g * MP + zz)
        loaded(("above", g, k))

        @pl.when(s == 0)
        def _():
            total = held[g][y * MP + zz].astype(WIDE) + from_x[g][zz].astype(WIDE)
            mine[g][zz] = total.astype(LOW)

        @pl.when(s == 1)
        def _():
            add_into(mine[g].at[zz], from_x[g].at[zz])

        if k:
            moves.send(mine[g].at[zz], from_z[g].at[z], "from_z", g * MP + z, section=s, dp=d, mp=zz)

    def columns_step(g):
        total = mine[g][z].astype(WIDE)
        for k in range(1, MP):
            zz = place.other_z(k)
            moves.wait(from_z[g].at[zz], "from_z", g * MP + zz)
            total = total + from_z[g][zz].astype(WIDE)
        outs[g][...] = total

    early, lag = 4, 2
    for at in range(-early, len(steps) + lag):
        if at + early < len(steps):
            pair_step(*steps[at + early])
        if 0 <= at < len(steps):
            rows_step(*steps[at])
        if at >= lag:
            section_step(*steps[at - lag])
        if at == 1:
            total = vec_here[s, y, z]
            for r in range(1, MP):
                moves.wait(vec_z.at[place.other_z(r)], "vec_z", place.other_z(r))
                total = total + vec_z[place.other_z(r)]
            sums_ref[...] = total

    for g in ORDER:
        columns_step(g)
    for p in range(pieces):
        moves.wait(ends_ref.at[p], "back", p)
    moves.finish()


def scatter(table, first, last, grads, shapes):
    S, DP, MP = (lax.axis_size(name) for name in ("section", "dp", "mp"))
    Y = DP // 2
    rows, block = first.shape[0], first.shape[1] // MP
    pieces = grads["pieces"]
    names = ("qkv", "out", "fc1", "fc2")
    flat = [grads["own"][n] for n in names] + [grads["there"][n] for n in names] + [grads["above"][n] for n in names]
    counts = scatter_counts(S, Y, MP, pieces)
    vmem = pl.BlockSpec(memory_space=pltpu.VMEM)

    def room(count):
        return [pltpu.VMEM((count,) + shape, LOW) for shape in shapes]

    sends = 2 + Y - 1 + MP - 1 + S * MP + 4 * (Y * MP + (Y - 1) * MP + 2 * MP + MP - 1)
    return pl.pallas_call(
        functools.partial(scatter_kernel, pieces),
        in_specs=[vmem] + [HBM] * (2 + len(flat)),
        out_specs=[HBM] + [vmem] * 5,
        out_shape=[jax.ShapeDtypeStruct((pieces, rows, block), LOW), jax.ShapeDtypeStruct(table.shape[4:], WIDE)]
        + [jax.ShapeDtypeStruct(shape, WIDE) for shape in shapes],
        scratch_shapes=room(Y * MP)
        + room(Y * MP)
        + room(MP)
        + room(MP)
        + room((Y - 1) * MP)
        + room(MP)
        + [
            pltpu.SemaphoreType.DMA((sends,)),
            pltpu.SemaphoreType.DMA((sum(counts.values()),)),
            pltpu.SemaphoreType.DMA((4 * (Y + 1) * MP,)),
            pltpu.VMEM(table.shape[1:], WIDE),
            pltpu.VMEM(table.shape[1:], WIDE),
            pltpu.VMEM(table.shape[2:], WIDE),
            pltpu.VMEM((Y - 1,) + table.shape[3:], WIDE),
            pltpu.VMEM(table.shape[3:], WIDE),
        ],
        compiler_params=pltpu.CompilerParams(has_side_effects=True, vmem_limit_bytes=63 << 20),
    )(table, first, last, *flat)


def finish_kernel(small, landing_ref, sums_ref, qkv_ref, out_ref, fc1_ref, fc2_ref, ends_ref, *refs):
    projections, (g_out, g_fc1, g_fc2), vectors = refs[0:3], refs[3:6], refs[6:-2]
    wide, sems = refs[-2:]
    pieces, rows, _ = landing_ref.shape
    seq_len = ends_ref.shape[1]

    def end_copy(p):
        start = (seq_len - rows) * (p % 2)
        return pltpu.make_async_copy(wide.at[p], ends_ref.at[p // 2, pl.ds(start, rows), 0], sems.at[p])

    for p in list(range(1, pieces, 2)) + list(range(0, pieces, 2)):
        wide[p] = landing_ref[p].astype(WIDE)
        if p % 2:
            end_copy(p).start()
    for p in range(1, pieces, 2):
        end_copy(p).wait()
        end_copy(p - 1).start()
    for kind, ref in enumerate(projections):
        ref[...] = qkv_ref[kind]
    g_out[...] = out_ref[...].T
    g_fc1[...] = fc1_ref[...]
    g_fc2[...] = fc2_ref[...].T
    start = 0
    for ref in vectors:
        size = ref.shape[1]
        done = 0
        while done < size:
            row, lane = divmod(start + done, 128)
            count = min(128 - lane, size - done)
            ref[0:1, done : done + count] = sums_ref[row : row + 1, lane : lane + count]
            done += count
        start += size
    for p in range(0, pieces, 2):
        end_copy(p).wait()


def finish(ends, sums, grads, seq_len, sizes):
    pieces, rows, columns = ends.shape
    vmem = pl.BlockSpec(memory_space=pltpu.VMEM)
    qkv, out, fc1, fc2 = grads
    shapes = [qkv.shape[1:]] * 3 + [out.shape[::-1], fc1.shape, fc2.shape[::-1]] + [(1, size) for size in sizes]
    return pl.pallas_call(
        functools.partial(finish_kernel, sizes[0]),
        in_specs=[vmem] * 6,
        out_specs=[HBM] + [vmem] * len(shapes),
        out_shape=[jax.ShapeDtypeStruct((pieces // 2, seq_len, 1, columns), WIDE)]
        + [jax.ShapeDtypeStruct(shape, WIDE) for shape in shapes],
        scratch_shapes=[pltpu.VMEM((pieces, rows, columns), WIDE), pltpu.SemaphoreType.DMA((pieces,))],
        compiler_params=pltpu.CompilerParams(vmem_limit_bytes=32 << 20),
    )(ends, sums, qkv, out, fc1, fc2)


def nn(left, right):
    return lax.dot_general(left, right, (((1,), (0,)), ((), ())), preferred_element_type=WIDE)


def nt(left, right):
    return lax.dot_general(left, right, (((1,), (1,)), ((), ())), preferred_element_type=WIDE)


def tn(left, right):
    return lax.dot_general(left, right, (((0,), (0,)), ((), ())), preferred_element_type=WIDE)


def row_mean(value):
    return jnp.mean(value, 1, keepdims=True)


def column_sum(value):
    return jnp.sum(value.astype(WIDE), 0, keepdims=True)


def centre(rows_in):
    mean = row_mean(rows_in)
    inv_std = lax.rsqrt(row_mean(rows_in * rows_in) - mean * mean + epsilon)
    return (rows_in - mean) * inv_std, inv_std


def norm_back(grad, rows_in, gain):
    xhat, inv_std = centre(rows_in)
    weighted = grad * gain
    d_rows = inv_std * (weighted - row_mean(weighted) - xhat * row_mean(weighted * xhat))
    return d_rows, column_sum(grad * xhat), column_sum(grad)


def full(shape):
    return pl.BlockSpec(shape, lambda i: (0,) * len(shape))


def compute_call(kernel, steps, ins, outs, scratch, flops, args):
    return pl.pallas_call(
        kernel,
        grid=(steps,),
        in_specs=ins,
        out_specs=[spec for spec, _ in outs],
        out_shape=[shape for _, shape in outs],
        scratch_shapes=scratch,
        compiler_params=pltpu.CompilerParams(vmem_limit_bytes=58 << 20),
        cost_estimate=pl.CostEstimate(flops=1000, bytes_accessed=1000, transcendentals=0),
    )(*args)


LN1_GAIN, LN1_BIAS, B_QUERY, B_VALUE, B_OUT, SCALE_ATTN, LN2_GAIN, LN2_BIAS, B_FC2, SCALE_MLP = range(10)


def project_kernel(x_ref, vec_ref, w_ref, n_ref, kv_ref, q_ref):
    step = pl.program_id(0)

    @pl.when(step == 0)
    def _():
        xhat, _ = centre(x_ref[...])
        n_ref[...] = (xhat * vec_ref[LN1_GAIN][None] + vec_ref[LN1_BIAS][None]).astype(LOW)
        kv_ref[0] = nn(n_ref[...], w_ref[...]).astype(LOW)

    @pl.when(step == 1)
    def _():
        kv_ref[1] = (nn(n_ref[...], w_ref[...]) + vec_ref[B_VALUE][None]).astype(LOW)

    @pl.when(step == 2)
    def _():
        q_ref[...] = (nn(n_ref[...], w_ref[...]) + vec_ref[B_QUERY][None]).astype(LOW)


def project(rows_in, vec, attn):
    rows, width = rows_in.shape
    low = jax.ShapeDtypeStruct((rows, width), LOW)
    return compute_call(
        project_kernel,
        3,
        [
            full(rows_in.shape),
            full(vec.shape),
            pl.BlockSpec((None, width, width), lambda i: (lax.rem(i + 1, 3), 0, 0)),
        ],
        [
            (full(rows_in.shape), low),
            (full((2, rows, width)), jax.ShapeDtypeStruct((2, rows, width), LOW)),
            (full(rows_in.shape), low),
        ],
        [],
        6 * rows * width * width,
        (rows_in, vec, attn),
    )


PAD = 32
GROUP = 4


def of_head(value, head):
    lane = lax.broadcasted_iota(jnp.int32, (1, value.shape[1]), 1)
    return jnp.where((lane >= head * HD) & (lane < (head + 1) * HD), value, jnp.zeros_like(value))


def attend_kernel(q_ref, k0, k1, v0, v1, mask_ref, o_ref, wide_ref, scale_ref, p_ref, score_ref):
    rows = q_ref.shape[0]
    heads = q_ref.shape[1] // HD
    q = (q_ref[...].astype(WIDE) * (HD**-0.5)).astype(LOW)
    tops, totals, sums, outs, scales = {}, {}, {}, [], []

    def put(store, head, value, join):
        store[head] = join(store[head], value) if head in store else value

    for turn in range(heads + 2):
        for half, (k, v) in enumerate(((k0, v0), (k1, v1))):
            head = turn
            if head < heads:
                lanes = slice(head // 2 * 128, head // 2 * 128 + 128)
                score = nt(k[:, lanes], of_head(q[:, lanes], head % 2))
                first = score[:PAD] + mask_ref[:PAD, half : half + 1]
                score_ref[head % 2, half, :PAD] = first
                score_ref[head % 2, half, PAD:] = score[PAD:]
                put(tops, head, jnp.max(first, 0, keepdims=True), jnp.maximum)
                put(tops, head, jnp.max(score[PAD:], 0, keepdims=True), jnp.maximum)
            head = turn - 1
            if 0 <= head < heads:
                power = jnp.exp(score_ref[head % 2, half] - tops[head])
                put(totals, head, jnp.sum(power, 0, keepdims=True), jnp.add)
                p_ref[head, half] = power.astype(LOW)
            head = turn - 2
            if 0 <= head < heads:
                lanes = slice(head // 2 * 128, head // 2 * 128 + 128)
                put(sums, head, tn(v[:, lanes], p_ref[head, half]), jnp.add)
        head = turn - 2
        if 0 <= head < heads:
            scale = 1.0 / totals[head]
            outs.append(sums[head][head % 2 * HD : (head % 2 + 1) * HD] * scale)
            scales.append(jnp.broadcast_to(scale, (HD, rows)))
    out = jnp.concatenate(outs, 0).T
    wide_ref[...] = out
    o_ref[...] = out.astype(LOW)
    scale_ref[...] = jnp.concatenate(scales, 0).T


def attend(q, kv0, kv1, mask):
    rows, width = q.shape
    heads = width // HD
    lanes = GROUP * HD
    one = pl.BlockSpec((rows, lanes), lambda i: (0, i))
    key = pl.BlockSpec((None, rows, lanes), lambda i: (0, 0, i))
    value = pl.BlockSpec((None, rows, lanes), lambda i: (1, 0, i))
    return compute_call(
        attend_kernel,
        heads // GROUP,
        [one, key, key, value, value, full(mask.shape)],
        [
            (one, jax.ShapeDtypeStruct((rows, width), LOW)),
            (one, jax.ShapeDtypeStruct((rows, width), WIDE)),
            (one, jax.ShapeDtypeStruct((rows, width), WIDE)),
            (
                pl.BlockSpec((GROUP, 2, rows, rows), lambda i: (i, 0, 0, 0)),
                jax.ShapeDtypeStruct((heads, 2, rows, rows), LOW),
            ),
        ],
        [pltpu.VMEM((2, 2, rows, rows), WIDE)],
        32 * heads * rows * rows * HD,
        (q, kv0, kv1, kv0, kv1, mask),
    )


def mlp_kernel(x_ref, o_ref, vec_ref, bias_ref, wo_ref, w1_ref, w2_ref, y_ref, low_ref, branch_ref, middle_ref, n_ref, act_ref, slope_ref, two_ref, total):
    step = pl.program_id(0)

    @pl.when(step == 0)
    def _():
        branch = nt(o_ref[...], wo_ref[...]) + vec_ref[B_OUT][None]
        branch_ref[...] = branch.astype(LOW)
        middle = x_ref[...] + vec_ref[SCALE_ATTN][None] * branch
        middle_ref[...] = middle
        xhat, _ = centre(middle)
        n_ref[...] = (xhat * vec_ref[LN2_GAIN][None] + vec_ref[LN2_BIAS][None]).astype(LOW)
        total[...] = jnp.zeros_like(total)

    hidden = nn(n_ref[...], w1_ref[...]) + bias_ref[0:1]
    cdf = 0.5 + 0.5 * lax.erf(hidden * inv_root_two)
    active = (hidden * cdf).astype(LOW)
    act_ref[...] = active
    slope_ref[...] = (cdf + hidden * jnp.exp(-0.5 * hidden * hidden) * inv_root_tau).astype(LOW)
    total[...] += nt(active, w2_ref[...])

    @pl.when(step == pl.num_programs(0) - 1)
    def _():
        two = total[...] + vec_ref[B_FC2][None]
        two_ref[...] = two.astype(LOW)
        low = (middle_ref[...] + vec_ref[SCALE_MLP][None] * two).astype(LOW)
        low_ref[...] = low
        y_ref[...] = low.astype(WIDE)


CHUNK = 512


def mlp(rows_in, out, vec, bias, weights):
    _, w_out, fc1, fc2 = weights
    rows, width = rows_in.shape
    hidden = fc1.shape[1]
    low = (full(rows_in.shape), jax.ShapeDtypeStruct((rows, width), LOW))
    wide = (full(rows_in.shape), jax.ShapeDtypeStruct((rows, width), WIDE))
    units = (pl.BlockSpec((rows, CHUNK), lambda i: (0, i)), jax.ShapeDtypeStruct((rows, hidden), LOW))
    weight = pl.BlockSpec((width, CHUNK), lambda i: (0, i))
    return compute_call(
        mlp_kernel,
        hidden // CHUNK,
        [
            full(rows_in.shape),
            full(rows_in.shape),
            full(vec.shape),
            pl.BlockSpec((8, CHUNK), lambda i: (0, i)),
            full((width, width)),
            weight,
            weight,
        ],
        [wide, low, low, wide, low, units, units, low],
        [pltpu.VMEM((rows, width), WIDE)],
        4 * rows * width * hidden,
        (rows_in, out, vec, bias, w_out, fc1, fc2),
    )


def own_rows_first(dst, value, c, count):
    size = value.shape[0] // (2 * count)
    for d in range(2 * count):
        at = lax.rem(c + d, 2) * count + d // 2
        dst[pl.ds(pl.multiple_of(at * size, size), size)] = value[d * size : (d + 1) * size]


def store_halves(value, own_ref, there_ref):
    count, size, _ = own_ref.shape
    for i in range(count):
        own_ref[i] = value[i * size : (i + 1) * size].astype(LOW)
        there_ref[i] = value[(count + i) * size : (count + i + 1) * size].astype(LOW)


def mlp_back_kernel(
    c_ref, dy_ref, vec_ref, two_ref, act_ref, slope_ref, n_ref, middle_ref, branch_ref, o_ref, wo_ref, w1_ref, w2_ref,
    grad_ref, do_ref, own1, there1, own2, there2, own_o, there_o, sums_ref, units_ref, dm, dm_t, n_t, total,
):
    step = pl.program_id(0)
    c, count = c_ref[0], own1.shape[0]

    @pl.when(step == 0)
    def _():
        low = (dy_ref[...] * vec_ref[SCALE_MLP][None]).astype(LOW)
        dm[...] = low
        own_rows_first(dm_t, low.T, c, count)
        own_rows_first(n_t, n_ref[...].T, c, count)
        sums_ref[0:1] = column_sum(dy_ref[...] * two_ref[...].astype(WIDE))
        sums_ref[1:2] = column_sum(low)
        total[...] = jnp.zeros_like(total)

    df = (nn(dm[...], w2_ref[...]) * slope_ref[...].astype(WIDE)).astype(LOW)
    units_ref[...] = jnp.broadcast_to(column_sum(df), units_ref.shape)
    store_halves(nn(dm_t[...], act_ref[...]), own2, there2)
    store_halves(nn(n_t[...], df), own1, there1)
    total[...] += nt(df, w1_ref[...])

    @pl.when(step == pl.num_programs(0) - 1)
    def _():
        d_rows, d_gain, d_bias = norm_back(total[...], middle_ref[...], vec_ref[LN2_GAIN][None])
        sums_ref[2:3] = d_gain
        sums_ref[3:4] = d_bias
        grad = dy_ref[...] + d_rows
        grad_ref[...] = grad
        sums_ref[4:5] = column_sum(grad * branch_ref[...].astype(WIDE))
        da = (grad * vec_ref[SCALE_ATTN][None]).astype(LOW)
        sums_ref[5:6] = column_sum(da)
        sums_ref[6:8] = jnp.zeros((2, sums_ref.shape[1]), WIDE)
        do_ref[...] = nn(da, wo_ref[...]).astype(LOW)
        own_rows_first(dm_t, da.T, c, count)
        store_halves(nn(dm_t[...], o_ref[...]), own_o, there_o)


def mlp_back(half, dy, vec, saved, weights, count):
    _, w_out, fc1, fc2 = weights
    rows, width = dy.shape
    hidden = fc1.shape[1]
    block = width // (2 * count)
    whole = full(dy.shape)
    low = (whole, jax.ShapeDtypeStruct((rows, width), LOW))
    wide = (whole, jax.ShapeDtypeStruct((rows, width), WIDE))
    units = pl.BlockSpec((rows, CHUNK), lambda i: (0, i))
    weight = pl.BlockSpec((width, CHUNK), lambda i: (0, i))
    grad = (
        pl.BlockSpec((count, block, CHUNK), lambda i: (0, 0, i)),
        jax.ShapeDtypeStruct((count, block, hidden), LOW),
    )
    grad_o = (full((count, block, width)), jax.ShapeDtypeStruct((count, block, width), LOW))
    return compute_call(
        mlp_back_kernel,
        hidden // CHUNK,
        [
            pl.BlockSpec(memory_space=pltpu.SMEM),
            whole,
            full(vec.shape),
            whole,
            units,
            units,
            whole,
            whole,
            whole,
            whole,
            full((width, width)),
            weight,
            weight,
        ],
        [
            wide,
            low,
            grad,
            grad,
            grad,
            grad,
            grad_o,
            grad_o,
            (full((8, width)), jax.ShapeDtypeStruct((8, width), WIDE)),
            (pl.BlockSpec((8, CHUNK), lambda i: (0, i)), jax.ShapeDtypeStruct((8, hidden), WIDE)),
        ],
        [
            pltpu.VMEM((rows, width), LOW),
            pltpu.VMEM((width, rows), LOW),
            pltpu.VMEM((width, rows), LOW),
            pltpu.VMEM((rows, width), WIDE),
        ],
        8 * rows * width * hidden,
        (
            half,
            dy,
            vec,
            saved["two"],
            saved["active"],
            saved["slope"],
            saved["n_two"],
            saved["middle"],
            saved["branch"],
            saved["out"],
            w_out,
            fc1,
            fc2,
        ),
    )


def attend_back_kernel(q_ref, k0, k1, v0, v1, p_ref, g_ref, o_ref, scale_ref, d0_ref, d1_ref):
    q = q_ref[...]
    scaled = (g_ref[...].astype(WIDE) * scale_ref[...]).astype(LOW)
    dots = (scaled.astype(WIDE) * o_ref[...]).T
    sums = {}
    dqs = []
    for head in range(q_ref.shape[1] // HD):
        g, here = of_head(scaled, head), of_head(q, head)
        dot = jnp.sum(dots[head * HD : (head + 1) * HD], 0, keepdims=True)
        dq = None
        for half, (k, v) in enumerate(((k0, v0), (k1, v1))):
            p = p_ref[head, half]
            ds = (p.astype(WIDE) * (nt(v[...], g) - dot)).astype(LOW)
            part = tn(k[...], ds)
            dq = part if dq is None else dq + part
            for name, value in (("v", nn(p, g)), ("k", nn(ds, here))):
                sums[name, half] = value if head == 0 else sums[name, half] + value
        dqs.append(dq[head * HD : (head + 1) * HD])
    d0_ref[0] = (jnp.concatenate(dqs, 0).T * (HD**-0.5)).astype(LOW)
    for half, (out, first) in enumerate(((d0_ref, 1), (d1_ref, 0))):
        out[first] = (sums["k", half] * (HD**-0.5)).astype(LOW)
        out[first + 1] = sums["v", half].astype(LOW)


def attend_back(q, kv0, kv1, probs, grad, out, scales):
    rows, width = q.shape
    steps, heads = width // 128, width // HD
    one = pl.BlockSpec((rows, 128), lambda i: (0, i))
    key = pl.BlockSpec((None, rows, 128), lambda i: (0, 0, i))
    value = pl.BlockSpec((None, rows, 128), lambda i: (1, 0, i))

    def several(count):
        return (
            pl.BlockSpec((count, rows, 128), lambda i: (0, 0, i)),
            jax.ShapeDtypeStruct((count, rows, width), LOW),
        )

    return compute_call(
        attend_back_kernel,
        steps,
        [one, key, key, value, value, pl.BlockSpec((2, 2, rows, rows), lambda i: (i, 0, 0, 0)), one, one, one],
        [several(3), several(2)],
        [],
        40 * heads * rows * rows * HD,
        (q, kv0, kv1, kv0, kv1, probs, grad, out, scales),
    )


def project_back_kernel(
    c_ref, d0_ref, d1_ref, n_ref, x_ref, grad_ref, vec_ref, w_ref, dx_ref, low_ref, own, there, sums_ref, n_t, total
):
    step = pl.program_id(0)
    c, count = c_ref[0], own.shape[0]

    @pl.when(step == 0)
    def _():
        total[...] = jnp.zeros_like(total)
        own_rows_first(n_t, n_ref[...].T, c, count)

    theirs = jnp.where(step == 0, 0.0, d1_ref[...].astype(WIDE))
    grad = (d0_ref[...].astype(WIDE) + theirs).astype(LOW)
    store_halves(nn(n_t[...], grad), own, there)
    total[...] += nt(grad, w_ref[...])
    sums = column_sum(grad)

    @pl.when(step == 0)
    def _():
        sums_ref[0:1] = sums

    @pl.when(step == 2)
    def _():
        sums_ref[1:2] = sums
        d_rows, d_gain, d_bias = norm_back(total[...], x_ref[...], vec_ref[LN1_GAIN][None])
        sums_ref[2:3] = d_gain
        sums_ref[3:4] = d_bias
        sums_ref[4:8] = jnp.zeros((4, sums_ref.shape[1]), WIDE)
        low = (grad_ref[...] + d_rows).astype(LOW)
        low_ref[...] = low
        dx_ref[...] = low.astype(WIDE)


def project_back(half, d0, d1, saved, grad, vec, attn, count):
    rows, width = grad.shape
    block = width // (2 * count)
    whole = full(grad.shape)
    out = (
        pl.BlockSpec((None, count, block, width), lambda i: (i, 0, 0, 0)),
        jax.ShapeDtypeStruct((3, count, block, width), LOW),
    )
    return compute_call(
        project_back_kernel,
        3,
        [
            pl.BlockSpec(memory_space=pltpu.SMEM),
            pl.BlockSpec((None, rows, width), lambda i: (i, 0, 0)),
            pl.BlockSpec((None, rows, width), lambda i: (jnp.maximum(i - 1, 0), 0, 0)),
            whole,
            whole,
            whole,
            full(vec.shape),
            pl.BlockSpec((None, width, width), lambda i: (i, 0, 0)),
        ],
        [
            (whole, jax.ShapeDtypeStruct((rows, width), WIDE)),
            (whole, jax.ShapeDtypeStruct((rows, width), LOW)),
            out,
            out,
            (full((8, width)), jax.ShapeDtypeStruct((8, width), WIDE)),
        ],
        [pltpu.VMEM((width, rows), LOW), pltpu.VMEM((rows, width), WIDE)],
        12 * rows * width * width,
        (half, d0, d1, saved["n_one"], saved["rows_in"], grad, vec, attn),
    )


def pick(stack, index, axis=0):
    return lax.dynamic_index_in_dim(stack, index, axis, keepdims=False)


def after(value, *others):
    return lax.optimization_barrier((value,) + others)[0]


def layer_forward(rows_in, vec, bias, weights, mask, from_pair, meanwhile):
    n_one, kv0, q = project(rows_in, vec, weights[0])
    kv1 = from_pair(kv0)
    out, out_wide, scales, probs = attend(q, kv0, kv1, mask)
    out = meanwhile(0, q, out)
    leaving, leaving_low, branch, middle, n_two, active, slope, two = mlp(rows_in, out, vec, bias, weights)
    leaving = meanwhile(1, out, leaving)
    saved = dict(
        rows_in=rows_in,
        n_one=n_one,
        q=q,
        kv0=kv0,
        kv1=kv1,
        out=out,
        out_wide=out_wide,
        scales=scales,
        probs=probs,
        branch=branch,
        middle=middle,
        n_two=n_two,
        active=active,
        slope=slope,
        two=two,
    )
    return (leaving, leaving_low, saved)


def layer_backward(grad_rows, saved, vec, weights, half, from_pair, sums_over, meanwhile):
    count = lax.axis_size("dp") // 2
    grad_middle, d_out, own1, there1, own2, there2, own_o, there_o, sums, units = mlp_back(
        half, grad_rows, vec, saved, weights, count
    )
    d_out = meanwhile("fc2", grad_rows, d_out)
    d0, d1 = attend_back(saved["q"], saved["kv0"], saved["kv1"], saved["probs"], d_out, saved["out_wide"], saved["scales"])
    own, there = dict(out=own_o, fc1=own1, fc2=own2), dict(out=there_o, fc1=there1, fc2=there2)
    d0 = meanwhile("fc1", d_out, d0)
    d1 = from_pair(d1)
    d0 = sums_over(own, there, d0)
    grad_in, grad_low, own["qkv"], there["qkv"], sums_one = project_back(
        half, d0, d1, saved, grad_middle, vec, weights[0], count
    )
    grad_in = meanwhile("out", d0, grad_in)
    grad_in = meanwhile("qkv", d0, grad_in)
    vectors = jnp.concatenate([sums[:6], sums_one[:4]], 0), units[0]
    return (grad_in, grad_low, own, there, vectors)


SUMS = ("scale_mlp", "b_fc2", "ln2_gain", "ln2_bias", "scale_attn", "b_out", "b_query", "b_value", "ln1_gain", "ln1_bias")
NARROW = ("ln1_gain", "ln1_bias", "b_query", "b_value", "b_out", "scale_attn", "ln2_gain", "ln2_bias", "b_fc2", "scale_mlp")


def local(
    boundary,
    ln1_gain,
    ln1_bias,
    w_query,
    w_key,
    w_value,
    b_query,
    b_value,
    w_out,
    b_out,
    scale_attn,
    ln2_gain,
    ln2_bias,
    w_fc1,
    b_fc1,
    w_fc2,
    b_fc2,
    scale_mlp,
):
    place = Place()
    _, micros, images, seq_len, columns = boundary.shape
    S, DP, MP = place.S, place.DP, place.MP
    width = columns * MP
    rows = half_rows(seq_len)
    pieces = 2 * micros
    number = place.s * MP + place.z
    active = number < pieces

    def from_pair(value):
        return lax.ppermute(value, "dp", [(i, i + 1 - 2 * (i % 2)) for i in range(DP)])

    def from_row(value, r):
        return lax.ppermute(value, "dp", [(i, (i - 2 * r) % DP) for i in range(DP)])

    turns = max(pieces, MP)
    spots = [(i, j, k) for i in range(S) for j in range(DP) for k in range(MP)]

    def move(value, target):
        number_of = {spot: i for i, spot in enumerate(spots)}
        pairs = [(number_of[spot], number_of[target(*spot)]) for spot in spots if target(*spot) is not None]
        return lax.ppermute(value, ("section", "dp", "mp"), pairs)

    def bring(blocks, which, began):
        got = []
        for turn in which:

            def target(i, j, k, turn=turn):
                piece = (turn + k) % turns
                image = 2 * (piece // 2) + j % 2
                if i != 1 or piece >= pieces:
                    return None
                return (image // MP, j // 2 * 2 + piece % 2, image % MP)

            piece = jnp.minimum(lax.rem(place.z + turn, turns), pieces - 1)
            got.append(move(after(pick(blocks, piece), began), target))
        return got

    def brought(got):
        here = 2 * lax.div(number, 2) + place.c
        stack = jnp.stack(got)
        return jnp.concatenate([pick(stack, lax.rem(here + turns - zz % turns, turns)) for zz in range(MP)], 1)

    waiting, above, projections = {}, {}, {}

    def join(name, own, got):
        axis = own.ndim - 3

        def row(r):
            at = lax.rem(place.y + r, DP // 2)
            return pick(own, at, axis).astype(WIDE) + pick(got, at, axis).astype(WIDE)

        others = [row(r).astype(LOW) for r in range(1, DP // 2)]
        waiting[name] = (row, others)
        return others

    def sums_over(own, there, before):
        parts = []
        for name in ("fc2", "fc1"):
            parts += join(name, own[name], from_pair(there[name]))
        projections["out"] = (own["out"], there["out"])
        return after(before, *parts)

    def rows_meanwhile(name, before, done):
        if name == "fc2":
            got = {key: from_pair(after(there, before)) for key, (_, there) in projections.items()}
            got, done = lax.optimization_barrier((got, done))
            for key in got:
                projections[key] = (projections[key][0], got[key])
        row, others = waiting[name]
        got = [from_row(after(part, before), DP // 2 - r) for r, part in enumerate(others, 1)]
        got, done = lax.optimization_barrier((got, done))
        above[name] = (row, got)
        if name == "fc1":
            for key in projections:
                done = after(done, *join(key, *projections[key]))
        return done

    def sums_done(name):
        row, got = above[name]
        total = row(0)
        for other in got:
            total = total + other.astype(WIDE)
        return total.astype(LOW)

    def from_rows(value, began):
        return [from_row(after(value, began), r) for r in range(1, DP // 2)]

    def from_section(value):
        return lax.ppermute(value, "section", [(i, S - 1 - i) for i in range(S)])

    def put_rows(weight, got, first=0):
        axis, block = weight.ndim - 2, weight.shape[-2] // DP
        for r, value in enumerate(got, 1):
            row = lax.rem(place.y + r, DP // 2) * 2
            for rows_of, part in ((row + place.c, value), (row + 1 - place.c, from_pair(value))):
                start = [jnp.int32(0)] * weight.ndim
                start[axis], start[-1] = rows_of * block, jnp.int32(first)
                weight = lax.dynamic_update_slice(weight, part, start)
        return weight

    spare = jnp.arange(rows)[:, None] < 2 * rows - seq_len
    mask = jnp.where(spare & (jnp.stack([place.c, 1 - place.c]) == 1)[None], -1e30, 0.0).astype(WIDE)
    mask = jnp.pad(mask, ((0, 0), (0, 126)))
    half = place.c.reshape(1)
    narrow = (ln1_gain, ln1_bias, b_query, b_value, b_out, scale_attn, ln2_gain, ln2_bias, b_fc2, scale_mlp)
    table = jnp.concatenate(list(narrow) + [jnp.zeros((16 - len(narrow), columns), WIDE)], 0)
    bias = jnp.broadcast_to(b_fc1, (8, b_fc1.shape[1]))
    qkv_shard = jnp.stack([w_query[0], w_key[0], w_value[0]])
    tokens = boundary.reshape(micros, seq_len, 1, columns)
    (arrived, sent, tables, all_biases), weights, later = gather(
        tokens, table, bias, qkv_shard, w_out[0].T, w_fc1[0], w_fc2[0].T
    )
    arrived = jnp.where(active, arrived.astype(WIDE), 0.0)
    vectors = [tables[layer] for layer in range(S)]
    biases = [all_biases[layer] for layer in range(S)]

    saved, cotangent, halves = [], [], []
    split = [range(turns)[i * turns // 3 : (i + 1) * turns // 3] for i in range(3)]
    rows_now = arrived
    for layer in range(S):
        def meanwhile(stage, before, done, layer=layer):
            at = 2 * layer + stage
            if at > 2:
                return done
            got = bring(sent, split[at], before)
            if at == 0:
                got, new, done = lax.optimization_barrier((got, from_rows(later[0], before), done))
                weights[1][0] = put_rows(weights[1][0], new)
            elif at == 1:
                got, new, done = lax.optimization_barrier((got, from_rows(later[3], before), done))
                halves.extend(new)
            else:
                new = ([from_section(after(h, before)) for h in halves], from_rows(later[2], before), from_rows(later[1], before))
                got, new, done = lax.optimization_barrier((got, new, done))
                first = place.s == 0
                fc2 = [
                    jnp.where(first, jnp.concatenate([h, o], -1), jnp.concatenate([o, h], -1))
                    for h, o in zip(halves, new[0])
                ]
                weights[1][3] = put_rows(weights[1][3], fc2)
                weights[1][2] = put_rows(weights[1][2], new[1], weights[1][2].shape[-1] // 2)
                weights[1][1] = put_rows(weights[1][1], new[2])
            cotangent.extend(got)
            return done

        rows_now, end_rows, kept = layer_forward(
            rows_now, vectors[layer], biases[layer], weights[layer], mask, from_pair, meanwhile
        )
        saved.append(kept)

    grad_now = jnp.where(active, brought(cotangent).astype(WIDE), 0.0)
    vector_grads = [None] * S

    for layer in reversed(range(S)):
        grad_now, grad_low, own, there, vector_grads[layer] = layer_backward(
            grad_now, saved[layer], vectors[layer], weights[layer], half, from_pair,
            sums_over if layer else (lambda own, there, before: before),
            (lambda name, before, done: done) if layer else rows_meanwhile,
        )
        if layer:
            projections["qkv"] = (own["qkv"], there["qkv"])

    above = {name: sums_done(name) for name in ("fc2", "fc1", "out", "qkv")}
    grads = dict(own=own, there=there, above=above, pieces=pieces)
    shapes = [qkv_shard.shape, w_query.shape[1:], w_fc1.shape[1:], (w_fc2.shape[2], w_fc2.shape[1])]
    names = SUMS + ("b_fc1",)
    table = jnp.stack(
        [
            jnp.concatenate(
                [
                    table.reshape(len(SUMS), MP, DP, -1).transpose(1, 2, 0, 3).reshape(MP, DP, -1),
                    units.reshape(MP, DP, -1),
                ],
                2,
            )
            for table, units in vector_grads
        ]
    )
    lines = -(-table.shape[3] // 1024) * 8
    table = jnp.pad(table, ((0, 0), (0, 0), (0, 0), (0, lines * 128 - table.shape[3])))
    table = table.reshape(S, MP, DP // 2, 2, lines, 128).transpose(3, 0, 2, 1, 4, 5)
    ends, summed, *sums = scatter(table, grad_low, end_rows, grads, shapes)
    sizes = [columns // DP] * len(NARROW) + [b_fc1.shape[1] // DP]
    ends, g_query, g_key, g_value, g_out, g_fc1, g_fc2, *vector_sums = finish(ends, summed, sums, seq_len, sizes)
    v = dict(zip(names, vector_sums))
    return (
        ends.reshape(boundary.shape),
        v["ln1_gain"],
        v["ln1_bias"],
        g_query[None],
        g_key[None],
        g_value[None],
        v["b_query"],
        v["b_value"],
        g_out[None],
        v["b_out"],
        v["scale_attn"],
        v["ln2_gain"],
        v["ln2_bias"],
        g_fc1[None],
        v["b_fc1"],
        g_fc2[None],
        v["b_fc2"],
        v["scale_mlp"],
    )


def solution(mesh):
    images = P("section", None, "dp", None, "mp")
    vector = P("section", "mp")
    small = P("section", ("mp", "dp"))
    rows = P("section", "dp", "mp")
    columns = P("section", "mp", "dp")

    def specs(ends, line):
        return (
            ends,
            line,
            line,
            rows,
            rows,
            rows,
            line,
            line,
            columns,
            line,
            line,
            line,
            line,
            rows,
            line,
            columns,
            line,
            line,
        )

    return jax.shard_map(
        local,
        mesh=mesh,
        in_specs=specs(images, vector),
        out_specs=specs(images, small),
        check_vma=False,
    )
```
